256 devices in a mesh: wall: 4 (over y), tile: 64 (over x, z, core).
Axes of the slice: x: 4, y: 4, z: 8, core: 2. Of those that a mesh axis runs over, the one named last changes fastest.
Arguments:
- adjoint: float32 [10, 32, 512, 128], P(None, 'wall', 'tile'), may hold values from -6 to 6
- source: float32 [10, 32, 512, 128], P(None, 'wall', 'tile'), may hold values from -1.8 to 1.8
- radius: float32 [32, 512, 128], P('wall', 'tile'), may hold values from 0.1 to 0.6
- frequency: float32 [32, 512, 128], P('wall', 'tile'), may hold values from 0.1 to 1
- lower_coupling: float32 [10, 10, 32, 512, 128], P(None, None, 'wall', 'tile'), may hold values from -0.04 to 1
- diag_inverse: float32 [10, 10, 32, 512, 128], P(None, None, 'wall', 'tile'), may hold values from -0.03 to 0.2
- upper_coupling: float32 [10, 10, 32, 512, 128], P(None, None, 'wall', 'tile'), may hold values from -0.04 to 1
- wall_weight: float32 [32], P('wall'), may hold values from 0.01 to 0.1
- surface_weight: float32 [16384, 10, 8], P('tile'), may hold values from -0.625 to 0.625
- patch_owner: int32 [16384, 1], P('tile'), may hold values from 0 to 63; in each aligned block of 256 rows (0 to 255, 256 to 511, ...) at most 8 rows name the same one
- patch_row: int32 [16384], P('tile'), may hold values from 0 to 63
- surface_count: int32 [64], P('tile'), may hold values from 1 to 256, 14336 in all
Outputs:
- adjoint_next: float32 [10, 32, 512, 128], P(None, 'wall', 'tile')
- patch_load: float32 [4096, 128], P('tile')
The draws below stay inside these ranges and needn't reach their ends.
Inputs may be any that keep to these rules, and one draw needn't show every extreme that they name: `patch_owner`: among the 256 blocks of one tile no owner is named more than 8 times. The live blocks of a tile are its first surface_count blocks.
All inputs are finite; a program needn't handle non-finite values.
Results may differ from the reference program's by a relative error of at most 0.0001.
Values sent between devices are 32-bit elements; how exact they have to be, the bound alone decides.
No kernel may reach another device: no remote copies, remote signals or barrier semaphores. Data moves between devices by JAX's collectives and lax.ppermute only.
A program may use at most 128 MiB of HBM per device.

```python
import math
import jax
import jax.numpy as jnp
import numpy as np
from jax import lax

NV = 10
CH_DEV = 8
WINGWISE_POINTS = 128
NB_DEV = 256
PATCH_DEV = 64
PROFILE_DEPTH = 32
AIRFOIL_POINTS = 512
NB = 16384
CAP = 8
LIVE = 14336
N_TILE = 64


def coupling_law(key):
    random_divisions = jax.random.split(key, 6)
    line_shape = (NV, 1, AIRFOIL_POINTS, WINGWISE_POINTS)
    cell_shape = (NV, PROFILE_DEPTH, AIRFOIL_POINTS, WINGWISE_POINTS)
    fast_share = 0.5
    fast_mask = jax.random.uniform(random_divisions[0], line_shape) < fast_share
    slow_rate = jnp.exp(jax.random.uniform(random_divisions[1], line_shape, minval=math.log(0.2 / PROFILE_DEPTH), maxval=math.log(1.0 / PROFILE_DEPTH)))
    fast_rate = jnp.exp(jax.random.uniform(random_divisions[2], line_shape, minval=math.log(1.0 / 16.0), maxval=math.log(0.25)))
    decay_factors = jnp.where(fast_mask, fast_rate, slow_rate) * jax.random.uniform(random_divisions[3], cell_shape, minval=0.5, maxval=2.0)
    packet_bundles = jax.random.uniform(random_divisions[4], (1, PROFILE_DEPTH, AIRFOIL_POINTS, WINGWISE_POINTS)) < 3.0 / PROFILE_DEPTH
    preserve_markers = jnp.exp(-decay_factors) * jnp.where(packet_bundles, 0.6, 1.0)
    spread = jax.random.uniform(random_divisions[5], (NV, NV, PROFILE_DEPTH, AIRFOIL_POINTS, WINGWISE_POINTS), minval=-0.04, maxval=0.04)
    identity_mat = jnp.eye(NV, dtype=jnp.float32)[:, :, None, None, None]
    return (spread * (1.0 - identity_mat) + identity_mat * preserve_markers[:, None]).astype(jnp.float32)


def draw_lower_coupling(key, part):
    return coupling_law(jax.random.fold_in(key, 11))


def draw_upper_coupling(key, part):
    return coupling_law(jax.random.fold_in(key, 12))


def draw_diag_inverse(key, part):
    random_divisions = jax.random.split(jax.random.fold_in(key, 13), 2)
    diagonal = jax.random.uniform(random_divisions[0], (NV, PROFILE_DEPTH, AIRFOIL_POINTS, WINGWISE_POINTS), minval=0.08, maxval=0.2)
    spread = jax.random.uniform(random_divisions[1], (NV, NV, PROFILE_DEPTH, AIRFOIL_POINTS, WINGWISE_POINTS), minval=-0.03, maxval=0.03)
    identity_mat = jnp.eye(NV, dtype=jnp.float32)[:, :, None, None, None]
    return (spread * (1.0 - identity_mat) + identity_mat * diagonal[:, None]).astype(jnp.float32)


def set_ends(entries, rng, smallest, high):
    index_at = [jax.random.randint(jax.random.fold_in(rng, axis), (), 0, length) for axis, length in enumerate(entries.shape)]
    main_axis = entries.shape.index(max(entries.shape))
    next_to = index_at[:main_axis] + [(index_at[main_axis] + 1) % entries.shape[main_axis]] + index_at[main_axis + 1:]
    return entries.at[tuple(index_at)].set(smallest).at[tuple(next_to)].set(high)


def block_scale(key, extent, cuts, low, top_value):
    def one(position, shards_of):
        steps = jax.random.uniform(jax.random.fold_in(jax.random.fold_in(key, 6), position), (shards_of,), jnp.float32, low / len(cuts), top_value / len(cuts))
        return jnp.repeat(jnp.exp(steps), extent[position] // shards_of).reshape((-1,) + (1,) * (len(extent) - position - 1))

    level = one(*cuts[0])
    for cut in cuts[1:]:
        level = level * one(*cut)
    return level


def length_profile(count, total, most, lean):
    loads = [(1 << 20) // math.isqrt(grade ** lean) + 1 for grade in range(2, count + 1)]
    rest, given = total - most - (count - 1), [1] * (count - 1)
    while rest > 0:
        candidates = [i for i in range(count - 1) if given[i] < most]
        mass, remaining = sum([loads[i] for i in candidates]), rest
        for i in candidates:
            more = min(most - given[i], max(1, remaining * loads[i] // mass), rest)
            given[i] = given[i] + more
            rest = rest - more
    return np.array([most] + given)


def uneven_parts(stream_key, amount, total, reach, slope):
    if amount == 2:
        one = jax.random.randint(stream_key, (), max(1, total - reach), min(reach, total - 1) + 1)
        return jnp.stack([one, total - one])
    sizes = jnp.asarray(length_profile(amount, total, reach, slope), jnp.int32)
    couples = (amount - 1) // 2
    giver, sink = sizes[1:1 + 2 * couples:2], sizes[2:2 + 2 * couples:2]
    margin = jnp.minimum(giver - 1, reach - sink)
    moved = jax.random.randint(jax.random.fold_in(stream_key, 1), (couples,), 0, 1 << 20) % (margin + 1)
    sizes = sizes.at[1:1 + 2 * couples:2].set(giver - moved).at[2:2 + 2 * couples:2].set(sink + moved)
    return sizes[jax.random.permutation(jax.random.fold_in(stream_key, 2), amount)]


def deal_out(rng, own, number, rows, amount, top, bound, slope):
    sequence = jax.random.permutation(rng, amount)
    packed, common = shares(amount, rows * top, bound, slope, True), shares(amount, rows * top, bound, slope, False)
    places = jnp.arange(amount)

    def named(tallies, offset_by):
        used = int((tallies > 0).sum())
        fixed = max(1, used // 4)
        shifted = fixed + (places - fixed + offset_by * (used - fixed)) % max(1, amount - fixed)
        return jnp.zeros((amount,), jnp.int32).at[sequence[jnp.where(places < fixed, places, shifted)]].set(jnp.asarray(tallies, jnp.int32))

    tallies = jnp.where(number % 4 == 0, named(packed, number // 4), named(common, number - number // 4 - 1))
    mixed = jax.random.permutation(jax.random.fold_in(own, 3), amount)
    donor, taker = mixed[0:amount // 2 * 2:2], mixed[1:amount // 2 * 2:2]
    slack = jnp.minimum(tallies[donor] - 1, bound - tallies[taker]) // 2
    slack = jnp.where((donor == sequence[0]) | (taker == sequence[0]) | (tallies[taker] == 0), 0, jnp.maximum(slack, 0))
    shifted = jax.random.randint(jax.random.fold_in(own, 4), (amount // 2,), 0, 1 << 20) % (slack + 1)
    tallies = tallies.at[donor].add(-shifted).at[taker].add(shifted)
    members = jnp.searchsorted(jnp.cumsum(tallies), jnp.arange(rows * top), side="right").astype(jnp.int32)
    table = members.reshape(top, rows).T
    table = table[jax.random.permutation(jax.random.fold_in(own, 1), rows)]
    offset_by = jax.random.randint(jax.random.fold_in(own, 2), (rows, 1), 0, top)
    return jnp.take_along_axis(table, (jnp.arange(top)[None, :] + offset_by) % top, axis=1)


def shares(number_of, total, limit, skew, full):
    loads = [(1 << 20) // math.isqrt(standing ** skew) + 1 for standing in range(1, number_of + 1)]
    largest = limit if full else min(limit, max(-(-total // number_of), total * loads[0] // sum(loads)))
    least = 1 if total - largest >= number_of - 1 else 0
    counts, spare = [largest] + [least] * (number_of - 1), total - largest - least * (number_of - 1)
    while spare > 0:
        free = [i for i in range(1, number_of) if counts[i] < largest] or [i for i in range(1, number_of) if counts[i] < limit]
        mass, left = sum([loads[i] for i in free]), spare
        for i in free:
            addition = min(limit - counts[i], max(1, left * loads[i] // mass), spare)
            counts[i] = counts[i] + addition
            spare = spare - addition
    return np.array(counts)


def normal_values(key, extent, deviation, bound, cuts=(), kind=jnp.bfloat16):
    loudness = block_scale(key, extent, cuts, -0.22, 0.18) if cuts else 1.0
    array = jax.random.normal(key, extent, jnp.float32) * deviation * loudness
    return jnp.minimum(jnp.maximum(array, -bound), bound).astype(kind)


def setup_inputs(seed: int = 0) -> dict:
    splits = jax.random.split(jax.random.key(seed), 13)
    adjoint = normal_values(splits[0], (NV, PROFILE_DEPTH, AIRFOIL_POINTS, WINGWISE_POINTS), 1.0, 6.0, ((1, 4), (2, 64)), jnp.float32)
    source = normal_values(splits[1], (NV, PROFILE_DEPTH, AIRFOIL_POINTS, WINGWISE_POINTS), 0.3, 1.8, ((1, 4), (2, 64)), jnp.float32)
    radius = jnp.clip(jnp.exp(math.log(0.6) - 1.7917595 * jax.random.uniform(splits[2], (PROFILE_DEPTH, AIRFOIL_POINTS, WINGWISE_POINTS), jnp.float32) ** block_scale(splits[2], (PROFILE_DEPTH, AIRFOIL_POINTS, WINGWISE_POINTS), ((0, 4), (1, 64)), -0.2, 0.2)), 0.1, 0.6)
    frequency = jnp.clip(jnp.exp(math.log(1.0) - 2.3025851 * jax.random.uniform(splits[3], (PROFILE_DEPTH, AIRFOIL_POINTS, WINGWISE_POINTS), jnp.float32) ** block_scale(splits[3], (PROFILE_DEPTH, AIRFOIL_POINTS, WINGWISE_POINTS), ((0, 4), (1, 64)), -0.2, 0.2)), 0.1, 1.0)
    lower_coupling = draw_lower_coupling(jax.random.fold_in(splits[12], 71), 0)
    diag_inverse = draw_diag_inverse(jax.random.fold_in(splits[12], 71), 0)
    upper_coupling = draw_upper_coupling(jax.random.fold_in(splits[12], 71), 0)
    wall_weight = jnp.clip(jnp.exp(math.log(0.1) - 2.3025851 * jax.random.uniform(splits[7], (PROFILE_DEPTH,), jnp.float32) ** block_scale(splits[7], (PROFILE_DEPTH,), ((0, 4),), -0.2, 0.2)), 0.01, 0.1)
    surface_weight = normal_values(splits[8], (NB, NV, CH_DEV), (NV * CH_DEV) ** -0.5, 0.625, ((0, 64),), jnp.float32)
    patch_owner_keys = jax.random.split(jax.random.fold_in(splits[9], 1), NB // NB_DEV)
    patch_owner_turns = jax.random.permutation(jax.random.fold_in(splits[9], 3), NB // NB_DEV)
    patch_owner = jax.vmap(lambda own, number: deal_out(jax.random.fold_in(splits[9], 2), own, number, NB_DEV, N_TILE, 1, CAP, 2))(patch_owner_keys, patch_owner_turns).reshape((NB, 1))
    patch_row = set_ends(jax.random.randint(splits[10], (NB,), 0, PATCH_DEV), jax.random.fold_in(splits[10], 1), 0, PATCH_DEV - 1).astype(jnp.int32)
    surface_count = uneven_parts(splits[11], N_TILE, LIVE, NB_DEV, 2).astype(jnp.int32)
    return dict(adjoint=adjoint, source=source, radius=radius, frequency=frequency, lower_coupling=lower_coupling, diag_inverse=diag_inverse, upper_coupling=upper_coupling, wall_weight=wall_weight, surface_weight=surface_weight, patch_owner=patch_owner, patch_row=patch_row, surface_count=surface_count)


highest = lax.Precision.HIGHEST


def flux_apply(stacked_pad, radius, adjoint, frequency):
    chord_cells = adjoint.shape[2]
    neighbours = stacked_pad[:-1]
    radii = stacked_pad[-1]
    applied = jnp.zeros_like(adjoint)
    for offset, weight in ((-2, -0.125), (-1, 0.5), (1, 0.5), (2, -0.125)):
        first_cell = 2 + offset
        applied = applied + weight * 0.5 * (radius + radii[:, first_cell:first_cell + chord_cells]) * neighbours[:, :, first_cell:first_cell + chord_cells]
    span_state = jnp.pad(adjoint, ((0, 0), (0, 0), (0, 0), (1, 1)))
    span_radius = jnp.pad(radius, ((0, 0), (0, 0), (1, 1)))
    span_cells = adjoint.shape[3]
    for first_cell in (0, 2):
        applied = applied + 0.5 * 0.5 * (radius + span_radius[:, :, first_cell:first_cell + span_cells]) * span_state[:, :, :, first_cell:first_cell + span_cells]
    half_count = adjoint.shape[0] // 2
    turned = jnp.concatenate([-adjoint[half_count:], adjoint[:half_count]], axis=0)
    return applied + frequency * turned


def reference(adjoint, source, radius, frequency, lower_coupling, diag_inverse, upper_coupling, wall_weight, surface_weight, patch_owner, patch_row, surface_count):
    stacked = jnp.concatenate([adjoint, radius[None]], axis=0)
    stacked_pad = jnp.pad(stacked, ((0, 0), (0, 0), (2, 2), (0, 0)))
    residual = source - flux_apply(stacked_pad, radius, adjoint, frequency)

    def forward_step(index, carried):
        previous, stack = carried
        matrix = lax.dynamic_index_in_dim(lower_coupling, index, 2, keepdims=False)
        current = jnp.einsum("ijcs,jcs->ics", matrix, previous, precision=highest) + lax.dynamic_index_in_dim(residual, index, 1, keepdims=False)
        return current, lax.dynamic_update_index_in_dim(stack, current, index, 1)

    last_state, forward = lax.fori_loop(0, PROFILE_DEPTH, forward_step, (jnp.zeros_like(residual[:, 0]), jnp.zeros_like(residual)))
    scaled = jnp.einsum("ijkcs,jkcs->ikcs", diag_inverse, forward, precision=highest)

    def backward_step(count, carried):
        previous, stack = carried
        index = PROFILE_DEPTH - 1 - count
        matrix = lax.dynamic_index_in_dim(upper_coupling, index, 2, keepdims=False)
        current = lax.dynamic_index_in_dim(scaled, index, 1, keepdims=False) - jnp.einsum("ijcs,jcs->ics", matrix, previous, precision=highest)
        return current, lax.dynamic_update_index_in_dim(stack, current, index, 1)

    first_state, adjoint_next = lax.fori_loop(0, PROFILE_DEPTH, backward_step, (jnp.zeros_like(scaled[:, 0]), jnp.zeros_like(scaled)))
    profile = jnp.einsum("ikcs,k->ics", adjoint_next, wall_weight, precision=highest)
    blocks = profile.reshape(NV, N_TILE, CH_DEV, WINGWISE_POINTS)
    weights = surface_weight.reshape(N_TILE, NB_DEV, NV, CH_DEV)
    sens_rows = jnp.einsum("tbvh,vths->tbs", weights, blocks, precision=highest)
    live_mask = (jnp.arange(NB_DEV).astype(jnp.int32)[None, :] < surface_count[:, None]).astype(sens_rows.dtype)
    sens_rows = (sens_rows * live_mask[:, :, None]).reshape(NB_DEV * N_TILE, WINGWISE_POINTS)
    patch_ids = patch_owner[:, 0] * PATCH_DEV + patch_row
    patch_load = jax.ops.segment_sum(sens_rows, patch_ids, num_segments=PATCH_DEV * N_TILE)
    return (adjoint_next, patch_load)
```

```python
import jax
import jax.numpy as jnp
from jax import lax
from jax.experimental import pallas as pl
from jax.experimental.pallas import tpu as pltpu
from jax.sharding import PartitionSpec as P

NV = 10
K = 8
H = 8
S = 128
PATCH_DEV = 64
SLOTS = 8
ROWS_PER_OWNER = SLOTS + 1
F32 = jnp.float32
highest = lax.Precision.HIGHEST

VM = pl.BlockSpec(memory_space=pltpu.VMEM)
SM = pl.BlockSpec(memory_space=pltpu.SMEM)


def f32(*shape):
    return jax.ShapeDtypeStruct(shape, F32)


def call(body, out_shape, n_in, smem=(), scratch=(), flops=0, nbytes=0):
    single = not isinstance(out_shape, (tuple, list))
    return pl.pallas_call(
        body,
        out_shape=out_shape,
        in_specs=[SM if i in smem else VM for i in range(n_in)],
        out_specs=VM if single else [VM] * len(out_shape),
        scratch_shapes=list(scratch),
        compiler_params=pltpu.CompilerParams(vmem_limit_bytes=40 * 1024 * 1024),
        cost_estimate=pl.CostEstimate(flops=flops, bytes_accessed=nbytes, transcendentals=0),
    )


def block_dot(m_ref, k, x):
    acc = None
    for j in range(NV):
        term = m_ref[:, j, k] * x[j][None]
        acc = term if acc is None else acc + term
    return acc


def forward_sweep(l_ref, d_ref, r_ref, s_ref, x):
    f = x
    for k in range(K):
        r = r_ref[:, k]
        f = r if f is None else r + block_dot(l_ref, k, f)
        s_ref[k] = block_dot(d_ref, k, f)
    return f


def backward_sweep(u_ref, s_ref, w_ref, y, emit=None):
    b, p = y, None
    for k in range(K - 1, -1, -1):
        s = s_ref[k]
        b = s if b is None else s - block_dot(u_ref, k, b)
        if w_ref is not None:
            p = b * w_ref[k] if p is None else p + b * w_ref[k]
        if emit is not None:
            emit(k, b)
    return b, p


def map_dot(m_ref, base, x):
    acc = None
    for j in range(NV):
        term = m_ref[base + j] * x[j][None]
        acc = term if acc is None else acc + term
    return acc


def pack_kernel(a_ref, rad_ref, lo_ref, hi_ref):
    for v in range(NV + 1):
        for k in range(K):
            cell = a_ref[v, k] if v < NV else rad_ref[k]
            at = 2 * (v * K + k)
            lo_ref[at : at + 2, :] = cell[0:2]
            hi_ref[at : at + 2, :] = cell[6:8]


def interior_kernel(a_ref, src_ref, rad_ref, frq_ref, out_ref):
    row = lax.broadcasted_iota(jnp.int32, (H, S), 0)
    lane = lax.broadcasted_iota(jnp.int32, (H, S), 1)
    for k in range(K):
        a = a_ref[:, k]
        rad = rad_ref[k]
        applied = None
        for d, w in ((-2, -0.0625), (-1, 0.25), (1, 0.25), (2, -0.0625)):
            inside = (row + d >= 0) & (row + d < H)
            coef = jnp.where(inside, w * (rad + pltpu.roll(rad, (-d) % H, 0)), 0.0)
            term = coef[None] * pltpu.roll(a, (-d) % H, 1)
            applied = term if applied is None else applied + term
        for d in (-1, 1):
            inside = (lane + d >= 0) & (lane + d < S)
            coef = jnp.where(inside, 0.25 * (rad + pltpu.roll(rad, (-d) % S, 1)), 0.0)
            applied = applied + coef[None] * pltpu.roll(a, (-d) % S, 2)
        frq = frq_ref[k][None]
        half = NV // 2
        src = src_ref[:, k] - applied
        out_ref[:half, k] = src[:half] + frq * a[half:]
        out_ref[half:, k] = src[half:] - frq * a[:half]


def maps_kernel(pos_ref, w_ref, l_ref, d_ref, u_ref, ab_ref, q_ref, s_ref):
    wall = pos_ref[0]

    def pair_dot(m_ref, k, xs):
        accs = [None] * len(xs)
        for j in range(NV):
            m = m_ref[:, j, k]
            for n, x in enumerate(xs):
                term = m * x[j][None]
                accs[n] = term if accs[n] is None else accs[n] + term
        return accs

    @pl.when(wall <= 1)
    def _():
        @pl.loop(0, NV // 2)
        def _(pair):
            cols = [2 * pair, 2 * pair + 1]
            bs = [-u_ref[:, c, K - 1] for c in cols]
            ps = [b * w_ref[K - 1] for b in bs]
            for k in range(K - 2, -1, -1):
                bs = [-b for b in pair_dot(u_ref, k, bs)]
                ps = [p + b * w_ref[k] for p, b in zip(ps, bs)]
            for c, b, p in zip(cols, bs, ps):
                ab_ref[c] = b
                ab_ref[NV + c] = p
                q_ref[c] = p

    @pl.when(wall == 3)
    def _():
        @pl.loop(0, NV // 2)
        def _(pair):
            cols = [2 * pair, 2 * pair + 1]
            gs = [l_ref[:, c, 0] for c in cols]
            for k in range(K):
                if k > 0:
                    gs = pair_dot(l_ref, k, gs)
                for n, s in enumerate(pair_dot(d_ref, k, gs)):
                    s_ref[k, n] = s
            cs = [s_ref[K - 1, n] for n in range(2)]
            ps = [c * w_ref[K - 1] for c in cs]
            for k in range(K - 2, -1, -1):
                cs = [s_ref[k, n] - c for n, c in enumerate(pair_dot(u_ref, k, cs))]
                ps = [p + c * w_ref[k] for p, c in zip(ps, cs)]
            for col, c, p in zip(cols, cs, ps):
                ab_ref[col] = c
                ab_ref[NV + col] = p


def residual_kernel(pos_ref, w_ref, r_ref, left_ref, right_ref, rad_ref, l_ref, d_ref, u_ref, out_ref, msg_ref, s_ref):
    wall, tile, last = pos_ref[0], pos_ref[1], pos_ref[2]
    row = lax.broadcasted_iota(jnp.int32, (H, S), 0)
    has_left = tile > 0
    has_right = tile < last

    def line(ref, v, k, c):
        at = 2 * (v * K + k) + c
        return jnp.broadcast_to(ref[at : at + 1, :], (H, S))

    for k in range(K):
        rad = rad_ref[k]
        l0, l1, r0, r1 = (line(ref, NV, k, c) for ref in (left_ref, right_ref) for c in (0, 1))
        zero = jnp.zeros((H, S), F32)
        f_l0 = jnp.where((row == 0) & has_left, -0.0625 * (rad + l0), zero)
        f_l1 = jnp.where(row == 0, 0.25 * (rad + l1), jnp.where(row == 1, -0.0625 * (rad + l1), zero))
        f_l1 = jnp.where(has_left, f_l1, zero)
        f_r0 = jnp.where(row == 7, 0.25 * (rad + r0), jnp.where(row == 6, -0.0625 * (rad + r0), zero))
        f_r0 = jnp.where(has_right, f_r0, zero)
        f_r1 = jnp.where((row == 7) & has_right, -0.0625 * (rad + r1), zero)
        for v in range(NV):
            applied = f_l0 * line(left_ref, v, k, 0) + f_l1 * line(left_ref, v, k, 1)
            applied = applied + (f_r0 * line(right_ref, v, k, 0) + f_r1 * line(right_ref, v, k, 1))
            out_ref[v, k] = r_ref[v, k] - applied

    @pl.when((wall == 0) | (wall == 3))
    def _():
        f = forward_sweep(l_ref, d_ref, out_ref, s_ref, None)
        b, p = backward_sweep(u_ref, s_ref, w_ref, None)
        msg_ref[:NV] = jnp.where(wall == 0, f, b)
        msg_ref[NV:] = p


def middle_kernel(pos_ref, w_ref, msg_ref, r_ref, l_ref, d_ref, u_ref, out_ref, s_ref):
    @pl.when(pos_ref[0] == 1)
    def _():
        x = msg_ref[:NV]
        out_ref[:NV] = forward_sweep(l_ref, d_ref, r_ref, s_ref, x)
        b, p = backward_sweep(u_ref, s_ref, w_ref, None)
        out_ref[NV : 2 * NV] = b
        out_ref[2 * NV :] = p + msg_ref[NV:]


def decide_kernel(
    pos_ref, w_ref, low_ref, high_ref, m1_ref, m3_ref, m0_ref, pw_ref, r_ref, l_ref, d_ref, u_ref,
    x3_ref, y2_ref, y1_ref, y0_ref, rows_ref, s_ref, prof_ref,
):
    @pl.when(pos_ref[0] == 2)
    def _():
        x3 = forward_sweep(l_ref, d_ref, r_ref, s_ref, low_ref[:NV])
        x3_ref[...] = x3
        y2 = high_ref[:NV] + map_dot(m3_ref, 0, x3)
        y2_ref[...] = y2
        total = low_ref[2 * NV :] + high_ref[NV:] + map_dot(m3_ref, NV, x3)
        y1, p2 = backward_sweep(u_ref, s_ref, w_ref, y2)
        y1_ref[...] = y1
        y0 = low_ref[NV : 2 * NV] + map_dot(m1_ref, 0, y1)
        y0_ref[...] = y0
        total = total + p2 + map_dot(m1_ref, NV, y1) + map_dot(m0_ref, 0, y0)
        for v in range(NV):
            prof_ref[v * H : (v + 1) * H, :] = total[v]
        row = lax.broadcasted_iota(jnp.int32, (SLOTS, S), 0)
        lane = lax.broadcasted_iota(jnp.int32, (SLOTS, S), 1)
        prof_ref[NV * H :, :] = (row == lane).astype(F32)
        rows_ref[...] = jnp.dot(pw_ref[...], prof_ref[...], precision=highest, preferred_element_type=F32)


def finish_kernel(pos_ref, low_ref, mid_ref, x3_ref, y2_ref, y1_ref, y0_ref, r_ref, l_ref, d_ref, u_ref, out_ref, s_ref, x_ref, y_ref):
    wall = pos_ref[0]
    zero = jnp.zeros((NV, H, S), F32)
    x = jnp.where(wall == 1, low_ref[:NV], zero)
    x = jnp.where(wall == 2, mid_ref[:NV], x)
    x_ref[...] = jnp.where(wall == 3, x3_ref[...], x)
    y = jnp.where(wall == 0, y0_ref[...], zero)
    y = jnp.where(wall == 1, y1_ref[...], y)
    y_ref[...] = jnp.where(wall == 2, y2_ref[...], y)
    forward_sweep(l_ref, d_ref, r_ref, s_ref, x_ref[...])

    def emit(k, b):
        out_ref[:, k] = b

    backward_sweep(u_ref, s_ref, None, y_ref[...], emit)


def place_kernel(count_ref, w_ref, owner_ref, tag_ref, out_ref):
    blocks = owner_ref.shape[0]
    owners = out_ref.shape[0] // ROWS_PER_OWNER
    owner = owner_ref[...]
    index = lax.broadcasted_iota(jnp.int32, (blocks, 1), 0)
    live = index < count_ref[0]
    hits = (owner == lax.broadcasted_iota(jnp.int32, (blocks, owners), 1)).astype(F32)
    earlier = lax.broadcasted_iota(jnp.int32, (blocks, blocks), 1) < lax.broadcasted_iota(jnp.int32, (blocks, blocks), 0)
    before = jnp.dot(earlier.astype(F32), hits, preferred_element_type=F32)
    slot = jnp.sum(before * hits, axis=1, keepdims=True).astype(jnp.int32)
    column = lax.broadcasted_iota(jnp.int32, (blocks, owners * ROWS_PER_OWNER), 1)
    placed = ((owner * ROWS_PER_OWNER + slot == column) & live).astype(F32)
    tagged = ((owner * ROWS_PER_OWNER + SLOTS == column) & live).astype(F32)
    width = NV * H
    lanes = lax.broadcasted_iota(jnp.int32, (blocks, SLOTS), 1)
    tags = jnp.where(lanes == slot, (tag_ref[...] + 1).astype(F32), 0.0)
    dims = (((0,), (0,)), ((), ()))
    out_ref[:, :width] = lax.dot_general(placed, w_ref[...], dims, precision=highest, preferred_element_type=F32)
    out_ref[:, width:] = lax.dot_general(tagged, tags, dims, precision=highest, preferred_element_type=F32)


def pick_kernel(got_ref, out_ref):
    rows = got_ref.shape[0]
    sources = rows // ROWS_PER_OWNER
    tag_rows = got_ref[pl.ds(SLOTS, sources, stride=ROWS_PER_OWNER), :]
    lane_of = (
        lax.broadcasted_iota(jnp.int32, (SLOTS, S), 0) == lax.broadcasted_iota(jnp.int32, (SLOTS, S), 1)
    ).astype(F32)
    tags = lax.dot_general(
        lane_of, tag_rows, (((1,), (1,)), ((), ())), precision=highest, preferred_element_type=F32
    )
    column = lax.broadcasted_iota(jnp.int32, (sources, rows), 1)
    first = lax.broadcasted_iota(jnp.int32, (sources, rows), 0) * ROWS_PER_OWNER
    spread = ((column >= first) & (column < first + ROWS_PER_OWNER)).astype(F32)
    wide = jnp.dot(tags, spread, precision=highest, preferred_element_type=F32)
    slot = lax.broadcasted_iota(jnp.int32, (SLOTS, rows), 1) % ROWS_PER_OWNER
    mine = slot == lax.broadcasted_iota(jnp.int32, (SLOTS, rows), 0)
    tag = jnp.sum(jnp.where(mine, wide, 0.0), axis=0, keepdims=True)
    target = (lax.broadcasted_iota(jnp.int32, (PATCH_DEV, rows), 0) + 1).astype(F32)
    picker = (tag == target).astype(F32)
    out_ref[...] = jnp.dot(picker, got_ref[...], precision=highest, preferred_element_type=F32)


def on_device(
    adjoint, source, radius, frequency, lower, diag, upper, wall_weight,
    surface_weight, patch_owner, patch_row, surface_count,
):
    tiles = lax.axis_size("tile")
    pos = jnp.stack([lax.axis_index("wall"), lax.axis_index("tile"), jnp.int32(tiles - 1)]).astype(jnp.int32)
    vm = lambda x: pltpu.with_memory_space_constraint(x, pltpu.VMEM)
    lower, diag, upper = vm(lower), vm(diag), vm(upper)
    vec = f32(NV, H, S)
    levels = pltpu.VMEM((K, NV, H, S), F32)

    lo, hi = call(pack_kernel, (f32(22 * K, S), f32(22 * K, S)), 2, nbytes=800_000)(adjoint, radius)
    left = lax.ppermute(hi, "tile", [(i, (i + 1) % tiles) for i in range(tiles)])
    right = lax.ppermute(lo, "tile", [((i + 1) % tiles, i) for i in range(tiles)])

    inner = call(interior_kernel, f32(NV, K, H, S), 4, flops=4_000_000, nbytes=1_200_000)(
        adjoint, source, radius, frequency
    )
    maps, q0 = call(
        maps_kernel, (f32(2 * NV, NV, H, S), f32(NV, NV, H, S)), 5, smem=(0, 1),
        scratch=(pltpu.VMEM((K, 2, NV, H, S), F32),), flops=44_000_000, nbytes=11_000_000,
    )(pos, wall_weight, lower, diag, upper)
    map1 = lax.ppermute(maps, "wall", [(1, 2)])
    map3 = lax.ppermute(maps, "wall", [(3, 2)])
    map0 = lax.ppermute(q0, "wall", [(0, 2)])

    resid, first = call(
        residual_kernel, (f32(NV, K, H, S), f32(2 * NV, H, S)), 9, smem=(0, 1), scratch=(levels,),
        flops=6_000_000, nbytes=2_000_000,
    )(pos, wall_weight, inner, left, right, radius, lower, diag, upper)
    low = lax.ppermute(first, "wall", [(0, 1), (3, 2)])
    second = call(
        middle_kernel, f32(3 * NV, H, S), 7, smem=(0, 1), scratch=(levels,), flops=5_000_000, nbytes=2_000_000
    )(pos, wall_weight, low, resid, lower, diag, upper)
    mid = lax.ppermute(second, "wall", [(1, 2)])

    placed = call(
        place_kernel, f32(tiles * ROWS_PER_OWNER, NV * H + SLOTS), 4, smem=(0,), flops=50_000_000, nbytes=1_000_000
    )(surface_count, surface_weight.reshape(-1, NV * H), patch_owner, patch_row.reshape(-1, 1))

    x3, y2, y1, y0, rows = call(
        decide_kernel, (vec, vec, vec, vec, f32(tiles * ROWS_PER_OWNER, S)), 12, smem=(0, 1),
        scratch=(levels, pltpu.VMEM((NV * H + SLOTS, S), F32)), flops=20_000_000, nbytes=3_000_000,
    )(pos, wall_weight, mid, low, map1, map3, map0, placed, resid, lower, diag, upper)
    x3 = lax.ppermute(x3, "wall", [(2, 3)])
    y1 = lax.ppermute(y1, "wall", [(2, 1)])
    y0 = lax.ppermute(y0, "wall", [(2, 0)])
    got = lax.all_to_all(rows, "tile", split_axis=0, concat_axis=0, tiled=True)
    adjoint_next = call(
        finish_kernel, f32(NV, K, H, S), 11, smem=(0,),
        scratch=(levels, pltpu.VMEM((NV, H, S), F32), pltpu.VMEM((NV, H, S), F32)), flops=5_000_000, nbytes=2_000_000,
    )(pos, low, mid, x3, y2, y1, y0, resid, lower, diag, upper)
    part = call(pick_kernel, f32(PATCH_DEV, S), 1, flops=20_000_000, nbytes=400_000)(got)
    part = jnp.where(lax.axis_index("wall") == 2, part, 0.0)
    patch = part
    for w in (0, 1, 3):
        patch = patch + lax.ppermute(part, "wall", [(2, w)])
    return adjoint_next, patch


def solution(mesh):
    in_specs = (
        P(None, "wall", "tile", None),
        P(None, "wall", "tile", None),
        P("wall", "tile", None),
        P("wall", "tile", None),
        P(None, None, "wall", "tile", None),
        P(None, None, "wall", "tile", None),
        P(None, None, "wall", "tile", None),
        P("wall"),
        P("tile", None, None),
        P("tile", None),
        P("tile"),
        P("tile"),
    )
    out_specs = (P(None, "wall", "tile", None), P("tile", None))
    return jax.shard_map(
        on_device, mesh=mesh, in_specs=in_specs, out_specs=out_specs, check_vma=False
    )
```

```python
import jax
import jax.numpy as jnp
from jax import lax
from jax.experimental import pallas as pl
from jax.experimental.pallas import tpu as pltpu
from jax.sharding import PartitionSpec as P

NV = 10
K = 8
H = 8
S = 128
PATCH_DEV = 64
SLOTS = 8
ROWS_PER_OWNER = SLOTS + 1
F32 = jnp.float32
highest = lax.Precision.HIGHEST

VM = pl.BlockSpec(memory_space=pltpu.VMEM)
SM = pl.BlockSpec(memory_space=pltpu.SMEM)
HB = pl.BlockSpec(memory_space=pltpu.HBM)


def f32(*shape):
    return jax.ShapeDtypeStruct(shape, F32)


def held(*shape):
    return pltpu.VMEM(shape, F32)


def away(*shape):
    return pltpu.HBM(shape, F32)


def far_off(x):
    return pltpu.with_memory_space_constraint(x, pltpu.HBM)


def call(name, body, out_shape, n_in, smem=(), far=(), scratch=(), flops=0, nbytes=0):
    single = not isinstance(out_shape, (tuple, list))
    run = pl.pallas_call(
        body,
        name=name,
        out_shape=out_shape,
        in_specs=[SM if i in smem else HB if i in far else VM for i in range(n_in)],
        out_specs=VM if single else [VM] * len(out_shape),
        scratch_shapes=list(scratch),
        compiler_params=pltpu.CompilerParams(vmem_limit_bytes=12 * 1024 * 1024),
        cost_estimate=pl.CostEstimate(flops=flops, bytes_accessed=nbytes, transcendentals=0),
    )
    return run


def block_dot(m_ref, k, x):
    acc = None
    for j in range(NV):
        term = m_ref[:, j, k] * x[j][None]
        acc = term if acc is None else acc + term
    return acc


def forward_sweep(l_ref, d_ref, r_ref, s_ref, x):
    f = x
    for k in range(K):
        r = r_ref[:, k]
        f = r if f is None else r + block_dot(l_ref, k, f)
        s_ref[k] = block_dot(d_ref, k, f)
    return f


def backward_sweep(u_ref, s_ref, w_ref, y, emit=None):
    b, p = y, None
    for k in range(K - 1, -1, -1):
        s = s_ref[k]
        b = s if b is None else s - block_dot(u_ref, k, b)
        if w_ref is not None:
            p = b * w_ref[k] if p is None else p + b * w_ref[k]
        if emit is not None:
            emit(k, b)
    return b, p


def map_dot(m_ref, base, x):
    acc = None
    for j in range(NV):
        term = m_ref[base + j] * x[j][None]
        acc = term if acc is None else acc + term
    return acc


def pack_kernel(a_ref, rad_ref, lo_ref, hi_ref):
    for v in range(NV + 1):
        for k in range(K):
            cell = a_ref[v, k] if v < NV else rad_ref[k]
            at = 2 * (v * K + k)
            lo_ref[at : at + 2, :] = cell[0:2]
            hi_ref[at : at + 2, :] = cell[6:8]


def pair_dot(m_ref, k, xs):
    accs = [None] * len(xs)
    for j in range(NV):
        m = m_ref[:, j, k]
        for n, x in enumerate(xs):
            term = m * x[j][None]
            accs[n] = term if accs[n] is None else accs[n] + term
    return accs


def back_map(u_ref, w_ref, s_ref, cols):
    xs = [u_ref[:, c, K - 1] for c in cols]
    for n, x in enumerate(xs):
        s_ref[K - 1, n] = x
    for k in range(K - 2, -1, -1):
        xs = pair_dot(u_ref, k, xs)
        for n, x in enumerate(xs):
            s_ref[k, n] = x
    sums = []
    for n in range(len(cols)):
        total = None
        for k in range(K):
            weight = w_ref[k] if (K - k) % 2 == 0 else -w_ref[k]
            term = s_ref[k, n] * weight
            total = term if total is None else total + term
        sums.append(total)
    return sums


def interior(a_ref, src_ref, rad_ref, frq_ref, out_ref):
    row = lax.broadcasted_iota(jnp.int32, (H, S), 0)
    lane = lax.broadcasted_iota(jnp.int32, (H, S), 1)
    for k in range(K):
        a = a_ref[:, k]
        rad = rad_ref[k]
        applied = None
        for d, w in ((-2, -0.0625), (-1, 0.25), (1, 0.25), (2, -0.0625)):
            inside = (row + d >= 0) & (row + d < H)
            coef = jnp.where(inside, w * (rad + pltpu.roll(rad, (-d) % H, 0)), 0.0)
            term = coef[None] * pltpu.roll(a, (-d) % H, 1)
            applied = term if applied is None else applied + term
        for d in (-1, 1):
            inside = (lane + d >= 0) & (lane + d < S)
            coef = jnp.where(inside, 0.25 * (rad + pltpu.roll(rad, (-d) % S, 1)), 0.0)
            applied = applied + coef[None] * pltpu.roll(a, (-d) % S, 2)
        frq = frq_ref[k][None]
        half = NV // 2
        src = src_ref[:, k] - applied
        out_ref[:half, k] = src[:half] + frq * a[half:]
        out_ref[half:, k] = src[half:] - frq * a[:half]


def start_kernel(
    pos_ref, w_in, a_in, src_in, rad_in, frq_in, l_in, d_in, u_in,
    l_ref, d_ref, u_ref, r_ref, w_ref, ab_ref, q_ref, a_ref, src_ref, rad_ref, frq_ref, s_ref, sems,
):
    wall = pos_ref[0]
    pairs = (
        (a_in, a_ref), (src_in, src_ref), (rad_in, rad_ref), (frq_in, frq_ref),
        (l_in, l_ref), (d_in, d_ref), (u_in, u_ref),
    )
    copies = [pltpu.make_async_copy(out_there, here, sems.at[n]) for n, (out_there, here) in enumerate(pairs)]
    state, (lower, diag, upper) = copies[:4], copies[4:]
    for copy in state + [upper, lower, diag]:
        copy.start()
    for k in range(K):
        w_ref[k] = jnp.broadcast_to(w_in[:, k : k + 1], (H, S))
    for copy in state:
        copy.wait()
    interior(a_ref, src_ref, rad_ref, frq_ref, r_ref)
    upper.wait()

    @pl.when(wall <= 1)
    def _():
        @pl.loop(0, NV // 2)
        def _(pair):
            cols = [2 * pair, 2 * pair + 1]
            sums = back_map(u_ref, w_ref, s_ref, cols)
            for n, c in enumerate(cols):
                ab_ref[c] = s_ref[0, n]
                ab_ref[NV + c] = sums[n]
                q_ref[c] = sums[n]

    lower.wait()
    diag.wait()

    @pl.when(wall == 3)
    def _():
        @pl.loop(0, NV // 2)
        def _(pair):
            cols = [2 * pair, 2 * pair + 1]
            gs = [l_ref[:, c, 0] for c in cols]
            for k in range(K):
                if k > 0:
                    gs = pair_dot(l_ref, k, gs)
                for n, s in enumerate(pair_dot(d_ref, k, gs)):
                    s_ref[k, n] = s
            cs = [s_ref[K - 1, n] for n in range(2)]
            for k in range(K - 2, -1, -1):
                cs = [s_ref[k, n] - c for n, c in enumerate(pair_dot(u_ref, k, cs))]
                for n, c in enumerate(cs):
                    s_ref[k, n] = c
            for n, col in enumerate(cols):
                ab_ref[col] = s_ref[0, n]
                total = s_ref[0, n] * w_ref[0]
                for k in range(1, K):
                    total = total + s_ref[k, n] * w_ref[k]
                ab_ref[NV + col] = total


def residual_kernel(pos_ref, w_ref, r_ref, left_ref, right_ref, rad_ref, l_ref, d_ref, u_ref, out_ref, msg_ref, s_ref):
    wall, tile, last = pos_ref[0], pos_ref[1], pos_ref[2]
    row = lax.broadcasted_iota(jnp.int32, (H, S), 0)
    has_left = tile > 0
    has_right = tile < last

    def line(ref, v, k, c):
        at = 2 * (v * K + k) + c
        return jnp.broadcast_to(ref[at : at + 1, :], (H, S))

    for k in range(K):
        rad = rad_ref[k]
        l0, l1, r0, r1 = (line(ref, NV, k, c) for ref in (left_ref, right_ref) for c in (0, 1))
        zero = jnp.zeros((H, S), F32)
        f_l0 = jnp.where((row == 0) & has_left, -0.0625 * (rad + l0), zero)
        f_l1 = jnp.where(row == 0, 0.25 * (rad + l1), jnp.where(row == 1, -0.0625 * (rad + l1), zero))
        f_l1 = jnp.where(has_left, f_l1, zero)
        f_r0 = jnp.where(row == 7, 0.25 * (rad + r0), jnp.where(row == 6, -0.0625 * (rad + r0), zero))
        f_r0 = jnp.where(has_right, f_r0, zero)
        f_r1 = jnp.where((row == 7) & has_right, -0.0625 * (rad + r1), zero)
        for v in range(NV):
            applied = f_l0 * line(left_ref, v, k, 0) + f_l1 * line(left_ref, v, k, 1)
            applied = applied + (f_r0 * line(right_ref, v, k, 0) + f_r1 * line(right_ref, v, k, 1))
            out_ref[v, k] = r_ref[v, k] - applied

    @pl.when((wall == 0) | (wall == 3))
    def _():
        f = forward_sweep(l_ref, d_ref, out_ref, s_ref, None)
        b, p = backward_sweep(u_ref, s_ref, w_ref, None)
        msg_ref[:NV] = jnp.where(wall == 0, f, b)
        msg_ref[NV:] = p


def middle_kernel(pos_ref, w_ref, msg_ref, r_ref, l_ref, d_ref, u_ref, out_ref, s_ref):
    @pl.when(pos_ref[0] == 1)
    def _():
        x = msg_ref[:NV]
        out_ref[:NV] = forward_sweep(l_ref, d_ref, r_ref, s_ref, x)
        b, p = backward_sweep(u_ref, s_ref, w_ref, None)
        out_ref[NV : 2 * NV] = b
        out_ref[2 * NV :] = p + msg_ref[NV:]


def decide_kernel(
    pos_ref, w_ref, low_ref, high_ref, m1_ref, m3_ref, m0_ref, pw_ref, r_ref, l_ref, d_ref, u_ref,
    x3_ref, y2_ref, y1_ref, y0_ref, rows_ref, s_ref, prof_ref,
):
    @pl.when(pos_ref[0] == 2)
    def _():
        x3 = forward_sweep(l_ref, d_ref, r_ref, s_ref, low_ref[:NV])
        x3_ref[...] = x3
        y2 = high_ref[:NV] + map_dot(m3_ref, 0, x3)
        y2_ref[...] = y2
        total = low_ref[2 * NV :] + high_ref[NV:] + map_dot(m3_ref, NV, x3)
        y1, p2 = backward_sweep(u_ref, s_ref, w_ref, y2)
        y1_ref[...] = y1
        y0 = low_ref[NV : 2 * NV] + map_dot(m1_ref, 0, y1)
        y0_ref[...] = y0
        total = total + p2 + map_dot(m1_ref, NV, y1) + map_dot(m0_ref, 0, y0)
        for v in range(NV):
            prof_ref[v * H : (v + 1) * H, :] = total[v]
        row = lax.broadcasted_iota(jnp.int32, (SLOTS, S), 0)
        lane = lax.broadcasted_iota(jnp.int32, (SLOTS, S), 1)
        prof_ref[NV * H :, :] = (row == lane).astype(F32)
        rows_ref[...] = jnp.dot(pw_ref[...], prof_ref[...], precision=highest, preferred_element_type=F32)


def finish_kernel(pos_ref, low_ref, mid_ref, x3_ref, y2_ref, y1_ref, y0_ref, r_ref, l_ref, d_ref, u_ref, out_ref, s_ref, x_ref, y_ref):
    wall = pos_ref[0]
    zero = jnp.zeros((NV, H, S), F32)
    x = jnp.where(wall == 1, low_ref[:NV], zero)
    x = jnp.where(wall == 2, mid_ref[:NV], x)
    x_ref[...] = jnp.where(wall == 3, x3_ref[...], x)
    y = jnp.where(wall == 0, y0_ref[...], zero)
    y = jnp.where(wall == 1, y1_ref[...], y)
    y_ref[...] = jnp.where(wall == 2, y2_ref[...], y)
    forward_sweep(l_ref, d_ref, r_ref, s_ref, x_ref[...])

    def emit(k, b):
        out_ref[:, k] = b

    backward_sweep(u_ref, s_ref, None, y_ref[...], emit)


def place_kernel(count_ref, w_ref, owner_ref, tag_ref, out_ref):
    blocks = owner_ref.shape[1]
    owners = out_ref.shape[0] // ROWS_PER_OWNER
    owner = owner_ref[...]
    live = lax.broadcasted_iota(jnp.int32, (1, blocks), 1) < count_ref[0]
    hits = (owner == lax.broadcasted_iota(jnp.int32, (owners, blocks), 0)).astype(F32)
    earlier = lax.broadcasted_iota(jnp.int32, (blocks, blocks), 0) < lax.broadcasted_iota(jnp.int32, (blocks, blocks), 1)
    before = jnp.dot(hits, earlier.astype(F32), preferred_element_type=F32)
    slot = jnp.sum(before * hits, axis=0, keepdims=True).astype(jnp.int32)
    row = lax.broadcasted_iota(jnp.int32, (owners * ROWS_PER_OWNER, blocks), 0)
    placed = ((owner * ROWS_PER_OWNER + slot == row) & live).astype(F32)
    tagged = ((owner * ROWS_PER_OWNER + SLOTS == row) & live).astype(F32)
    width = NV * H
    lanes = lax.broadcasted_iota(jnp.int32, (SLOTS, blocks), 0)
    tags = jnp.where(lanes == slot, (tag_ref[...] + 1).astype(F32), 0.0)
    dims = (((1,), (1,)), ((), ()))
    out_ref[:, :width] = lax.dot_general(placed, w_ref[...], dims, precision=highest, preferred_element_type=F32)
    out_ref[:, width:] = lax.dot_general(tagged, tags, dims, precision=highest, preferred_element_type=F32)


def pick_kernel(pos_ref, got_ref, out_ref):
    rows = got_ref.shape[0]
    sources = rows // ROWS_PER_OWNER
    tag_rows = got_ref[pl.ds(SLOTS, sources, stride=ROWS_PER_OWNER), :]
    lane_of = (
        lax.broadcasted_iota(jnp.int32, (SLOTS, S), 0) == lax.broadcasted_iota(jnp.int32, (SLOTS, S), 1)
    ).astype(F32)
    tags = lax.dot_general(
        lane_of, tag_rows, (((1,), (1,)), ((), ())), precision=highest, preferred_element_type=F32
    )
    column = lax.broadcasted_iota(jnp.int32, (sources, rows), 1)
    first = lax.broadcasted_iota(jnp.int32, (sources, rows), 0) * ROWS_PER_OWNER
    spread = ((column >= first) & (column < first + ROWS_PER_OWNER)).astype(F32)
    wide = jnp.dot(tags, spread, precision=highest, preferred_element_type=F32)
    slot = lax.broadcasted_iota(jnp.int32, (SLOTS, rows), 1) % ROWS_PER_OWNER
    mine = slot == lax.broadcasted_iota(jnp.int32, (SLOTS, rows), 0)
    tag = jnp.sum(jnp.where(mine, wide, 0.0), axis=0, keepdims=True)
    target = (lax.broadcasted_iota(jnp.int32, (PATCH_DEV, rows), 0) + 1).astype(F32)
    picker = (tag == target).astype(F32)
    sums = jnp.dot(picker, got_ref[...], precision=highest, preferred_element_type=F32)
    out_ref[...] = jnp.where(pos_ref[0] == 2, sums, 0.0)


def on_device(
    adjoint, source, radius, frequency, lower, diag, upper, wall_weight,
    surface_weight, patch_owner, patch_row, surface_count,
):
    tiles = lax.axis_size("tile")
    tie = lax.optimization_barrier
    pos = jnp.stack([lax.axis_index("wall"), lax.axis_index("tile"), jnp.int32(tiles - 1)]).astype(jnp.int32)
    levels = pltpu.VMEM((K, NV, H, S), F32)
    pair_levels = pltpu.VMEM((K, 2, NV, H, S), F32)
    block, state, cell = held(NV, NV, K, H, S), held(NV, K, H, S), held(K, H, S)
    adjoint, source, radius, frequency, lower, diag, upper = (
        far_off(x) for x in (adjoint, source, radius, frequency, lower, diag, upper)
    )

    lo, hi = call("pack", pack_kernel, (f32(22 * K, S), f32(22 * K, S)), 2, nbytes=800_000)(adjoint, radius)
    left = lax.ppermute(hi, "tile", [(i, (i + 1) % tiles) for i in range(tiles)])
    right = lax.ppermute(lo, "tile", [((i + 1) % tiles, i) for i in range(tiles)])

    lo, pos1 = tie((lo, pos))
    lower, diag, upper, inner, weight, maps, q0 = call(
        "start", start_kernel, (block, block, block, state, cell, f32(2 * NV, NV, H, S), f32(NV, NV, H, S)), 9, smem=(0,),
        far=(2, 3, 4, 5, 6, 7, 8), scratch=(state, state, cell, cell, pair_levels, pltpu.SemaphoreType.DMA((7,))),
        flops=44_000_000, nbytes=11_000_000,
    )(pos1, wall_weight.reshape(1, K), adjoint, source, radius, frequency, lower, diag, upper)
    maps, left, right = tie((maps, left, right))
    map3 = lax.ppermute(maps, "wall", [(3, 2)])
    map1 = lax.ppermute(maps, "wall", [(1, 2)])
    maps, pos2 = tie((maps, pos))
    swt = surface_weight.transpose(1, 2, 0).reshape(NV * H, -1)
    placed = call(
        "place", place_kernel, held(tiles * ROWS_PER_OWNER, NV * H + SLOTS), 4, smem=(0,), flops=50_000_000, nbytes=1_000_000
    )(surface_count, swt, patch_owner.reshape(1, -1), patch_row.reshape(1, -1))

    resid, first = call(
        "residual", residual_kernel, (state, f32(2 * NV, H, S)), 9, smem=(0,), scratch=(levels,),
        flops=6_000_000, nbytes=2_000_000,
    )(pos2, weight, inner, left, right, radius, lower, diag, upper)
    low = lax.ppermute(first, "wall", [(0, 1), (3, 2)])
    second = call(
        "middle", middle_kernel, f32(3 * NV, H, S), 7, smem=(0,), scratch=(levels,), flops=5_000_000, nbytes=2_000_000
    )(pos, weight, low, resid, lower, diag, upper)
    mid = lax.ppermute(second, "wall", [(1, 2)])
    second, q0 = tie((second, q0))
    map0 = lax.ppermute(q0, "wall", [(0, 2)])

    vec = away(NV, H, S)
    x3, y2, y1, y0, rows = call(
        "decide", decide_kernel, (vec, vec, vec, vec, away(tiles * ROWS_PER_OWNER, S)), 12, smem=(0,),
        scratch=(levels, pltpu.VMEM((NV * H + SLOTS, S), F32)), flops=20_000_000, nbytes=3_000_000,
    )(pos, weight, mid, low, map1, map3, map0, placed, resid, lower, diag, upper)
    got = lax.all_to_all(rows.reshape(tiles, ROWS_PER_OWNER, 1, S), "tile", split_axis=0, concat_axis=0)
    x3 = lax.ppermute(x3, "wall", [(2, 3)])
    y1 = lax.ppermute(y1, "wall", [(2, 1)])
    y0 = lax.ppermute(y0, "wall", [(2, 0)])
    adjoint_next = call(
        "finish", finish_kernel, f32(NV, K, H, S), 11, smem=(0,),
        scratch=(levels, pltpu.VMEM((NV, H, S), F32), pltpu.VMEM((NV, H, S), F32)), flops=5_000_000, nbytes=2_000_000,
    )(pos, low, mid, x3, y2, y1, y0, resid, lower, diag, upper)
    got, adjoint_next = tie((got, adjoint_next))
    got = got.reshape(tiles * ROWS_PER_OWNER, S)
    part = call("pick", pick_kernel, f32(PATCH_DEV, S), 2, smem=(0,), flops=20_000_000, nbytes=400_000)(pos, got)
    patch = part
    for w in (0, 1, 3):
        patch = patch + lax.ppermute(part, "wall", [(2, w)])
    return adjoint_next, patch


def solution(mesh):
    in_specs = (
        P(None, "wall", "tile", None),
        P(None, "wall", "tile", None),
        P("wall", "tile", None),
        P("wall", "tile", None),
        P(None, None, "wall", "tile", None),
        P(None, None, "wall", "tile", None),
        P(None, None, "wall", "tile", None),
        P("wall"),
        P("tile", None, None),
        P("tile", None),
        P("tile"),
        P("tile"),
    )
    out_specs = (P(None, "wall", "tile", None), P("tile", None))
    return jax.shard_map(
        on_device, mesh=mesh, in_specs=in_specs, out_specs=out_specs, check_vma=False
    )
```

```python
import jax
import jax.numpy as jnp
from jax import lax
from jax.experimental import pallas as pl
from jax.experimental.pallas import tpu as pltpu
from jax.sharding import PartitionSpec as P

NV = 10
K = 8
H = 8
S = 128
PATCH_DEV = 64
SLOTS = 8
ROWS_PER_OWNER = SLOTS + 1
F32 = jnp.float32
highest = lax.Precision.HIGHEST

VM = pl.BlockSpec(memory_space=pltpu.VMEM)
SM = pl.BlockSpec(memory_space=pltpu.SMEM)
HB = pl.BlockSpec(memory_space=pltpu.HBM)


def f32(*shape):
    return jax.ShapeDtypeStruct(shape, F32)


def held(*shape):
    return pltpu.VMEM(shape, F32)


def away(*shape):
    return pltpu.HBM(shape, F32)


def far_off(x):
    return pltpu.with_memory_space_constraint(x, pltpu.HBM)


def call(name, body, out_shape, n_in, smem=(), far=(), scratch=(), flops=0, nbytes=0):
    single = not isinstance(out_shape, (tuple, list))
    run = pl.pallas_call(
        body,
        name=name,
        out_shape=out_shape,
        in_specs=[SM if i in smem else HB if i in far else VM for i in range(n_in)],
        out_specs=VM if single else [VM] * len(out_shape),
        scratch_shapes=list(scratch),
        compiler_params=pltpu.CompilerParams(vmem_limit_bytes=12 * 1024 * 1024),
        cost_estimate=pl.CostEstimate(flops=flops, bytes_accessed=nbytes, transcendentals=0),
    )
    return run


def block_dot(m_ref, k, x):
    acc = None
    for j in range(NV):
        term = m_ref[:, j, k] * x[j][None]
        acc = term if acc is None else acc + term
    return acc


def forward_sweep(l_ref, d_ref, r_ref, s_ref, x):
    f = x
    for k in range(K):
        r = r_ref[:, k]
        f = r if f is None else r + block_dot(l_ref, k, f)
        s_ref[k] = block_dot(d_ref, k, f)
    return f


def backward_sweep(u_ref, s_ref, w_ref, y, emit=None):
    b, p = y, None
    for k in range(K - 1, -1, -1):
        s = s_ref[k]
        b = s if b is None else s - block_dot(u_ref, k, b)
        if w_ref is not None:
            p = b * w_ref[k] if p is None else p + b * w_ref[k]
        if emit is not None:
            emit(k, b)
    return b, p


def map_dot(m_ref, base, x):
    acc = None
    for j in range(NV):
        term = m_ref[base + j] * x[j][None]
        acc = term if acc is None else acc + term
    return acc


def pack_kernel(a_ref, rad_ref, lo_ref, hi_ref):
    for v in range(NV + 1):
        for k in range(K):
            cell = a_ref[v, k] if v < NV else rad_ref[k]
            at = 2 * (v * K + k)
            lo_ref[at : at + 2, :] = cell[0:2]
            hi_ref[at : at + 2, :] = cell[6:8]


def pair_dot(m_ref, k, xs):
    accs = [None] * len(xs)
    for j in range(NV):
        m = m_ref[:, j, k]
        for n, x in enumerate(xs):
            term = m * x[j][None]
            accs[n] = term if accs[n] is None else accs[n] + term
    return accs


def pair_map(m_ref, half, xs):
    accs = [None] * len(xs)
    for j in range(NV):
        m = m_ref[half, j]
        for n, x in enumerate(xs):
            term = m * x[j][None]
            accs[n] = term if accs[n] is None else accs[n] + term
    return accs


def interior(a_ref, src_ref, rad_ref, frq_ref, out_ref):
    row = lax.broadcasted_iota(jnp.int32, (H, S), 0)
    lane = lax.broadcasted_iota(jnp.int32, (H, S), 1)
    for k in range(K):
        a = a_ref[:, k]
        rad = rad_ref[k]
        applied = None
        for d, w in ((-2, -0.0625), (-1, 0.25), (1, 0.25), (2, -0.0625)):
            inside = (row + d >= 0) & (row + d < H)
            coef = jnp.where(inside, w * (rad + pltpu.roll(rad, (-d) % H, 0)), 0.0)
            term = coef[None] * pltpu.roll(a, (-d) % H, 1)
            applied = term if applied is None else applied + term
        for d in (-1, 1):
            inside = (lane + d >= 0) & (lane + d < S)
            coef = jnp.where(inside, 0.25 * (rad + pltpu.roll(rad, (-d) % S, 1)), 0.0)
            applied = applied + coef[None] * pltpu.roll(a, (-d) % S, 2)
        frq = frq_ref[k][None]
        half = NV // 2
        src = src_ref[:, k] - applied
        out_ref[:half, k] = src[:half] + frq * a[half:]
        out_ref[half:, k] = src[half:] - frq * a[:half]


def start_kernel(
    pos_ref, w_in, a_in, src_in, rad_in, frq_in, l_in, d_in, u_in,
    l_ref, d_ref, u_ref, r_ref, w_ref, map_ref, a_ref, src_ref, rad_ref, frq_ref, s_ref, state_sems, block_sems,
):
    wall = pos_ref[0]
    state = [
        pltpu.make_async_copy(there, here, state_sems.at[n])
        for n, (there, here) in enumerate(((a_in, a_ref), (src_in, src_ref), (rad_in, rad_ref), (frq_in, frq_ref)))
    ]
    blocks = [
        [
            pltpu.make_async_copy(there.at[:, :, k], here.at[:, :, k], block_sems.at[k, n])
            for n, (there, here) in enumerate(((l_in, l_ref), (d_in, d_ref), (u_in, u_ref)))
        ]
        for k in range(K)
    ]
    for copy in state:
        copy.start()
    for k in range(K - 1, -1, -1):
        for copy in blocks[k]:
            copy.start()
    for k in range(K):
        w_ref[k] = jnp.broadcast_to(w_in[:, k : k + 1], (H, S))
    for copy in state:
        copy.wait()
    interior(a_ref, src_ref, rad_ref, frq_ref, r_ref)

    def arrived(k):
        for copy in blocks[k]:
            copy.wait()

    @pl.when((wall == 0) | (wall == 2))
    def _():
        for k in range(K - 1, -1, -1):
            arrived(k)

    @pl.when(wall == 1)
    def _():
        arrived(K - 1)
        for c in range(NV):
            s_ref[(K - 1) % 2, c] = u_ref[:, c, K - 1]
        for k in range(K - 2, -1, -1):
            arrived(k)

            @pl.loop(0, NV // 2)
            def _(pair):
                cols = [2 * pair, 2 * pair + 1]
                outs = pair_dot(u_ref, k, [s_ref[(k + 1) % 2, c] for c in cols])
                for c, out in zip(cols, outs):
                    if k > 0:
                        s_ref[k % 2, c] = out
                    else:
                        map_ref[c] = out

    @pl.when(wall == 3)
    def _():
        arrived(K - 1)
        for c in range(NV):
            s_ref[(K - 1) % 2, c] = d_ref[:, c, K - 1]
        for k in range(K - 2, -1, -1):
            arrived(k)

            @pl.loop(0, NV // 2)
            def _(pair):
                cols = [2 * pair, 2 * pair + 1]
                outs = pair_map(s_ref, (k + 1) % 2, [l_ref[:, c, k + 1] for c in cols])
                outs = pair_dot(u_ref, k, outs)
                for c, out in zip(cols, outs):
                    s_ref[k % 2, c] = d_ref[:, c, k] - out

        @pl.loop(0, NV // 2)
        def _(pair):
            cols = [2 * pair, 2 * pair + 1]
            for c, out in zip(cols, pair_map(s_ref, 0, [l_ref[:, c, 0] for c in cols])):
                map_ref[c] = out


def residual_kernel(pos_ref, r_ref, left_ref, right_ref, rad_ref, l_ref, d_ref, u_ref, out_ref, msg_ref, s_ref):
    wall, tile, last = pos_ref[0], pos_ref[1], pos_ref[2]
    row = lax.broadcasted_iota(jnp.int32, (H, S), 0)
    has_left = tile > 0
    has_right = tile < last

    def line(ref, v, k, c):
        at = 2 * (v * K + k) + c
        return jnp.broadcast_to(ref[at : at + 1, :], (H, S))

    for k in range(K):
        rad = rad_ref[k]
        l0, l1, r0, r1 = (line(ref, NV, k, c) for ref in (left_ref, right_ref) for c in (0, 1))
        zero = jnp.zeros((H, S), F32)
        f_l0 = jnp.where((row == 0) & has_left, -0.0625 * (rad + l0), zero)
        f_l1 = jnp.where(row == 0, 0.25 * (rad + l1), jnp.where(row == 1, -0.0625 * (rad + l1), zero))
        f_l1 = jnp.where(has_left, f_l1, zero)
        f_r0 = jnp.where(row == 7, 0.25 * (rad + r0), jnp.where(row == 6, -0.0625 * (rad + r0), zero))
        f_r0 = jnp.where(has_right, f_r0, zero)
        f_r1 = jnp.where((row == 7) & has_right, -0.0625 * (rad + r1), zero)
        for v in range(NV):
            applied = f_l0 * line(left_ref, v, k, 0) + f_l1 * line(left_ref, v, k, 1)
            applied = applied + (f_r0 * line(right_ref, v, k, 0) + f_r1 * line(right_ref, v, k, 1))
            out_ref[v, k] = r_ref[v, k] - applied

    @pl.when((wall == 0) | (wall == 3))
    def _():
        f = forward_sweep(l_ref, d_ref, out_ref, s_ref, None)
        b, _ = backward_sweep(u_ref, s_ref, None, None)
        msg_ref[...] = jnp.where(wall == 0, f, b)


def middle_kernel(pos_ref, x_ref, map_ref, r_ref, l_ref, d_ref, u_ref, out_ref, below_ref, s_ref):
    @pl.when(pos_ref[0] == 1)
    def _():
        out_ref[...] = forward_sweep(l_ref, d_ref, r_ref, s_ref, x_ref[...])
        below_ref[NV] = backward_sweep(u_ref, s_ref, None, None)[0]
        for c in range(NV):
            below_ref[c] = map_ref[c]


def decide_kernel(pos_ref, x_ref, b_ref, map_ref, r_ref, l_ref, d_ref, u_ref, x3_ref, y2_ref, y1_ref, s_ref):
    @pl.when(pos_ref[0] == 2)
    def _():
        x3 = forward_sweep(l_ref, d_ref, r_ref, s_ref, x_ref[...])
        x3_ref[...] = x3
        y2 = b_ref[...] + map_dot(map_ref, 0, x3)
        y2_ref[...] = y2
        y1_ref[...] = backward_sweep(u_ref, s_ref, None, y2)[0]


def finish_kernel(
    pos_ref, x1_ref, x2_ref, x3_ref, y2_ref, y1_ref, y10_ref, below_ref, w_ref, pw_ref, r_ref, l_ref, d_ref, u_ref,
    out_ref, rows_ref, s_ref, x_ref, y_ref, prof_ref,
):
    wall = pos_ref[0]

    @pl.when(wall == 0)
    def _():
        x_ref[...] = jnp.zeros((NV, H, S), F32)
        y_ref[...] = below_ref[NV] + map_dot(below_ref, 0, y10_ref[...])

    @pl.when(wall == 1)
    def _():
        x_ref[...] = x1_ref[...]
        y_ref[...] = y1_ref[...]

    @pl.when(wall == 2)
    def _():
        x_ref[...] = x2_ref[...]
        y_ref[...] = y2_ref[...]

    @pl.when(wall == 3)
    def _():
        x_ref[...] = x3_ref[...]
        y_ref[...] = jnp.zeros((NV, H, S), F32)

    forward_sweep(l_ref, d_ref, r_ref, s_ref, x_ref[...])

    def emit(k, b):
        out_ref[:, k] = b

    _, profile = backward_sweep(u_ref, s_ref, w_ref, y_ref[...], emit)
    for v in range(NV):
        prof_ref[v * H : (v + 1) * H, :] = profile[v]
    row = lax.broadcasted_iota(jnp.int32, (SLOTS, S), 0)
    lane = lax.broadcasted_iota(jnp.int32, (SLOTS, S), 1)
    prof_ref[NV * H :, :] = (row == lane).astype(F32)
    rows_ref[...] = jnp.dot(pw_ref[...], prof_ref[...], precision=highest, preferred_element_type=F32)


def place_kernel(count_ref, w_ref, owner_ref, tag_ref, out_ref):
    blocks = owner_ref.shape[1]
    owners = out_ref.shape[0] // ROWS_PER_OWNER
    owner = owner_ref[...]
    live = lax.broadcasted_iota(jnp.int32, (1, blocks), 1) < count_ref[0]
    hits = (owner == lax.broadcasted_iota(jnp.int32, (owners, blocks), 0)).astype(F32)
    earlier = lax.broadcasted_iota(jnp.int32, (blocks, blocks), 0) < lax.broadcasted_iota(jnp.int32, (blocks, blocks), 1)
    before = jnp.dot(hits, earlier.astype(F32), preferred_element_type=F32)
    slot = jnp.sum(before * hits, axis=0, keepdims=True).astype(jnp.int32)
    row = lax.broadcasted_iota(jnp.int32, (owners * ROWS_PER_OWNER, blocks), 0)
    placed = ((owner * ROWS_PER_OWNER + slot == row) & live).astype(F32)
    tagged = ((owner * ROWS_PER_OWNER + SLOTS == row) & live).astype(F32)
    width = NV * H
    lanes = lax.broadcasted_iota(jnp.int32, (SLOTS, blocks), 0)
    tags = jnp.where(lanes == slot, (tag_ref[...] + 1).astype(F32), 0.0)
    dims = (((1,), (1,)), ((), ()))
    out_ref[:, :width] = lax.dot_general(placed, w_ref[...], dims, precision=highest, preferred_element_type=F32)
    out_ref[:, width:] = lax.dot_general(tagged, tags, dims, precision=highest, preferred_element_type=F32)


def pick_kernel(got_ref, out_ref):
    rows = got_ref.shape[0]
    sources = rows // ROWS_PER_OWNER
    tag_rows = got_ref[pl.ds(SLOTS, sources, stride=ROWS_PER_OWNER), :]
    lane_of = (
        lax.broadcasted_iota(jnp.int32, (SLOTS, S), 0) == lax.broadcasted_iota(jnp.int32, (SLOTS, S), 1)
    ).astype(F32)
    tags = lax.dot_general(
        lane_of, tag_rows, (((1,), (1,)), ((), ())), precision=highest, preferred_element_type=F32
    )
    column = lax.broadcasted_iota(jnp.int32, (sources, rows), 1)
    first = lax.broadcasted_iota(jnp.int32, (sources, rows), 0) * ROWS_PER_OWNER
    spread = ((column >= first) & (column < first + ROWS_PER_OWNER)).astype(F32)
    wide = jnp.dot(tags, spread, precision=highest, preferred_element_type=F32)
    slot = lax.broadcasted_iota(jnp.int32, (SLOTS, rows), 1) % ROWS_PER_OWNER
    mine = slot == lax.broadcasted_iota(jnp.int32, (SLOTS, rows), 0)
    tag = jnp.sum(jnp.where(mine, wide, 0.0), axis=0, keepdims=True)
    target = (lax.broadcasted_iota(jnp.int32, (PATCH_DEV, rows), 0) + 1).astype(F32)
    picker = (tag == target).astype(F32)
    out_ref[...] = jnp.dot(picker, got_ref[...], precision=highest, preferred_element_type=F32)


def on_device(
    adjoint, source, radius, frequency, lower, diag, upper, wall_weight,
    surface_weight, patch_owner, patch_row, surface_count,
):
    tiles = lax.axis_size("tile")
    tie = lax.optimization_barrier
    pos = jnp.stack([lax.axis_index("wall"), lax.axis_index("tile"), jnp.int32(tiles - 1)]).astype(jnp.int32)
    levels = held(K, NV, H, S)
    block, state, cell, vec = held(NV, NV, K, H, S), held(NV, K, H, S), held(K, H, S), f32(NV, H, S)
    adjoint, source, radius, frequency, lower, diag, upper, wall_weight = (
        far_off(x)
        for x in (adjoint, source, radius, frequency, lower, diag, upper, wall_weight.reshape(1, K))
    )

    lo, hi = call("pack", pack_kernel, (f32(22 * K, S), f32(22 * K, S)), 2, nbytes=800_000)(adjoint, radius)
    left = lax.ppermute(hi, "tile", [(i, (i + 1) % tiles) for i in range(tiles)])
    right = lax.ppermute(lo, "tile", [((i + 1) % tiles, i) for i in range(tiles)])

    lo, pos1 = tie((lo, pos))
    lower, diag, upper, inner, weight, maps = call(
        "start", start_kernel, (block, block, block, state, cell, f32(NV, NV, H, S)), 9, smem=(0,),
        far=(2, 3, 4, 5, 6, 7, 8),
        scratch=(
            state, state, cell, cell, held(2, NV, NV, H, S), pltpu.SemaphoreType.DMA((4,)), pltpu.SemaphoreType.DMA((K, 3)),
        ),
        flops=30_000_000, nbytes=11_000_000,
    )(pos1, wall_weight, adjoint, source, radius, frequency, lower, diag, upper)
    maps, left, right = tie((maps, left, right))
    map3 = lax.ppermute(maps, "wall", [(3, 2)])

    resid, first = call(
        "residual", residual_kernel, (state, vec), 8, smem=(0,), scratch=(levels,),
        flops=6_000_000, nbytes=2_000_000,
    )(pos, inner, left, right, radius, lower, diag, upper)
    x1 = b3 = lax.ppermute(first, "wall", [(0, 1), (3, 2)])
    x2, below = call(
        "middle", middle_kernel, (vec, f32(NV + 1, NV, H, S)), 7, smem=(0,), scratch=(levels,), flops=5_000_000, nbytes=2_000_000
    )(pos, x1, maps, resid, lower, diag, upper)
    x2 = lax.ppermute(x2, "wall", [(1, 2)])
    x2, below = tie((x2, below))
    below = lax.ppermute(below, "wall", [(1, 0)])

    swt = surface_weight.transpose(1, 2, 0).reshape(NV * H, -1)
    placed = call(
        "place", place_kernel, held(tiles * ROWS_PER_OWNER, NV * H + SLOTS), 4, smem=(0,), flops=50_000_000, nbytes=1_000_000
    )(surface_count, swt, patch_owner.reshape(1, -1), patch_row.reshape(1, -1))

    x3, y2, y1 = call(
        "decide", decide_kernel, (vec, vec, vec), 8, smem=(0,), scratch=(levels,), flops=20_000_000, nbytes=3_000_000,
    )(pos, x2, b3, map3, resid, lower, diag, upper)
    x3 = lax.ppermute(x3, "wall", [(2, 3)])
    y11 = lax.ppermute(y1, "wall", [(2, 1)])
    y10 = lax.ppermute(y1, "wall", [(2, 0)])
    adjoint_next, rows = call(
        "finish", finish_kernel, (f32(NV, K, H, S), away(tiles * ROWS_PER_OWNER, S)), 14, smem=(0,),
        scratch=(levels, held(NV, H, S), held(NV, H, S), held(NV * H + SLOTS, S)), flops=5_000_000, nbytes=2_000_000,
    )(pos, x1, x2, x3, y2, y11, y10, below, weight, placed, resid, lower, diag, upper)
    got = lax.all_to_all(rows.reshape(tiles, ROWS_PER_OWNER, 1, S), "tile", split_axis=0, concat_axis=0)
    got = got.reshape(tiles * ROWS_PER_OWNER, S)
    part = call("pick", pick_kernel, f32(PATCH_DEV, S), 1, flops=20_000_000, nbytes=400_000)(got)
    walls = lax.axis_size("wall")
    patch = part
    for d in range(1, walls):
        patch = patch + lax.ppermute(part, "wall", [(w, (w + d) % walls) for w in range(walls)])
    return adjoint_next, patch


def solution(mesh):
    in_specs = (
        P(None, "wall", "tile", None),
        P(None, "wall", "tile", None),
        P("wall", "tile", None),
        P("wall", "tile", None),
        P(None, None, "wall", "tile", None),
        P(None, None, "wall", "tile", None),
        P(None, None, "wall", "tile", None),
        P("wall"),
        P("tile", None, None),
        P("tile", None),
        P("tile"),
        P("tile"),
    )
    out_specs = (P(None, "wall", "tile", None), P("tile", None))
    return jax.shard_map(
        on_device, mesh=mesh, in_specs=in_specs, out_specs=out_specs, check_vma=False
    )
```

```python
import jax
import jax.numpy as jnp
from jax import lax
from jax.experimental import pallas as pl
from jax.experimental.pallas import tpu as pltpu
from jax.sharding import PartitionSpec as P

NV = 10
K = 8
H = 8
S = 128
PATCH_DEV = 64
SLOTS = 8
ROWS_PER_OWNER = SLOTS + 1
F32 = jnp.float32
highest = lax.Precision.HIGHEST

VM = pl.BlockSpec(memory_space=pltpu.VMEM)
SM = pl.BlockSpec(memory_space=pltpu.SMEM)
HB = pl.BlockSpec(memory_space=pltpu.HBM)


def f32(*shape):
    return jax.ShapeDtypeStruct(shape, F32)


def held(*shape):
    return pltpu.VMEM(shape, F32)


def away(*shape):
    return pltpu.HBM(shape, F32)


def far_off(x):
    return pltpu.with_memory_space_constraint(x, pltpu.HBM)


def call(name, body, out_shape, n_in, smem=(), far=(), scratch=(), flops=0, nbytes=0):
    single = not isinstance(out_shape, (tuple, list))
    run = pl.pallas_call(
        body,
        name=name,
        out_shape=out_shape,
        in_specs=[SM if i in smem else HB if i in far else VM for i in range(n_in)],
        out_specs=VM if single else [VM] * len(out_shape),
        scratch_shapes=list(scratch),
        compiler_params=pltpu.CompilerParams(vmem_limit_bytes=12 * 1024 * 1024),
        cost_estimate=pl.CostEstimate(flops=flops, bytes_accessed=nbytes, transcendentals=0),
    )
    return run


def block_dot(m_ref, k, x):
    acc = None
    for j in range(NV):
        term = m_ref[:, j, k] * x[j][None]
        acc = term if acc is None else acc + term
    return acc


def forward_sweep(l_ref, d_ref, r_ref, s_ref, x):
    f = x
    for k in range(K):
        r = r_ref[:, k]
        f = r if f is None else r + block_dot(l_ref, k, f)
        s_ref[k] = block_dot(d_ref, k, f)
    return f


def backward_sweep(u_ref, s_ref, w_ref, y, emit=None):
    b, p = y, None
    for k in range(K - 1, -1, -1):
        s = s_ref[k]
        b = s if b is None else s - block_dot(u_ref, k, b)
        if w_ref is not None:
            p = b * w_ref[k] if p is None else p + b * w_ref[k]
        if emit is not None:
            emit(k, b)
    return b, p


def map_dot(m_ref, base, x):
    acc = None
    for j in range(NV):
        term = m_ref[base + j] * x[j][None]
        acc = term if acc is None else acc + term
    return acc


def pack_kernel(a_ref, rad_ref, lo_ref, hi_ref):
    for v in range(NV + 1):
        for k in range(K):
            cell = a_ref[v, k] if v < NV else rad_ref[k]
            at = 2 * (v * K + k)
            lo_ref[at : at + 2, :] = cell[0:2]
            hi_ref[at : at + 2, :] = cell[6:8]


def pair_dot(m_ref, k, xs):
    accs = [None] * len(xs)
    for j in range(NV):
        m = m_ref[:, j, k]
        for n, x in enumerate(xs):
            term = m * x[j][None]
            accs[n] = term if accs[n] is None else accs[n] + term
    return accs


def pair_map(m_ref, half, xs):
    accs = [None] * len(xs)
    for j in range(NV):
        m = m_ref[half, j]
        for n, x in enumerate(xs):
            term = m * x[j][None]
            accs[n] = term if accs[n] is None else accs[n] + term
    return accs


def interior(a_ref, src_ref, rad_ref, frq_ref, out_ref):
    row = lax.broadcasted_iota(jnp.int32, (H, S), 0)
    lane = lax.broadcasted_iota(jnp.int32, (H, S), 1)
    for k in range(K):
        a = a_ref[:, k]
        rad = rad_ref[k]
        applied = None
        for d, w in ((-2, -0.0625), (-1, 0.25), (1, 0.25), (2, -0.0625)):
            inside = (row + d >= 0) & (row + d < H)
            coef = jnp.where(inside, w * (rad + pltpu.roll(rad, (-d) % H, 0)), 0.0)
            term = coef[None] * pltpu.roll(a, (-d) % H, 1)
            applied = term if applied is None else applied + term
        for d in (-1, 1):
            inside = (lane + d >= 0) & (lane + d < S)
            coef = jnp.where(inside, 0.25 * (rad + pltpu.roll(rad, (-d) % S, 1)), 0.0)
            applied = applied + coef[None] * pltpu.roll(a, (-d) % S, 2)
        frq = frq_ref[k][None]
        half = NV // 2
        src = src_ref[:, k] - applied
        out_ref[:half, k] = src[:half] + frq * a[half:]
        out_ref[half:, k] = src[half:] - frq * a[:half]


def start_kernel(
    pos_ref, w_in, a_in, src_in, rad_in, frq_in, l_in, d_in, u_in,
    l_ref, d_ref, u_ref, r_ref, w_ref, map_ref, a_ref, src_ref, rad_ref, frq_ref, s_ref, state_sems, block_sems,
):
    wall = pos_ref[0]
    state = [
        pltpu.make_async_copy(there, here, state_sems.at[n])
        for n, (there, here) in enumerate(((a_in, a_ref), (src_in, src_ref), (rad_in, rad_ref), (frq_in, frq_ref)))
    ]
    blocks = [
        [
            pltpu.make_async_copy(there.at[:, :, k], here.at[:, :, k], block_sems.at[k, n])
            for n, (there, here) in enumerate(((l_in, l_ref), (d_in, d_ref), (u_in, u_ref)))
        ]
        for k in range(K)
    ]
    def depart(k):
        if k >= 0:
            for copy in blocks[k]:
                copy.start()

    def arrived(k):
        for copy in blocks[k]:
            copy.wait()

    ahead = 2
    for copy in state:
        copy.start()
    for k in range(K - 1, K - 1 - ahead, -1):
        depart(k)
    for k in range(K):
        w_ref[k] = jnp.broadcast_to(w_in[:, k : k + 1], (H, S))
    for copy in state:
        copy.wait()

    @pl.when(wall != 3)
    def _():
        for k in range(K - 1 - ahead, -1, -1):
            depart(k)

    interior(a_ref, src_ref, rad_ref, frq_ref, r_ref)

    @pl.when(wall != 3)
    def _():
        for k in range(K - 1, -1, -1):
            arrived(k)

    @pl.when(wall == 3)
    def _():
        arrived(K - 1)
        depart(K - 1 - ahead)
        for c in range(NV):
            s_ref[(K - 1) % 2, c] = d_ref[:, c, K - 1]
        for k in range(K - 2, -1, -1):
            arrived(k)
            depart(k - ahead)

            @pl.loop(0, NV // 2)
            def _(pair):
                cols = [2 * pair, 2 * pair + 1]
                outs = pair_map(s_ref, (k + 1) % 2, [l_ref[:, c, k + 1] for c in cols])
                outs = pair_dot(u_ref, k, outs)
                for c, out in zip(cols, outs):
                    s_ref[k % 2, c] = d_ref[:, c, k] - out

        @pl.loop(0, NV // 2)
        def _(pair):
            cols = [2 * pair, 2 * pair + 1]
            for c, out in zip(cols, pair_map(s_ref, 0, [l_ref[:, c, 0] for c in cols])):
                map_ref[c] = out


def residual_kernel(pos_ref, map_ref, r_ref, left_ref, right_ref, rad_ref, l_ref, d_ref, u_ref, out_ref, up_ref, down_ref, s_ref):
    wall, tile, last = pos_ref[0], pos_ref[1], pos_ref[2]
    row = lax.broadcasted_iota(jnp.int32, (H, S), 0)
    has_left = tile > 0
    has_right = tile < last

    def line(ref, v, k, c):
        at = 2 * (v * K + k) + c
        return jnp.broadcast_to(ref[at : at + 1, :], (H, S))

    for k in range(K):
        rad = rad_ref[k]
        l0, l1, r0, r1 = (line(ref, NV, k, c) for ref in (left_ref, right_ref) for c in (0, 1))
        zero = jnp.zeros((H, S), F32)
        f_l0 = jnp.where((row == 0) & has_left, -0.0625 * (rad + l0), zero)
        f_l1 = jnp.where(row == 0, 0.25 * (rad + l1), jnp.where(row == 1, -0.0625 * (rad + l1), zero))
        f_l1 = jnp.where(has_left, f_l1, zero)
        f_r0 = jnp.where(row == 7, 0.25 * (rad + r0), jnp.where(row == 6, -0.0625 * (rad + r0), zero))
        f_r0 = jnp.where(has_right, f_r0, zero)
        f_r1 = jnp.where((row == 7) & has_right, -0.0625 * (rad + r1), zero)
        for v in range(NV):
            applied = f_l0 * line(left_ref, v, k, 0) + f_l1 * line(left_ref, v, k, 1)
            applied = applied + (f_r0 * line(right_ref, v, k, 0) + f_r1 * line(right_ref, v, k, 1))
            out_ref[v, k] = r_ref[v, k] - applied

    @pl.when((wall == 0) | (wall == 3))
    def _():
        f = forward_sweep(l_ref, d_ref, out_ref, s_ref, None)
        up_ref[...] = f
        down_ref[NV] = backward_sweep(u_ref, s_ref, None, None)[0]

    @pl.when(wall == 3)
    def _():
        for c in range(NV):
            down_ref[c] = map_ref[c]


def middle_kernel(pos_ref, x_ref, r_ref, l_ref, d_ref, u_ref, out_ref, s_ref):
    @pl.when(pos_ref[0] == 1)
    def _():
        f = x_ref[...]
        for k in range(K):
            f = r_ref[:, k] + block_dot(l_ref, k, f)
        out_ref[...] = f


def below_kernel(pos_ref, x_ref, r_ref, l_ref, d_ref, u_ref, below_ref, s_ref):
    @pl.when(pos_ref[0] == 1)
    def _():
        forward_sweep(l_ref, d_ref, r_ref, s_ref, x_ref[...])
        below_ref[NV] = backward_sweep(u_ref, s_ref, None, None)[0]

        @pl.loop(0, NV // 2)
        def _(pair):
            cols = [2 * pair, 2 * pair + 1]
            xs = [u_ref[:, c, K - 1] for c in cols]
            for k in range(K - 2, -1, -1):
                xs = pair_dot(u_ref, k, xs)
            for c, x in zip(cols, xs):
                below_ref[c] = x


def decide_kernel(pos_ref, x_ref, map_ref, r_ref, l_ref, d_ref, u_ref, x3_ref, y2_ref, y1_ref, s_ref):
    @pl.when(pos_ref[0] == 2)
    def _():
        x3 = forward_sweep(l_ref, d_ref, r_ref, s_ref, x_ref[...])
        x3_ref[...] = x3
        y2 = map_ref[NV] + map_dot(map_ref, 0, x3)
        y2_ref[...] = y2
        y1_ref[...] = backward_sweep(u_ref, s_ref, None, y2)[0]


def finish_kernel(
    pos_ref, x1_ref, x2_ref, x3_ref, y2_ref, y1_ref, y10_ref, below_ref, w_ref, pw_ref, r_ref, l_ref, d_ref, u_ref,
    out_ref, rows_ref, s_ref, x_ref, y_ref, prof_ref,
):
    wall = pos_ref[0]

    @pl.when(wall == 0)
    def _():
        x_ref[...] = jnp.zeros((NV, H, S), F32)
        y_ref[...] = below_ref[NV] + map_dot(below_ref, 0, y10_ref[...])

    @pl.when(wall == 1)
    def _():
        x_ref[...] = x1_ref[...]
        y_ref[...] = y1_ref[...]

    @pl.when(wall == 2)
    def _():
        x_ref[...] = x2_ref[...]
        y_ref[...] = y2_ref[...]

    @pl.when(wall == 3)
    def _():
        x_ref[...] = x3_ref[...]
        y_ref[...] = jnp.zeros((NV, H, S), F32)

    forward_sweep(l_ref, d_ref, r_ref, s_ref, x_ref[...])

    def emit(k, b):
        out_ref[:, k] = b

    _, profile = backward_sweep(u_ref, s_ref, w_ref, y_ref[...], emit)
    for v in range(NV):
        prof_ref[v * H : (v + 1) * H, :] = profile[v]
    row = lax.broadcasted_iota(jnp.int32, (SLOTS, S), 0)
    lane = lax.broadcasted_iota(jnp.int32, (SLOTS, S), 1)
    prof_ref[NV * H :, :] = (row == lane).astype(F32)
    rows_ref[...] = jnp.dot(pw_ref[...], prof_ref[...], precision=highest, preferred_element_type=F32)


def place_kernel(count_ref, w_ref, owner_ref, tag_ref, out_ref):
    blocks = owner_ref.shape[1]
    owners = out_ref.shape[0] // ROWS_PER_OWNER
    owner = owner_ref[...]
    live = lax.broadcasted_iota(jnp.int32, (1, blocks), 1) < count_ref[0]
    hits = (owner == lax.broadcasted_iota(jnp.int32, (owners, blocks), 0)).astype(F32)
    earlier = lax.broadcasted_iota(jnp.int32, (blocks, blocks), 0) < lax.broadcasted_iota(jnp.int32, (blocks, blocks), 1)
    before = jnp.dot(hits, earlier.astype(F32), preferred_element_type=F32)
    slot = jnp.sum(before * hits, axis=0, keepdims=True).astype(jnp.int32)
    row = lax.broadcasted_iota(jnp.int32, (owners * ROWS_PER_OWNER, blocks), 0)
    placed = ((owner * ROWS_PER_OWNER + slot == row) & live).astype(F32)
    tagged = ((owner * ROWS_PER_OWNER + SLOTS == row) & live).astype(F32)
    width = NV * H
    lanes = lax.broadcasted_iota(jnp.int32, (SLOTS, blocks), 0)
    tags = jnp.where(lanes == slot, (tag_ref[...] + 1).astype(F32), 0.0)
    dims = (((1,), (1,)), ((), ()))
    out_ref[:, :width] = lax.dot_general(placed, w_ref[...], dims, precision=highest, preferred_element_type=F32)
    out_ref[:, width:] = lax.dot_general(tagged, tags, dims, precision=highest, preferred_element_type=F32)


def pick_kernel(got_ref, out_ref):
    rows = got_ref.shape[0]
    sources = rows // ROWS_PER_OWNER
    tag_rows = got_ref[pl.ds(SLOTS, sources, stride=ROWS_PER_OWNER), :]
    lane_of = (
        lax.broadcasted_iota(jnp.int32, (SLOTS, S), 0) == lax.broadcasted_iota(jnp.int32, (SLOTS, S), 1)
    ).astype(F32)
    tags = lax.dot_general(
        lane_of, tag_rows, (((1,), (1,)), ((), ())), precision=highest, preferred_element_type=F32
    )
    column = lax.broadcasted_iota(jnp.int32, (sources, rows), 1)
    first = lax.broadcasted_iota(jnp.int32, (sources, rows), 0) * ROWS_PER_OWNER
    spread = ((column >= first) & (column < first + ROWS_PER_OWNER)).astype(F32)
    wide = jnp.dot(tags, spread, precision=highest, preferred_element_type=F32)
    slot = lax.broadcasted_iota(jnp.int32, (SLOTS, rows), 1) % ROWS_PER_OWNER
    mine = slot == lax.broadcasted_iota(jnp.int32, (SLOTS, rows), 0)
    tag = jnp.sum(jnp.where(mine, wide, 0.0), axis=0, keepdims=True)
    target = (lax.broadcasted_iota(jnp.int32, (PATCH_DEV, rows), 0) + 1).astype(F32)
    picker = (tag == target).astype(F32)
    out_ref[...] = jnp.dot(picker, got_ref[...], precision=highest, preferred_element_type=F32)


def on_device(
    adjoint, source, radius, frequency, lower, diag, upper, wall_weight,
    surface_weight, patch_owner, patch_row, surface_count,
):
    tiles = lax.axis_size("tile")
    tie = lax.optimization_barrier
    pos = jnp.stack([lax.axis_index("wall"), lax.axis_index("tile"), jnp.int32(tiles - 1)]).astype(jnp.int32)
    levels = held(K, NV, H, S)
    block, state, cell, vec = held(NV, NV, K, H, S), held(NV, K, H, S), held(K, H, S), f32(NV, H, S)
    adjoint, source, radius, frequency, lower, diag, upper, wall_weight = (
        far_off(x)
        for x in (adjoint, source, radius, frequency, lower, diag, upper, wall_weight.reshape(1, K))
    )

    lo, hi = call("pack", pack_kernel, (f32(22 * K, S), f32(22 * K, S)), 2, nbytes=800_000)(adjoint, radius)
    left = lax.ppermute(hi, "tile", [(i, (i + 1) % tiles) for i in range(tiles)])
    right = lax.ppermute(lo, "tile", [((i + 1) % tiles, i) for i in range(tiles)])

    lo, pos1 = tie((lo, pos))
    lower, diag, upper, inner, weight, maps = call(
        "start", start_kernel, (block, block, block, state, cell, f32(NV, NV, H, S)), 9, smem=(0,),
        far=(2, 3, 4, 5, 6, 7, 8),
        scratch=(
            state, state, cell, cell, held(2, NV, NV, H, S), pltpu.SemaphoreType.DMA((4,)), pltpu.SemaphoreType.DMA((K, 3)),
        ),
        flops=30_000_000, nbytes=11_000_000,
    )(pos1, wall_weight, adjoint, source, radius, frequency, lower, diag, upper)

    resid, up, down = call(
        "residual", residual_kernel, (state, vec, f32(NV + 1, NV, H, S)), 9, smem=(0,), scratch=(levels,)
    )(pos, maps, inner, left, right, radius, lower, diag, upper)
    x1 = lax.ppermute(up, "wall", [(0, 1)])
    above = lax.ppermute(down, "wall", [(3, 2)])
    x2 = call("middle", middle_kernel, vec, 6, smem=(0,), scratch=(levels,))(pos, x1, resid, lower, diag, upper)
    x2, pos2 = tie((x2, pos))
    x2 = lax.ppermute(x2, "wall", [(1, 2)])
    below = call("below", below_kernel, f32(NV + 1, NV, H, S), 6, smem=(0,), scratch=(levels,))(
        pos2, x1, resid, lower, diag, upper
    )
    swt = surface_weight.transpose(1, 2, 0).reshape(NV * H, -1)
    placed = call("place", place_kernel, held(tiles * ROWS_PER_OWNER, NV * H + SLOTS), 4, smem=(0,))(
        surface_count, swt, patch_owner.reshape(1, -1), patch_row.reshape(1, -1)
    )

    x2, placed = tie((x2, placed))
    x3, y2, y1 = call(
        "decide", decide_kernel, (vec, vec, vec), 7, smem=(0,), scratch=(levels,)
    )(pos, x2, above, resid, lower, diag, upper)
    x3, below = tie((x3, below))
    below = lax.ppermute(below, "wall", [(1, 0)])
    x3 = lax.ppermute(x3, "wall", [(2, 3)])
    y11 = lax.ppermute(y1, "wall", [(2, 1)])
    y10 = lax.ppermute(y1, "wall", [(2, 0)])
    adjoint_next, rows = call(
        "finish", finish_kernel, (f32(NV, K, H, S), away(tiles * ROWS_PER_OWNER, S)), 14, smem=(0,),
        scratch=(levels, held(NV, H, S), held(NV, H, S), held(NV * H + SLOTS, S)),
    )(pos, x1, x2, x3, y2, y11, y10, below, weight, placed, resid, lower, diag, upper)
    got = lax.all_to_all(rows.reshape(tiles, ROWS_PER_OWNER, 1, S), "tile", split_axis=0, concat_axis=0)
    got = got.reshape(tiles * ROWS_PER_OWNER, S)
    part = call("pick", pick_kernel, f32(PATCH_DEV, S), 1)(got)
    walls = lax.axis_size("wall")
    patch = part
    for d in range(1, walls):
        patch = patch + lax.ppermute(part, "wall", [(w, (w + d) % walls) for w in range(walls)])
    return adjoint_next, patch


def solution(mesh):
    in_specs = (
        P(None, "wall", "tile", None),
        P(None, "wall", "tile", None),
        P("wall", "tile", None),
        P("wall", "tile", None),
        P(None, None, "wall", "tile", None),
        P(None, None, "wall", "tile", None),
        P(None, None, "wall", "tile", None),
        P("wall"),
        P("tile", None, None),
        P("tile", None),
        P("tile"),
        P("tile"),
    )
    out_specs = (P(None, "wall", "tile", None), P("tile", None))
    return jax.shard_map(
        on_device, mesh=mesh, in_specs=in_specs, out_specs=out_specs, check_vma=False
    )
```

```python
import jax
import jax.numpy as jnp
from jax import lax
from jax.experimental import pallas as pl
from jax.experimental.pallas import tpu as pltpu
from jax.sharding import PartitionSpec as P

NV = 10
K = 8
H = 8
S = 128
PATCH_DEV = 64
SLOTS = 8
ROWS_PER_OWNER = SLOTS + 1
F32 = jnp.float32
highest = lax.Precision.HIGHEST

VM = pl.BlockSpec(memory_space=pltpu.VMEM)
SM = pl.BlockSpec(memory_space=pltpu.SMEM)
HB = pl.BlockSpec(memory_space=pltpu.HBM)


def f32(*shape):
    return jax.ShapeDtypeStruct(shape, F32)


def held(*shape):
    return pltpu.VMEM(shape, F32)


def away(*shape):
    return pltpu.HBM(shape, F32)


def far_off(x):
    return pltpu.with_memory_space_constraint(x, pltpu.HBM)


def call(name, body, out_shape, n_in, smem=(), far=(), scratch=(), flops=0, nbytes=0):
    single = not isinstance(out_shape, (tuple, list))
    run = pl.pallas_call(
        body,
        name=name,
        out_shape=out_shape,
        in_specs=[SM if i in smem else HB if i in far else VM for i in range(n_in)],
        out_specs=VM if single else [VM] * len(out_shape),
        scratch_shapes=list(scratch),
        compiler_params=pltpu.CompilerParams(vmem_limit_bytes=12 * 1024 * 1024),
        cost_estimate=pl.CostEstimate(flops=flops, bytes_accessed=nbytes, transcendentals=0),
    )
    return run


def block_dot(m_ref, k, x):
    acc = None
    for j in range(NV):
        term = m_ref[:, j, k] * x[j][None]
        acc = term if acc is None else acc + term
    return acc


def forward_sweep(l_ref, d_ref, r_ref, s_ref, x):
    f = x
    for k in range(K):
        r = r_ref[:, k]
        f = r if f is None else r + block_dot(l_ref, k, f)
        s_ref[k] = block_dot(d_ref, k, f)
    return f


def forward_chain(l_ref, r_ref, f):
    for k in range(K):
        r = r_ref[:, k]
        f = r if f is None else r + block_dot(l_ref, k, f)
    return f


def backward_sweep(u_ref, s_ref, w_ref, y, emit=None):
    b, p = y, None
    for k in range(K - 1, -1, -1):
        s = s_ref[k]
        b = s if b is None else s - block_dot(u_ref, k, b)
        if w_ref is not None:
            p = b * w_ref[k] if p is None else p + b * w_ref[k]
        if emit is not None:
            emit(k, b)
    return b, p


def map_dot(m_ref, base, x):
    acc = None
    for j in range(NV):
        term = m_ref[base + j] * x[j][None]
        acc = term if acc is None else acc + term
    return acc


def pack_kernel(a_ref, rad_ref, lo_ref, hi_ref):
    for v in range(NV + 1):
        for k in range(K):
            cell = a_ref[v, k] if v < NV else rad_ref[k]
            at = 2 * (v * K + k)
            lo_ref[at : at + 2, :] = cell[0:2]
            hi_ref[at : at + 2, :] = cell[6:8]


def pair_dot(m_ref, k, xs):
    accs = [None] * len(xs)
    for j in range(NV):
        m = m_ref[:, j, k]
        for n, x in enumerate(xs):
            term = m * x[j][None]
            accs[n] = term if accs[n] is None else accs[n] + term
    return accs


def pair_map(m_ref, xs):
    accs = [None] * len(xs)
    for j in range(NV):
        m = m_ref[j]
        for n, x in enumerate(xs):
            term = m * x[j][None]
            accs[n] = term if accs[n] is None else accs[n] + term
    return accs


def interior(a_ref, src_ref, rad_ref, frq_ref, out_ref):
    row = lax.broadcasted_iota(jnp.int32, (H, S), 0)
    lane = lax.broadcasted_iota(jnp.int32, (H, S), 1)
    for k in range(K):
        a = a_ref[:, k]
        rad = rad_ref[k]
        applied = None
        for d, w in ((-2, -0.0625), (-1, 0.25), (1, 0.25), (2, -0.0625)):
            inside = (row + d >= 0) & (row + d < H)
            coef = jnp.where(inside, w * (rad + pltpu.roll(rad, (-d) % H, 0)), 0.0)
            term = coef[None] * pltpu.roll(a, (-d) % H, 1)
            applied = term if applied is None else applied + term
        for d in (-1, 1):
            inside = (lane + d >= 0) & (lane + d < S)
            coef = jnp.where(inside, 0.25 * (rad + pltpu.roll(rad, (-d) % S, 1)), 0.0)
            applied = applied + coef[None] * pltpu.roll(a, (-d) % S, 2)
        frq = frq_ref[k][None]
        half = NV // 2
        src = src_ref[:, k] - applied
        out_ref[:half, k] = src[:half] + frq * a[half:]
        out_ref[half:, k] = src[half:] - frq * a[:half]


def start_kernel(
    pos_ref, w_in, a_in, src_in, rad_in, frq_in, l_in, d_in, u_in,
    l_ref, d_ref, u_ref, r_ref, w_ref, map_ref, a_ref, src_ref, rad_ref, frq_ref, s0_ref, s1_ref, state_sems, block_sems,
):
    wall = pos_ref[0]
    state = [
        pltpu.make_async_copy(there, here, state_sems.at[n])
        for n, (there, here) in enumerate(((a_in, a_ref), (src_in, src_ref), (rad_in, rad_ref), (frq_in, frq_ref)))
    ]
    def block_copies(k):
        pairs = ((l_in, l_ref), (d_in, d_ref), (u_in, u_ref))
        return [
            pltpu.make_async_copy(there.at[:, :, k], here.at[:, :, k], block_sems.at[k, n])
            for n, (there, here) in enumerate(pairs)
        ]

    def depart(k):
        for copy in block_copies(k):
            copy.start()

    def arrived(k):
        for copy in block_copies(k):
            copy.wait()

    ahead = 3
    for copy in state:
        copy.start()
    for k in range(K - 1, K - 1 - ahead, -1):
        depart(k)

    @pl.when(wall != 3)
    def _():
        for k in range(K - 1 - ahead, -1, -1):
            depart(k)

    for k in range(K):
        w_ref[k] = jnp.broadcast_to(w_in[:, k : k + 1], (H, S))
    for copy in state:
        copy.wait()
    interior(a_ref, src_ref, rad_ref, frq_ref, r_ref)

    @pl.when(wall != 3)
    def _():
        for k in range(K - 1, -1, -1):
            arrived(k)

    @pl.when(wall == 3)
    def _():
        pairs = [(c, c + 1) for c in range(0, NV, 2)]

        def descend(k, old_ref, new_ref):
            arrived(k)

            @pl.when(k >= ahead)
            def _():
                depart(k - ahead)

            for cols in pairs:
                outs = pair_map(old_ref, [l_ref[:, c, k + 1] for c in cols])
                outs = pair_dot(u_ref, k, outs)
                for c, out in zip(cols, outs):
                    new_ref[c] = d_ref[:, c, k] - out

        arrived(K - 1)
        depart(K - 1 - ahead)
        for c in range(NV):
            s0_ref[c] = d_ref[:, c, K - 1]

        @pl.loop(0, K // 2 - 1)
        def _(step):
            descend(K - 2 - 2 * step, s0_ref, s1_ref)
            descend(K - 3 - 2 * step, s1_ref, s0_ref)

        descend(jnp.int32(0), s0_ref, s1_ref)
        for cols in pairs:
            for c, out in zip(cols, pair_map(s1_ref, [l_ref[:, c, 0] for c in cols])):
                map_ref[c] = out


def residual_kernel(pos_ref, map_ref, r_ref, left_ref, right_ref, rad_ref, l_ref, d_ref, u_ref, out_ref, up_ref, down_ref, s_ref):
    wall, tile, last = pos_ref[0], pos_ref[1], pos_ref[2]
    row = lax.broadcasted_iota(jnp.int32, (H, S), 0)
    has_left = tile > 0
    has_right = tile < last

    def line(ref, v, k, c):
        at = 2 * (v * K + k) + c
        return jnp.broadcast_to(ref[at : at + 1, :], (H, S))

    for k in range(K):
        rad = rad_ref[k]
        l0, l1, r0, r1 = (line(ref, NV, k, c) for ref in (left_ref, right_ref) for c in (0, 1))
        zero = jnp.zeros((H, S), F32)
        f_l0 = jnp.where((row == 0) & has_left, -0.0625 * (rad + l0), zero)
        f_l1 = jnp.where(row == 0, 0.25 * (rad + l1), jnp.where(row == 1, -0.0625 * (rad + l1), zero))
        f_l1 = jnp.where(has_left, f_l1, zero)
        f_r0 = jnp.where(row == 7, 0.25 * (rad + r0), jnp.where(row == 6, -0.0625 * (rad + r0), zero))
        f_r0 = jnp.where(has_right, f_r0, zero)
        f_r1 = jnp.where((row == 7) & has_right, -0.0625 * (rad + r1), zero)
        for v in range(NV):
            applied = f_l0 * line(left_ref, v, k, 0) + f_l1 * line(left_ref, v, k, 1)
            applied = applied + (f_r0 * line(right_ref, v, k, 0) + f_r1 * line(right_ref, v, k, 1))
            out_ref[v, k] = r_ref[v, k] - applied

    @pl.when(wall == 0)
    def _():
        up_ref[...] = forward_chain(l_ref, out_ref, None)

    @pl.when(wall == 3)
    def _():
        forward_sweep(l_ref, d_ref, out_ref, s_ref, None)
        down_ref[NV] = backward_sweep(u_ref, s_ref, None, None)[0]
        for c in range(NV):
            down_ref[c] = map_ref[c]


def middle_kernel(pos_ref, x_ref, r_ref, l_ref, out_ref):
    @pl.when(pos_ref[0] == 1)
    def _():
        out_ref[...] = forward_chain(l_ref, r_ref, x_ref[...])


def below_kernel(pos_ref, x_ref, r_ref, l_ref, d_ref, u_ref, below_ref, s_ref):
    @pl.when(pos_ref[0] == 1)
    def _():
        forward_sweep(l_ref, d_ref, r_ref, s_ref, x_ref[...])
        below_ref[NV] = backward_sweep(u_ref, s_ref, None, None)[0]

        @pl.loop(0, NV // 2)
        def _(pair):
            cols = [2 * pair, 2 * pair + 1]
            xs = [u_ref[:, c, K - 1] for c in cols]
            for k in range(K - 2, -1, -1):
                xs = pair_dot(u_ref, k, xs)
            for c, x in zip(cols, xs):
                below_ref[c] = x


def rise_kernel(pos_ref, x_ref, r_ref, l_ref, d_ref, x3_ref, s_ref):
    @pl.when(pos_ref[0] == 2)
    def _():
        x3_ref[...] = forward_sweep(l_ref, d_ref, r_ref, s_ref, x_ref[...])


def decide_kernel(pos_ref, x3_ref, map_ref, s_ref, u_ref, y2_ref, y1_ref):
    @pl.when(pos_ref[0] == 2)
    def _():
        y2 = map_ref[NV] + map_dot(map_ref, 0, x3_ref[...])
        y2_ref[...] = y2
        y1_ref[...] = backward_sweep(u_ref, s_ref, None, y2)[0]


def scale_kernel(pos_ref, x1_ref, x3_ref, s2_ref, r_ref, l_ref, d_ref, s_ref, x_ref):
    wall = pos_ref[0]

    @pl.when(wall == 0)
    def _():
        x_ref[...] = jnp.zeros((NV, H, S), F32)

    @pl.when(wall == 1)
    def _():
        x_ref[...] = x1_ref[...]

    @pl.when(wall == 3)
    def _():
        x_ref[...] = x3_ref[...]

    @pl.when(wall == 2)
    def _():
        s_ref[...] = s2_ref[...]

    @pl.when(wall != 2)
    def _():
        forward_sweep(l_ref, d_ref, r_ref, s_ref, x_ref[...])


def finish_kernel(
    pos_ref, y2_ref, y1_ref, y10_ref, below_ref, w_ref, pw_ref, s_ref, u_ref, out_ref, rows_ref, y_ref, prof_ref
):
    wall = pos_ref[0]

    @pl.when(wall == 0)
    def _():
        y_ref[...] = below_ref[NV] + map_dot(below_ref, 0, y10_ref[...])

    @pl.when(wall == 1)
    def _():
        y_ref[...] = y1_ref[...]

    @pl.when(wall == 2)
    def _():
        y_ref[...] = y2_ref[...]

    @pl.when(wall == 3)
    def _():
        y_ref[...] = jnp.zeros((NV, H, S), F32)

    def emit(k, b):
        out_ref[:, k] = b

    _, profile = backward_sweep(u_ref, s_ref, w_ref, y_ref[...], emit)
    for v in range(NV):
        prof_ref[v * H : (v + 1) * H, :] = profile[v]
    row = lax.broadcasted_iota(jnp.int32, (SLOTS, S), 0)
    lane = lax.broadcasted_iota(jnp.int32, (SLOTS, S), 1)
    prof_ref[NV * H :, :] = (row == lane).astype(F32)
    rows_ref[...] = jnp.dot(pw_ref[...], prof_ref[...], precision=highest, preferred_element_type=F32)


def place_kernel(count_ref, w_ref, owner_ref, tag_ref, out_ref):
    blocks = owner_ref.shape[1]
    owners = out_ref.shape[0] // ROWS_PER_OWNER
    owner = owner_ref[...]
    live = lax.broadcasted_iota(jnp.int32, (1, blocks), 1) < count_ref[0]
    hits = (owner == lax.broadcasted_iota(jnp.int32, (owners, blocks), 0)).astype(F32)
    earlier = lax.broadcasted_iota(jnp.int32, (blocks, blocks), 0) < lax.broadcasted_iota(jnp.int32, (blocks, blocks), 1)
    before = jnp.dot(hits, earlier.astype(F32), preferred_element_type=F32)
    slot = jnp.sum(before * hits, axis=0, keepdims=True).astype(jnp.int32)
    row = lax.broadcasted_iota(jnp.int32, (owners * ROWS_PER_OWNER, blocks), 0)
    placed = ((owner * ROWS_PER_OWNER + slot == row) & live).astype(F32)
    tagged = ((owner * ROWS_PER_OWNER + SLOTS == row) & live).astype(F32)
    width = NV * H
    lanes = lax.broadcasted_iota(jnp.int32, (SLOTS, blocks), 0)
    tags = jnp.where(lanes == slot, (tag_ref[...] + 1).astype(F32), 0.0)
    dims = (((1,), (1,)), ((), ()))
    out_ref[:, :width] = lax.dot_general(placed, w_ref[...], dims, precision=highest, preferred_element_type=F32)
    out_ref[:, width:] = lax.dot_general(tagged, tags, dims, precision=highest, preferred_element_type=F32)


def pick_kernel(got_ref, out_ref):
    rows = got_ref.shape[0]
    sources = rows // ROWS_PER_OWNER
    tag_rows = got_ref[pl.ds(SLOTS, sources, stride=ROWS_PER_OWNER), :]
    lane_of = (
        lax.broadcasted_iota(jnp.int32, (SLOTS, S), 0) == lax.broadcasted_iota(jnp.int32, (SLOTS, S), 1)
    ).astype(F32)
    tags = lax.dot_general(
        lane_of, tag_rows, (((1,), (1,)), ((), ())), precision=highest, preferred_element_type=F32
    )
    column = lax.broadcasted_iota(jnp.int32, (sources, rows), 1)
    first = lax.broadcasted_iota(jnp.int32, (sources, rows), 0) * ROWS_PER_OWNER
    spread = ((column >= first) & (column < first + ROWS_PER_OWNER)).astype(F32)
    wide = jnp.dot(tags, spread, precision=highest, preferred_element_type=F32)
    slot = lax.broadcasted_iota(jnp.int32, (SLOTS, rows), 1) % ROWS_PER_OWNER
    mine = slot == lax.broadcasted_iota(jnp.int32, (SLOTS, rows), 0)
    tag = jnp.sum(jnp.where(mine, wide, 0.0), axis=0, keepdims=True)
    target = (lax.broadcasted_iota(jnp.int32, (PATCH_DEV, rows), 0) + 1).astype(F32)
    picker = (tag == target).astype(F32)
    out_ref[...] = jnp.dot(picker, got_ref[...], precision=highest, preferred_element_type=F32)


def on_device(
    adjoint, source, radius, frequency, lower, diag, upper, wall_weight,
    surface_weight, patch_owner, patch_row, surface_count,
):
    tiles = lax.axis_size("tile")
    tie = lax.optimization_barrier
    pos = jnp.stack([lax.axis_index("wall"), lax.axis_index("tile"), jnp.int32(tiles - 1)]).astype(jnp.int32)
    levels = held(K, NV, H, S)
    block, state, cell, vec = held(NV, NV, K, H, S), held(NV, K, H, S), held(K, H, S), f32(NV, H, S)
    adjoint, source, radius, frequency, lower, diag, upper, wall_weight = (
        far_off(x)
        for x in (adjoint, source, radius, frequency, lower, diag, upper, wall_weight.reshape(1, K))
    )

    lo, hi = call("pack", pack_kernel, (f32(22 * K, S), f32(22 * K, S)), 2, nbytes=800_000)(adjoint, radius)
    left = lax.ppermute(hi, "tile", [(i, (i + 1) % tiles) for i in range(tiles)])
    right = lax.ppermute(lo, "tile", [((i + 1) % tiles, i) for i in range(tiles)])

    lo, pos1 = tie((lo, pos))
    lower, diag, upper, inner, weight, maps = call(
        "start", start_kernel, (block, block, block, state, cell, f32(NV, NV, H, S)), 9, smem=(0,),
        far=(2, 3, 4, 5, 6, 7, 8),
        scratch=(
            state, state, cell, cell, held(NV, NV, H, S), held(NV, NV, H, S), pltpu.SemaphoreType.DMA((4,)), pltpu.SemaphoreType.DMA((K, 3)),
        ),
        flops=30_000_000, nbytes=11_000_000,
    )(pos1, wall_weight, adjoint, source, radius, frequency, lower, diag, upper)

    resid, up, down = call(
        "residual", residual_kernel, (state, vec, f32(NV + 1, NV, H, S)), 9, smem=(0,), scratch=(levels,)
    )(pos, maps, inner, left, right, radius, lower, diag, upper)
    x1 = lax.ppermute(up, "wall", [(0, 1)])
    above = lax.ppermute(down, "wall", [(3, 2)])
    x2 = call("middle", middle_kernel, vec, 4, smem=(0,))(pos, x1, resid, lower)
    x2, pos2 = tie((x2, pos))
    x2 = lax.ppermute(x2, "wall", [(1, 2)])
    below = call("below", below_kernel, f32(NV + 1, NV, H, S), 6, smem=(0,), scratch=(levels,))(
        pos2, x1, resid, lower, diag, upper
    )
    swt = surface_weight.transpose(1, 2, 0).reshape(NV * H, -1)
    placed = call("place", place_kernel, held(tiles * ROWS_PER_OWNER, NV * H + SLOTS), 4, smem=(0,))(
        surface_count, swt, patch_owner.reshape(1, -1), patch_row.reshape(1, -1)
    )

    x2, placed = tie((x2, placed))
    x3, scaled2 = call("rise", rise_kernel, (vec, levels), 5, smem=(0,))(pos, x2, resid, lower, diag)
    x3, below = tie((x3, below))
    below = lax.ppermute(below, "wall", [(1, 0)])
    x33 = lax.ppermute(x3, "wall", [(2, 3)])
    y2, y1 = call("decide", decide_kernel, (vec, vec), 5, smem=(0,))(pos, x3, above, scaled2, upper)
    y10 = lax.ppermute(y1, "wall", [(2, 0)])
    y11 = lax.ppermute(y1, "wall", [(2, 1)])
    scaled = call("scale", scale_kernel, levels, 7, smem=(0,), scratch=(held(NV, H, S),))(
        pos, x1, x33, scaled2, resid, lower, diag
    )
    adjoint_next, rows = call(
        "finish", finish_kernel, (f32(NV, K, H, S), away(tiles * ROWS_PER_OWNER, S)), 9, smem=(0,),
        scratch=(held(NV, H, S), held(NV * H + SLOTS, S)),
    )(pos, y2, y11, y10, below, weight, placed, scaled, upper)
    got = lax.all_to_all(rows.reshape(tiles, ROWS_PER_OWNER, 1, S), "tile", split_axis=0, concat_axis=0)
    got = got.reshape(tiles * ROWS_PER_OWNER, S)
    part = call("pick", pick_kernel, f32(PATCH_DEV, S), 1)(got)
    walls = lax.axis_size("wall")
    patch = part
    for d in range(1, walls):
        patch = patch + lax.ppermute(part, "wall", [(w, (w + d) % walls) for w in range(walls)])
    return adjoint_next, patch


def solution(mesh):
    in_specs = (
        P(None, "wall", "tile", None),
        P(None, "wall", "tile", None),
        P("wall", "tile", None),
        P("wall", "tile", None),
        P(None, None, "wall", "tile", None),
        P(None, None, "wall", "tile", None),
        P(None, None, "wall", "tile", None),
        P("wall"),
        P("tile", None, None),
        P("tile", None),
        P("tile"),
        P("tile"),
    )
    out_specs = (P(None, "wall", "tile", None), P("tile", None))
    return jax.shard_map(
        on_device, mesh=mesh, in_specs=in_specs, out_specs=out_specs, check_vma=False
    )
```

```python
import jax
import jax.numpy as jnp
from jax import lax
from jax.experimental import pallas as pl
from jax.experimental.pallas import tpu as pltpu
from jax.sharding import PartitionSpec as P

NV = 10
K = 8
H = 8
S = 128
PATCH_DEV = 64
SLOTS = 8
ROWS_PER_OWNER = SLOTS + 1
F32 = jnp.float32
highest = lax.Precision.HIGHEST

VM = pl.BlockSpec(memory_space=pltpu.VMEM)
SM = pl.BlockSpec(memory_space=pltpu.SMEM)
HB = pl.BlockSpec(memory_space=pltpu.HBM)


def f32(*shape):
    return jax.ShapeDtypeStruct(shape, F32)


def held(*shape):
    return pltpu.VMEM(shape, F32)


def away(*shape):
    return pltpu.HBM(shape, F32)


def far_off(x):
    return pltpu.with_memory_space_constraint(x, pltpu.HBM)


def call(name, body, out_shape, n_in, smem=(), far=(), scratch=(), flops=0, nbytes=0):
    single = not isinstance(out_shape, (tuple, list))
    run = pl.pallas_call(
        body,
        name=name,
        out_shape=out_shape,
        in_specs=[SM if i in smem else HB if i in far else VM for i in range(n_in)],
        out_specs=VM if single else [VM] * len(out_shape),
        scratch_shapes=list(scratch),
        compiler_params=pltpu.CompilerParams(vmem_limit_bytes=12 * 1024 * 1024),
        cost_estimate=pl.CostEstimate(flops=flops, bytes_accessed=nbytes, transcendentals=0),
    )
    return run


def block_dot(m_ref, k, x):
    acc = None
    for j in range(NV):
        term = m_ref[:, j, k] * x[j][None]
        acc = term if acc is None else acc + term
    return acc


def forward_sweep(l_ref, d_ref, r_ref, s_ref, x):
    f = x
    for k in range(K):
        r = r_ref[:, k]
        f = r if f is None else r + block_dot(l_ref, k, f)
        s_ref[k] = block_dot(d_ref, k, f)
    return f


def forward_chain(l_ref, r_ref, f):
    for k in range(K):
        r = r_ref[:, k]
        f = r if f is None else r + block_dot(l_ref, k, f)
    return f


def backward_sweep(u_ref, s_ref, w_ref, y, emit=None):
    b, p = y, None
    for k in range(K - 1, -1, -1):
        s = s_ref[k]
        b = s if b is None else s - block_dot(u_ref, k, b)
        if w_ref is not None:
            p = b * w_ref[k] if p is None else p + b * w_ref[k]
        if emit is not None:
            emit(k, b)
    return b, p


def map_dot(m_ref, base, x):
    acc = None
    for j in range(NV):
        term = m_ref[base + j] * x[j][None]
        acc = term if acc is None else acc + term
    return acc


def pack_kernel(a_ref, rad_ref, lo_ref, hi_ref):
    for v in range(NV + 1):
        for k in range(K):
            cell = a_ref[v, k] if v < NV else rad_ref[k]
            at = 2 * (v * K + k)
            lo_ref[at : at + 2, :] = cell[0:2]
            hi_ref[at : at + 2, :] = cell[6:8]


def pair_dot(m_ref, k, xs):
    accs = [None] * len(xs)
    for j in range(NV):
        m = m_ref[:, j, k]
        for n, x in enumerate(xs):
            term = m * x[j][None]
            accs[n] = term if accs[n] is None else accs[n] + term
    return accs


def pair_map(m_ref, xs):
    accs = [None] * len(xs)
    for j in range(NV):
        m = m_ref[j]
        for n, x in enumerate(xs):
            term = m * x[j][None]
            accs[n] = term if accs[n] is None else accs[n] + term
    return accs


def interior(a_ref, src_ref, rad_ref, frq_ref, out_ref):
    row = lax.broadcasted_iota(jnp.int32, (H, S), 0)
    lane = lax.broadcasted_iota(jnp.int32, (H, S), 1)
    for k in range(K):
        a = a_ref[:, k]
        rad = rad_ref[k]
        applied = None
        for d, w in ((-2, -0.0625), (-1, 0.25), (1, 0.25), (2, -0.0625)):
            inside = (row + d >= 0) & (row + d < H)
            coef = jnp.where(inside, w * (rad + pltpu.roll(rad, (-d) % H, 0)), 0.0)
            term = coef[None] * pltpu.roll(a, (-d) % H, 1)
            applied = term if applied is None else applied + term
        for d in (-1, 1):
            inside = (lane + d >= 0) & (lane + d < S)
            coef = jnp.where(inside, 0.25 * (rad + pltpu.roll(rad, (-d) % S, 1)), 0.0)
            applied = applied + coef[None] * pltpu.roll(a, (-d) % S, 2)
        frq = frq_ref[k][None]
        half = NV // 2
        src = src_ref[:, k] - applied
        out_ref[:half, k] = src[:half] + frq * a[half:]
        out_ref[half:, k] = src[half:] - frq * a[:half]


def start_kernel(
    pos_ref, w_in, a_in, src_in, rad_in, frq_in, l_in, d_in, u_in,
    l_ref, d_ref, u_ref, r_ref, w_ref, map_ref, a_ref, src_ref, rad_ref, frq_ref, s0_ref, s1_ref, state_sems, block_sems,
):
    wall = pos_ref[0]
    state = [
        pltpu.make_async_copy(there, here, state_sems.at[n])
        for n, (there, here) in enumerate(((a_in, a_ref), (src_in, src_ref), (rad_in, rad_ref), (frq_in, frq_ref)))
    ]
    def block_copies(k):
        pairs = ((l_in, l_ref), (d_in, d_ref), (u_in, u_ref))
        return [
            pltpu.make_async_copy(there.at[:, :, k], here.at[:, :, k], block_sems.at[k, n])
            for n, (there, here) in enumerate(pairs)
        ]

    def depart(k):
        for copy in block_copies(k):
            copy.start()

    def arrived(k):
        for copy in block_copies(k):
            copy.wait()

    ahead = 3
    for copy in state:
        copy.start()
    for k in range(K - 1, K - 1 - ahead, -1):
        depart(k)

    @pl.when(wall != 3)
    def _():
        for k in range(K - 1 - ahead, -1, -1):
            depart(k)

    for k in range(K):
        w_ref[k] = jnp.broadcast_to(w_in[:, k : k + 1], (H, S))
    for copy in state:
        copy.wait()
    interior(a_ref, src_ref, rad_ref, frq_ref, r_ref)

    @pl.when(wall != 3)
    def _():
        for k in range(K - 1, -1, -1):
            arrived(k)

    @pl.when(wall == 3)
    def _():
        pairs = [(c, c + 1) for c in range(0, NV, 2)]

        def descend(k, old_ref, new_ref):
            arrived(k)

            @pl.when(k >= ahead)
            def _():
                depart(k - ahead)

            for cols in pairs:
                outs = pair_map(old_ref, [l_ref[:, c, k + 1] for c in cols])
                outs = pair_dot(u_ref, k, outs)
                for c, out in zip(cols, outs):
                    new_ref[c] = d_ref[:, c, k] - out

        arrived(K - 1)
        depart(K - 1 - ahead)
        for c in range(NV):
            s0_ref[c] = d_ref[:, c, K - 1]

        @pl.loop(0, K // 2 - 1)
        def _(step):
            descend(K - 2 - 2 * step, s0_ref, s1_ref)
            descend(K - 3 - 2 * step, s1_ref, s0_ref)

        descend(jnp.int32(0), s0_ref, s1_ref)
        for cols in pairs:
            for c, out in zip(cols, pair_map(s1_ref, [l_ref[:, c, 0] for c in cols])):
                map_ref[c] = out


def residual_kernel(pos_ref, r_ref, left_ref, right_ref, rad_ref, l_ref, d_ref, u_ref, out_ref, up_ref, down_ref, s_ref):
    wall, tile, last = pos_ref[0], pos_ref[1], pos_ref[2]
    row = lax.broadcasted_iota(jnp.int32, (H, S), 0)
    has_left = tile > 0
    has_right = tile < last

    def line(ref, v, k, c):
        at = 2 * (v * K + k) + c
        return jnp.broadcast_to(ref[at : at + 1, :], (H, S))

    for k in range(K):
        rad = rad_ref[k]
        l0, l1, r0, r1 = (line(ref, NV, k, c) for ref in (left_ref, right_ref) for c in (0, 1))
        zero = jnp.zeros((H, S), F32)
        f_l0 = jnp.where((row == 0) & has_left, -0.0625 * (rad + l0), zero)
        f_l1 = jnp.where(row == 0, 0.25 * (rad + l1), jnp.where(row == 1, -0.0625 * (rad + l1), zero))
        f_l1 = jnp.where(has_left, f_l1, zero)
        f_r0 = jnp.where(row == 7, 0.25 * (rad + r0), jnp.where(row == 6, -0.0625 * (rad + r0), zero))
        f_r0 = jnp.where(has_right, f_r0, zero)
        f_r1 = jnp.where((row == 7) & has_right, -0.0625 * (rad + r1), zero)
        for v in range(NV):
            applied = f_l0 * line(left_ref, v, k, 0) + f_l1 * line(left_ref, v, k, 1)
            applied = applied + (f_r0 * line(right_ref, v, k, 0) + f_r1 * line(right_ref, v, k, 1))
            out_ref[v, k] = r_ref[v, k] - applied

    @pl.when(wall == 0)
    def _():
        up_ref[...] = forward_chain(l_ref, out_ref, None)

    @pl.when(wall == 3)
    def _():
        forward_sweep(l_ref, d_ref, out_ref, s_ref, None)
        down_ref[...] = backward_sweep(u_ref, s_ref, None, None)[0]


def middle_kernel(pos_ref, x_ref, r_ref, l_ref, out_ref):
    @pl.when(pos_ref[0] == 1)
    def _():
        out_ref[...] = forward_chain(l_ref, r_ref, x_ref[...])


def shift_kernel(pos_ref, x_ref, r_ref, l_ref, d_ref, u_ref, shift_ref, s_ref):
    @pl.when(pos_ref[0] == 1)
    def _():
        forward_sweep(l_ref, d_ref, r_ref, s_ref, x_ref[...])
        shift_ref[...] = backward_sweep(u_ref, s_ref, None, None)[0]


def below_kernel(pos_ref, u_ref, below_ref):
    @pl.when(pos_ref[0] == 1)
    def _():
        @pl.loop(0, NV // 2)
        def _(pair):
            cols = [2 * pair, 2 * pair + 1]
            xs = [u_ref[:, c, K - 1] for c in cols]
            for k in range(K - 2, -1, -1):
                xs = pair_dot(u_ref, k, xs)
            for c, x in zip(cols, xs):
                below_ref[c] = x


def rise_kernel(pos_ref, x_ref, r_ref, l_ref, d_ref, x3_ref, s_ref):
    @pl.when(pos_ref[0] == 2)
    def _():
        x3_ref[...] = forward_sweep(l_ref, d_ref, r_ref, s_ref, x_ref[...])


def decide_kernel(pos_ref, x3_ref, b_ref, map_ref, s_ref, u_ref, y2_ref, y1_ref):
    @pl.when(pos_ref[0] == 2)
    def _():
        y2 = b_ref[...] + map_dot(map_ref, 0, x3_ref[...])
        y2_ref[...] = y2
        y1_ref[...] = backward_sweep(u_ref, s_ref, None, y2)[0]


def scale_kernel(pos_ref, x1_ref, x3_ref, s2_ref, r_ref, l_ref, d_ref, s_ref, x_ref):
    wall = pos_ref[0]

    @pl.when(wall == 0)
    def _():
        x_ref[...] = jnp.zeros((NV, H, S), F32)

    @pl.when(wall == 1)
    def _():
        x_ref[...] = x1_ref[...]

    @pl.when(wall == 3)
    def _():
        x_ref[...] = x3_ref[...]

    @pl.when(wall == 2)
    def _():
        s_ref[...] = s2_ref[...]

    @pl.when(wall != 2)
    def _():
        forward_sweep(l_ref, d_ref, r_ref, s_ref, x_ref[...])


def finish_kernel(
    pos_ref, y2_ref, y1_ref, y10_ref, below_ref, shift_ref, w_ref, pw_ref, s_ref, u_ref, out_ref, rows_ref, y_ref, prof_ref
):
    wall = pos_ref[0]

    @pl.when(wall == 0)
    def _():
        y_ref[...] = shift_ref[...] + map_dot(below_ref, 0, y10_ref[...])

    @pl.when(wall == 1)
    def _():
        y_ref[...] = y1_ref[...]

    @pl.when(wall == 2)
    def _():
        y_ref[...] = y2_ref[...]

    @pl.when(wall == 3)
    def _():
        y_ref[...] = jnp.zeros((NV, H, S), F32)

    def emit(k, b):
        out_ref[:, k] = b

    _, profile = backward_sweep(u_ref, s_ref, w_ref, y_ref[...], emit)
    for v in range(NV):
        prof_ref[v * H : (v + 1) * H, :] = profile[v]
    row = lax.broadcasted_iota(jnp.int32, (SLOTS, S), 0)
    lane = lax.broadcasted_iota(jnp.int32, (SLOTS, S), 1)
    prof_ref[NV * H :, :] = (row == lane).astype(F32)
    rows_ref[...] = jnp.dot(pw_ref[...], prof_ref[...], precision=highest, preferred_element_type=F32)


def place_kernel(count_ref, w_ref, owner_ref, tag_ref, out_ref):
    blocks = owner_ref.shape[1]
    owners = out_ref.shape[0] // ROWS_PER_OWNER
    owner = owner_ref[...]
    live = lax.broadcasted_iota(jnp.int32, (1, blocks), 1) < count_ref[0]
    hits = (owner == lax.broadcasted_iota(jnp.int32, (owners, blocks), 0)).astype(F32)
    earlier = lax.broadcasted_iota(jnp.int32, (blocks, blocks), 0) < lax.broadcasted_iota(jnp.int32, (blocks, blocks), 1)
    before = jnp.dot(hits, earlier.astype(F32), preferred_element_type=F32)
    slot = jnp.sum(before * hits, axis=0, keepdims=True).astype(jnp.int32)
    row = lax.broadcasted_iota(jnp.int32, (owners * ROWS_PER_OWNER, blocks), 0)
    placed = ((owner * ROWS_PER_OWNER + slot == row) & live).astype(F32)
    tagged = ((owner * ROWS_PER_OWNER + SLOTS == row) & live).astype(F32)
    width = NV * H
    lanes = lax.broadcasted_iota(jnp.int32, (SLOTS, blocks), 0)
    tags = jnp.where(lanes == slot, (tag_ref[...] + 1).astype(F32), 0.0)
    dims = (((1,), (1,)), ((), ()))
    out_ref[:, :width] = lax.dot_general(placed, w_ref[...], dims, precision=highest, preferred_element_type=F32)
    out_ref[:, width:] = lax.dot_general(tagged, tags, dims, precision=highest, preferred_element_type=F32)


def pick_kernel(got_ref, out_ref):
    rows = got_ref.shape[0]
    sources = rows // ROWS_PER_OWNER
    tag_rows = got_ref[pl.ds(SLOTS, sources, stride=ROWS_PER_OWNER), :]
    lane_of = (
        lax.broadcasted_iota(jnp.int32, (SLOTS, S), 0) == lax.broadcasted_iota(jnp.int32, (SLOTS, S), 1)
    ).astype(F32)
    tags = lax.dot_general(
        lane_of, tag_rows, (((1,), (1,)), ((), ())), precision=highest, preferred_element_type=F32
    )
    column = lax.broadcasted_iota(jnp.int32, (sources, rows), 1)
    first = lax.broadcasted_iota(jnp.int32, (sources, rows), 0) * ROWS_PER_OWNER
    spread = ((column >= first) & (column < first + ROWS_PER_OWNER)).astype(F32)
    wide = jnp.dot(tags, spread, precision=highest, preferred_element_type=F32)
    slot = lax.broadcasted_iota(jnp.int32, (SLOTS, rows), 1) % ROWS_PER_OWNER
    mine = slot == lax.broadcasted_iota(jnp.int32, (SLOTS, rows), 0)
    tag = jnp.sum(jnp.where(mine, wide, 0.0), axis=0, keepdims=True)
    target = (lax.broadcasted_iota(jnp.int32, (PATCH_DEV, rows), 0) + 1).astype(F32)
    picker = (tag == target).astype(F32)
    out_ref[...] = jnp.dot(picker, got_ref[...], precision=highest, preferred_element_type=F32)


def on_device(
    adjoint, source, radius, frequency, lower, diag, upper, wall_weight,
    surface_weight, patch_owner, patch_row, surface_count,
):
    tiles = lax.axis_size("tile")
    tie = lax.optimization_barrier
    pos = jnp.stack([lax.axis_index("wall"), lax.axis_index("tile"), jnp.int32(tiles - 1)]).astype(jnp.int32)
    levels = held(K, NV, H, S)
    block, state, cell, vec = held(NV, NV, K, H, S), held(NV, K, H, S), held(K, H, S), f32(NV, H, S)
    adjoint, source, radius, frequency, lower, diag, upper, wall_weight = (
        far_off(x)
        for x in (adjoint, source, radius, frequency, lower, diag, upper, wall_weight.reshape(1, K))
    )

    lo, hi = call("pack", pack_kernel, (f32(22 * K, S), f32(22 * K, S)), 2, nbytes=800_000)(adjoint, radius)
    left = lax.ppermute(hi, "tile", [(i, (i + 1) % tiles) for i in range(tiles)])
    right = lax.ppermute(lo, "tile", [((i + 1) % tiles, i) for i in range(tiles)])

    lo, pos1 = tie((lo, pos))
    lower, diag, upper, inner, weight, maps = call(
        "start", start_kernel, (block, block, block, state, cell, f32(NV, NV, H, S)), 9, smem=(0,),
        far=(2, 3, 4, 5, 6, 7, 8),
        scratch=(
            state, state, cell, cell, held(NV, NV, H, S), held(NV, NV, H, S), pltpu.SemaphoreType.DMA((4,)), pltpu.SemaphoreType.DMA((K, 3)),
        ),
        flops=30_000_000, nbytes=11_000_000,
    )(pos1, wall_weight, adjoint, source, radius, frequency, lower, diag, upper)

    maps, left, right = tie((maps, left, right))
    above = lax.ppermute(maps, "wall", [(3, 2)])
    resid, up, down = call(
        "residual", residual_kernel, (state, vec, vec), 8, smem=(0,), scratch=(levels,)
    )(pos, inner, left, right, radius, lower, diag, upper)
    x1 = lax.ppermute(up, "wall", [(0, 1)])
    b3 = lax.ppermute(down, "wall", [(3, 2)])
    up, pos1 = tie((up, pos))
    below = call("below", below_kernel, f32(NV, NV, H, S), 2, smem=(0,))(pos1, upper)
    x1, below = tie((x1, below))
    below = lax.ppermute(below, "wall", [(1, 0)])
    x2 = call("middle", middle_kernel, vec, 4, smem=(0,))(pos, x1, resid, lower)
    x2, pos2 = tie((x2, pos))
    x2 = lax.ppermute(x2, "wall", [(1, 2)])
    shift = call("shift", shift_kernel, vec, 6, smem=(0,), scratch=(levels,))(pos2, x1, resid, lower, diag, upper)
    swt = surface_weight.transpose(1, 2, 0).reshape(NV * H, -1)
    placed = call("place", place_kernel, held(tiles * ROWS_PER_OWNER, NV * H + SLOTS), 4, smem=(0,))(
        surface_count, swt, patch_owner.reshape(1, -1), patch_row.reshape(1, -1)
    )

    x2, placed = tie((x2, placed))
    x3, scaled2 = call("rise", rise_kernel, (vec, levels), 5, smem=(0,))(pos, x2, resid, lower, diag)
    x33 = lax.ppermute(x3, "wall", [(2, 3)])
    y2, y1 = call("decide", decide_kernel, (vec, vec), 6, smem=(0,))(pos, x3, b3, above, scaled2, upper)
    y1, shift = tie((y1, shift))
    y10 = lax.ppermute(y1, "wall", [(2, 0)])
    y11 = lax.ppermute(y1, "wall", [(2, 1)])
    shift = lax.ppermute(shift, "wall", [(1, 0)])
    scaled = call("scale", scale_kernel, levels, 7, smem=(0,), scratch=(held(NV, H, S),))(
        pos, x1, x33, scaled2, resid, lower, diag
    )
    adjoint_next, rows = call(
        "finish", finish_kernel, (f32(NV, K, H, S), away(tiles * ROWS_PER_OWNER, S)), 10, smem=(0,),
        scratch=(held(NV, H, S), held(NV * H + SLOTS, S)),
    )(pos, y2, y11, y10, below, shift, weight, placed, scaled, upper)
    got = lax.all_to_all(rows.reshape(tiles, ROWS_PER_OWNER, 1, S), "tile", split_axis=0, concat_axis=0)
    got = got.reshape(tiles * ROWS_PER_OWNER, S)
    part = call("pick", pick_kernel, f32(PATCH_DEV, S), 1)(got)
    walls = lax.axis_size("wall")
    patch = part
    for d in range(1, walls):
        patch = patch + lax.ppermute(part, "wall", [(w, (w + d) % walls) for w in range(walls)])
    return adjoint_next, patch


def solution(mesh):
    in_specs = (
        P(None, "wall", "tile", None),
        P(None, "wall", "tile", None),
        P("wall", "tile", None),
        P("wall", "tile", None),
        P(None, None, "wall", "tile", None),
        P(None, None, "wall", "tile", None),
        P(None, None, "wall", "tile", None),
        P("wall"),
        P("tile", None, None),
        P("tile", None),
        P("tile"),
        P("tile"),
    )
    out_specs = (P(None, "wall", "tile", None), P("tile", None))
    return jax.shard_map(
        on_device, mesh=mesh, in_specs=in_specs, out_specs=out_specs, check_vma=False
    )
```

```python
import jax
import jax.numpy as jnp
from jax import lax
from jax.experimental import pallas as pl
from jax.experimental.pallas import tpu as pltpu
from jax.sharding import PartitionSpec as P

NV = 10
K = 8
H = 8
S = 128
PATCH_DEV = 64
SLOTS = 8
ROWS_PER_OWNER = SLOTS + 1
F32 = jnp.float32
highest = lax.Precision.HIGHEST

VM = pl.BlockSpec(memory_space=pltpu.VMEM)
SM = pl.BlockSpec(memory_space=pltpu.SMEM)
HB = pl.BlockSpec(memory_space=pltpu.HBM)


def f32(*shape):
    return jax.ShapeDtypeStruct(shape, F32)


def held(*shape):
    return pltpu.VMEM(shape, F32)


def away(*shape):
    return pltpu.HBM(shape, F32)


def far_off(x):
    return pltpu.with_memory_space_constraint(x, pltpu.HBM)


def call(name, body, out_shape, n_in, smem=(), far=(), scratch=(), flops=0, nbytes=0):
    single = not isinstance(out_shape, (tuple, list))
    run = pl.pallas_call(
        body,
        name=name,
        out_shape=out_shape,
        in_specs=[SM if i in smem else HB if i in far else VM for i in range(n_in)],
        out_specs=VM if single else [VM] * len(out_shape),
        scratch_shapes=list(scratch),
        compiler_params=pltpu.CompilerParams(vmem_limit_bytes=12 * 1024 * 1024),
        cost_estimate=pl.CostEstimate(flops=flops, bytes_accessed=nbytes, transcendentals=0),
    )
    return run


def block_dot(m_ref, k, x):
    acc = None
    for j in range(NV):
        term = m_ref[:, j, k] * x[j][None]
        acc = term if acc is None else acc + term
    return acc


def forward_sweep(l_ref, d_ref, r_ref, s_ref, x):
    f = x
    for k in range(K):
        r = r_ref[:, k]
        f = r if f is None else r + block_dot(l_ref, k, f)
        s_ref[k] = block_dot(d_ref, k, f)
    return f


def forward_chain(l_ref, r_ref, f):
    for k in range(K):
        r = r_ref[:, k]
        f = r if f is None else r + block_dot(l_ref, k, f)
    return f


def backward_sweep(u_ref, s_ref, w_ref, y, emit=None):
    b, p = y, None
    for k in range(K - 1, -1, -1):
        s = s_ref[k]
        b = s if b is None else s - block_dot(u_ref, k, b)
        if w_ref is not None:
            p = b * w_ref[k] if p is None else p + b * w_ref[k]
        if emit is not None:
            emit(k, b)
    return b, p


def map_dot(m_ref, base, x):
    acc = None
    for j in range(NV):
        term = m_ref[base + j] * x[j][None]
        acc = term if acc is None else acc + term
    return acc


def pack_kernel(a_ref, rad_ref, lo_ref, hi_ref):
    for v in range(NV + 1):
        for k in range(K):
            cell = a_ref[v, k] if v < NV else rad_ref[k]
            at = 2 * (v * K + k)
            lo_ref[at : at + 2, :] = cell[0:2]
            hi_ref[at : at + 2, :] = cell[6:8]


def pair_dot(m_ref, k, xs):
    accs = [None] * len(xs)
    for j in range(NV):
        m = m_ref[:, j, k]
        for n, x in enumerate(xs):
            term = m * x[j][None]
            accs[n] = term if accs[n] is None else accs[n] + term
    return accs


def pair_map(m_ref, xs):
    accs = [None] * len(xs)
    for j in range(NV):
        m = m_ref[j]
        for n, x in enumerate(xs):
            term = m * x[j][None]
            accs[n] = term if accs[n] is None else accs[n] + term
    return accs


def interior(a_ref, src_ref, rad_ref, frq_ref, out_ref):
    row = lax.broadcasted_iota(jnp.int32, (H, S), 0)
    lane = lax.broadcasted_iota(jnp.int32, (H, S), 1)
    for k in range(K):
        a = a_ref[:, k]
        rad = rad_ref[k]
        applied = None
        for d, w in ((-2, -0.0625), (-1, 0.25), (1, 0.25), (2, -0.0625)):
            inside = (row + d >= 0) & (row + d < H)
            coef = jnp.where(inside, w * (rad + pltpu.roll(rad, (-d) % H, 0)), 0.0)
            term = coef[None] * pltpu.roll(a, (-d) % H, 1)
            applied = term if applied is None else applied + term
        for d in (-1, 1):
            inside = (lane + d >= 0) & (lane + d < S)
            coef = jnp.where(inside, 0.25 * (rad + pltpu.roll(rad, (-d) % S, 1)), 0.0)
            applied = applied + coef[None] * pltpu.roll(a, (-d) % S, 2)
        frq = frq_ref[k][None]
        half = NV // 2
        src = src_ref[:, k] - applied
        out_ref[:half, k] = src[:half] + frq * a[half:]
        out_ref[half:, k] = src[half:] - frq * a[:half]


def start_kernel(
    pos_ref, w_in, a_in, src_in, rad_in, frq_in, l_in, d_in, u_in,
    l_ref, d_ref, u_ref, r_ref, w_ref, map_ref, a_ref, src_ref, rad_ref, frq_ref, s0_ref, s1_ref, state_sems, block_sems,
):
    wall = pos_ref[0]
    state = [
        pltpu.make_async_copy(there, here, state_sems.at[n])
        for n, (there, here) in enumerate(((a_in, a_ref), (src_in, src_ref), (rad_in, rad_ref), (frq_in, frq_ref)))
    ]
    def block_copies(k):
        pairs = ((l_in, l_ref), (d_in, d_ref), (u_in, u_ref))
        return [
            pltpu.make_async_copy(there.at[:, :, k], here.at[:, :, k], block_sems.at[k, n])
            for n, (there, here) in enumerate(pairs)
        ]

    def depart(k):
        for copy in block_copies(k):
            copy.start()

    def arrived(k):
        for copy in block_copies(k):
            copy.wait()

    ahead = 3
    for copy in state:
        copy.start()
    for k in range(K - 1, K - 1 - ahead, -1):
        depart(k)

    @pl.when(wall != 3)
    def _():
        for k in range(K - 1 - ahead, -1, -1):
            depart(k)

    for k in range(K):
        w_ref[k] = jnp.broadcast_to(w_in[:, k : k + 1], (H, S))
    for copy in state:
        copy.wait()
    interior(a_ref, src_ref, rad_ref, frq_ref, r_ref)

    @pl.when(wall != 3)
    def _():
        for k in range(K - 1, -1, -1):
            arrived(k)

    @pl.when(wall == 3)
    def _():
        pairs = [(c, c + 1) for c in range(0, NV, 2)]

        def descend(k, old_ref, new_ref):
            arrived(k)

            @pl.when(k >= ahead)
            def _():
                depart(k - ahead)

            for cols in pairs:
                outs = pair_map(old_ref, [l_ref[:, c, k + 1] for c in cols])
                outs = pair_dot(u_ref, k, outs)
                for c, out in zip(cols, outs):
                    new_ref[c] = d_ref[:, c, k] - out

        arrived(K - 1)
        depart(K - 1 - ahead)
        for c in range(NV):
            s0_ref[c] = d_ref[:, c, K - 1]

        @pl.loop(0, K // 2 - 1)
        def _(step):
            descend(K - 2 - 2 * step, s0_ref, s1_ref)
            descend(K - 3 - 2 * step, s1_ref, s0_ref)

        descend(jnp.int32(0), s0_ref, s1_ref)
        for cols in pairs:
            for c, out in zip(cols, pair_map(s1_ref, [l_ref[:, c, 0] for c in cols])):
                map_ref[c] = out


def residual_kernel(pos_ref, r_ref, left_ref, right_ref, rad_ref, l_ref, d_ref, u_ref, out_ref, up_ref, down_ref, s_ref):
    wall, tile, last = pos_ref[0], pos_ref[1], pos_ref[2]
    row = lax.broadcasted_iota(jnp.int32, (H, S), 0)
    has_left = tile > 0
    has_right = tile < last

    def line(ref, v, k, c):
        at = 2 * (v * K + k) + c
        return jnp.broadcast_to(ref[at : at + 1, :], (H, S))

    for k in range(K):
        rad = rad_ref[k]
        l0, l1, r0, r1 = (line(ref, NV, k, c) for ref in (left_ref, right_ref) for c in (0, 1))
        zero = jnp.zeros((H, S), F32)
        f_l0 = jnp.where((row == 0) & has_left, -0.0625 * (rad + l0), zero)
        f_l1 = jnp.where(row == 0, 0.25 * (rad + l1), jnp.where(row == 1, -0.0625 * (rad + l1), zero))
        f_l1 = jnp.where(has_left, f_l1, zero)
        f_r0 = jnp.where(row == 7, 0.25 * (rad + r0), jnp.where(row == 6, -0.0625 * (rad + r0), zero))
        f_r0 = jnp.where(has_right, f_r0, zero)
        f_r1 = jnp.where((row == 7) & has_right, -0.0625 * (rad + r1), zero)
        for v in range(NV):
            applied = f_l0 * line(left_ref, v, k, 0) + f_l1 * line(left_ref, v, k, 1)
            applied = applied + (f_r0 * line(right_ref, v, k, 0) + f_r1 * line(right_ref, v, k, 1))
            out_ref[v, k] = r_ref[v, k] - applied

    @pl.when(wall == 0)
    def _():
        up_ref[...] = forward_chain(l_ref, out_ref, None)

    @pl.when(wall == 3)
    def _():
        forward_sweep(l_ref, d_ref, out_ref, s_ref, None)
        down_ref[...] = backward_sweep(u_ref, s_ref, None, None)[0]


def middle_kernel(pos_ref, x_ref, r_ref, l_ref, out_ref):
    @pl.when(pos_ref[0] == 1)
    def _():
        out_ref[...] = forward_chain(l_ref, r_ref, x_ref[...])


def shift_kernel(pos_ref, x_ref, r_ref, l_ref, d_ref, u_ref, shift_ref, s_ref):
    @pl.when(pos_ref[0] == 1)
    def _():
        forward_sweep(l_ref, d_ref, r_ref, s_ref, x_ref[...])
        shift_ref[...] = backward_sweep(u_ref, s_ref, None, None)[0]


def below_kernel(pos_ref, u_ref, below_ref):
    @pl.when(pos_ref[0] == 1)
    def _():
        @pl.loop(0, NV // 2)
        def _(pair):
            cols = [2 * pair, 2 * pair + 1]
            xs = [u_ref[:, c, K - 1] for c in cols]
            for k in range(K - 2, -1, -1):
                xs = pair_dot(u_ref, k, xs)
            for c, x in zip(cols, xs):
                below_ref[c] = x


def decide_kernel(pos_ref, x_ref, b_ref, map_ref, r_ref, l_ref, d_ref, u_ref, x3_ref, y2_ref, y1_ref, s_ref):
    @pl.when(pos_ref[0] == 2)
    def _():
        x3 = forward_sweep(l_ref, d_ref, r_ref, s_ref, x_ref[...])
        x3_ref[...] = x3
        y2 = b_ref[...] + map_dot(map_ref, 0, x3)
        y2_ref[...] = y2
        y1_ref[...] = backward_sweep(u_ref, s_ref, None, y2)[0]


def scale_kernel(pos_ref, x1_ref, x3_ref, s2_ref, r_ref, l_ref, d_ref, s_ref, x_ref):
    wall = pos_ref[0]

    @pl.when(wall == 0)
    def _():
        x_ref[...] = jnp.zeros((NV, H, S), F32)

    @pl.when(wall == 1)
    def _():
        x_ref[...] = x1_ref[...]

    @pl.when(wall == 3)
    def _():
        x_ref[...] = x3_ref[...]

    @pl.when(wall == 2)
    def _():
        s_ref[...] = s2_ref[...]

    @pl.when(wall != 2)
    def _():
        forward_sweep(l_ref, d_ref, r_ref, s_ref, x_ref[...])


def finish_kernel(
    pos_ref, y2_ref, y10_ref, y1_ref, below_ref, shift_ref, w_ref, pw_ref, s_ref, u_ref, out_ref, rows_ref, y_ref, prof_ref
):
    wall = pos_ref[0]

    @pl.when(wall == 0)
    def _():
        y_ref[...] = shift_ref[...] + map_dot(below_ref, 0, y10_ref[...])

    @pl.when(wall == 1)
    def _():
        y_ref[...] = y1_ref[...]

    @pl.when(wall == 2)
    def _():
        y_ref[...] = y2_ref[...]

    @pl.when(wall == 3)
    def _():
        y_ref[...] = jnp.zeros((NV, H, S), F32)

    def emit(k, b):
        out_ref[:, k] = b

    _, profile = backward_sweep(u_ref, s_ref, w_ref, y_ref[...], emit)
    for v in range(NV):
        prof_ref[v * H : (v + 1) * H, :] = profile[v]
    row = lax.broadcasted_iota(jnp.int32, (SLOTS, S), 0)
    lane = lax.broadcasted_iota(jnp.int32, (SLOTS, S), 1)
    prof_ref[NV * H :, :] = (row == lane).astype(F32)
    rows_ref[...] = jnp.dot(pw_ref[...], prof_ref[...], precision=highest, preferred_element_type=F32)


def place_kernel(count_ref, w_ref, owner_ref, tag_ref, out_ref):
    blocks = owner_ref.shape[1]
    owners = out_ref.shape[0] // ROWS_PER_OWNER
    owner = owner_ref[...]
    live = lax.broadcasted_iota(jnp.int32, (1, blocks), 1) < count_ref[0]
    hits = (owner == lax.broadcasted_iota(jnp.int32, (owners, blocks), 0)).astype(F32)
    earlier = lax.broadcasted_iota(jnp.int32, (blocks, blocks), 0) < lax.broadcasted_iota(jnp.int32, (blocks, blocks), 1)
    before = jnp.dot(hits, earlier.astype(F32), preferred_element_type=F32)
    slot = jnp.sum(before * hits, axis=0, keepdims=True).astype(jnp.int32)
    row = lax.broadcasted_iota(jnp.int32, (owners * ROWS_PER_OWNER, blocks), 0)
    placed = ((owner * ROWS_PER_OWNER + slot == row) & live).astype(F32)
    tagged = ((owner * ROWS_PER_OWNER + SLOTS == row) & live).astype(F32)
    width = NV * H
    lanes = lax.broadcasted_iota(jnp.int32, (SLOTS, blocks), 0)
    tags = jnp.where(lanes == slot, (tag_ref[...] + 1).astype(F32), 0.0)
    dims = (((1,), (1,)), ((), ()))
    out_ref[:, :width] = lax.dot_general(placed, w_ref[...], dims, precision=highest, preferred_element_type=F32)
    out_ref[:, width:] = lax.dot_general(tagged, tags, dims, precision=highest, preferred_element_type=F32)


def pick_kernel(got_ref, out_ref):
    rows = got_ref.shape[0]
    sources = rows // ROWS_PER_OWNER
    tag_rows = got_ref[pl.ds(SLOTS, sources, stride=ROWS_PER_OWNER), :]
    lane_of = (
        lax.broadcasted_iota(jnp.int32, (SLOTS, S), 0) == lax.broadcasted_iota(jnp.int32, (SLOTS, S), 1)
    ).astype(F32)
    tags = lax.dot_general(
        lane_of, tag_rows, (((1,), (1,)), ((), ())), precision=highest, preferred_element_type=F32
    )
    column = lax.broadcasted_iota(jnp.int32, (sources, rows), 1)
    first = lax.broadcasted_iota(jnp.int32, (sources, rows), 0) * ROWS_PER_OWNER
    spread = ((column >= first) & (column < first + ROWS_PER_OWNER)).astype(F32)
    wide = jnp.dot(tags, spread, precision=highest, preferred_element_type=F32)
    slot = lax.broadcasted_iota(jnp.int32, (SLOTS, rows), 1) % ROWS_PER_OWNER
    mine = slot == lax.broadcasted_iota(jnp.int32, (SLOTS, rows), 0)
    tag = jnp.sum(jnp.where(mine, wide, 0.0), axis=0, keepdims=True)
    target = (lax.broadcasted_iota(jnp.int32, (PATCH_DEV, rows), 0) + 1).astype(F32)
    picker = (tag == target).astype(F32)
    out_ref[...] = jnp.dot(picker, got_ref[...], precision=highest, preferred_element_type=F32)


def on_device(
    adjoint, source, radius, frequency, lower, diag, upper, wall_weight,
    surface_weight, patch_owner, patch_row, surface_count,
):
    tiles = lax.axis_size("tile")
    tie = lax.optimization_barrier
    pos = jnp.stack([lax.axis_index("wall"), lax.axis_index("tile"), jnp.int32(tiles - 1)]).astype(jnp.int32)
    levels = held(K, NV, H, S)
    block, state, cell, vec = held(NV, NV, K, H, S), held(NV, K, H, S), held(K, H, S), f32(NV, H, S)
    adjoint, source, radius, frequency, lower, diag, upper, wall_weight = (
        far_off(x)
        for x in (adjoint, source, radius, frequency, lower, diag, upper, wall_weight.reshape(1, K))
    )

    lo, hi = call("pack", pack_kernel, (f32(22 * K, S), f32(22 * K, S)), 2, nbytes=800_000)(adjoint, radius)
    left = lax.ppermute(hi, "tile", [(i, (i + 1) % tiles) for i in range(tiles)])
    right = lax.ppermute(lo, "tile", [((i + 1) % tiles, i) for i in range(tiles)])

    lo, pos1 = tie((lo, pos))
    lower, diag, upper, inner, weight, maps = call(
        "start", start_kernel, (block, block, block, state, cell, f32(NV, NV, H, S)), 9, smem=(0,),
        far=(2, 3, 4, 5, 6, 7, 8),
        scratch=(
            state, state, cell, cell, held(NV, NV, H, S), held(NV, NV, H, S), pltpu.SemaphoreType.DMA((4,)), pltpu.SemaphoreType.DMA((K, 3)),
        ),
        flops=30_000_000, nbytes=11_000_000,
    )(pos1, wall_weight, adjoint, source, radius, frequency, lower, diag, upper)

    maps, left, right = tie((maps, left, right))
    above = lax.ppermute(maps, "wall", [(3, 2)])
    resid, up, down = call(
        "residual", residual_kernel, (state, vec, vec), 8, smem=(0,), scratch=(levels,)
    )(pos, inner, left, right, radius, lower, diag, upper)
    x1 = lax.ppermute(up, "wall", [(0, 1)])
    b3 = lax.ppermute(down, "wall", [(3, 2)])
    up, pos1 = tie((up, pos))
    below = call("below", below_kernel, f32(NV, NV, H, S), 2, smem=(0,))(pos1, upper)
    x1, below = tie((x1, below))
    below = lax.ppermute(below, "wall", [(1, 0)])
    x2 = call("middle", middle_kernel, vec, 4, smem=(0,))(pos, x1, resid, lower)
    x2, pos2 = tie((x2, pos))
    x2 = lax.ppermute(x2, "wall", [(1, 2)])
    shift = call("shift", shift_kernel, vec, 6, smem=(0,), scratch=(levels,))(pos2, x1, resid, lower, diag, upper)
    swt = surface_weight.transpose(1, 2, 0).reshape(NV * H, -1)
    placed = call("place", place_kernel, held(tiles * ROWS_PER_OWNER, NV * H + SLOTS), 4, smem=(0,))(
        surface_count, swt, patch_owner.reshape(1, -1), patch_row.reshape(1, -1)
    )

    x2, placed = tie((x2, placed))
    x3, y2, y1, scaled2 = call("decide", decide_kernel, (vec, vec, vec, levels), 8, smem=(0,))(
        pos, x2, b3, above, resid, lower, diag, upper
    )
    y1, shift = tie((y1, shift))
    x33 = lax.ppermute(x3, "wall", [(2, 3)])
    y10 = lax.ppermute(y1, "wall", [(2, 0)])
    y11 = lax.ppermute(y1, "wall", [(2, 1)])
    shift = lax.ppermute(shift, "wall", [(1, 0)])
    scaled = call("scale", scale_kernel, levels, 7, smem=(0,), scratch=(held(NV, H, S),))(
        pos, x1, x33, scaled2, resid, lower, diag
    )
    adjoint_next, rows = call(
        "finish", finish_kernel, (f32(NV, K, H, S), away(tiles * ROWS_PER_OWNER, S)), 10, smem=(0,),
        scratch=(held(NV, H, S), held(NV * H + SLOTS, S)),
    )(pos, y2, y10, y11, below, shift, weight, placed, scaled, upper)
    got = lax.all_to_all(rows.reshape(tiles, ROWS_PER_OWNER, 1, S), "tile", split_axis=0, concat_axis=0)
    got = got.reshape(tiles * ROWS_PER_OWNER, S)
    part = call("pick", pick_kernel, f32(PATCH_DEV, S), 1)(got)
    walls = lax.axis_size("wall")
    patch = part
    for d in range(1, walls):
        patch = patch + lax.ppermute(part, "wall", [(w, (w + d) % walls) for w in range(walls)])
    return adjoint_next, patch


def solution(mesh):
    in_specs = (
        P(None, "wall", "tile", None),
        P(None, "wall", "tile", None),
        P("wall", "tile", None),
        P("wall", "tile", None),
        P(None, None, "wall", "tile", None),
        P(None, None, "wall", "tile", None),
        P(None, None, "wall", "tile", None),
        P("wall"),
        P("tile", None, None),
        P("tile", None),
        P("tile"),
        P("tile"),
    )
    out_specs = (P(None, "wall", "tile", None), P("tile", None))
    return jax.shard_map(
        on_device, mesh=mesh, in_specs=in_specs, out_specs=out_specs, check_vma=False
    )
```

```python
import jax
import jax.numpy as jnp
from jax import lax
from jax.experimental import pallas as pl
from jax.experimental.pallas import tpu as pltpu
from jax.sharding import PartitionSpec as P

NV = 10
K = 8
H = 8
S = 128
PATCH_DEV = 64
SLOTS = 8
ROWS_PER_OWNER = SLOTS + 1
F32 = jnp.float32
highest = lax.Precision.HIGHEST

VM = pl.BlockSpec(memory_space=pltpu.VMEM)
SM = pl.BlockSpec(memory_space=pltpu.SMEM)
HB = pl.BlockSpec(memory_space=pltpu.HBM)


def f32(*shape):
    return jax.ShapeDtypeStruct(shape, F32)


def held(*shape):
    return pltpu.VMEM(shape, F32)


def away(*shape):
    return pltpu.HBM(shape, F32)


def far_off(x):
    return pltpu.with_memory_space_constraint(x, pltpu.HBM)


def call(name, body, out_shape, n_in, smem=(), far=(), scratch=(), flops=0, nbytes=0):
    single = not isinstance(out_shape, (tuple, list))
    run = pl.pallas_call(
        body,
        name=name,
        out_shape=out_shape,
        in_specs=[SM if i in smem else HB if i in far else VM for i in range(n_in)],
        out_specs=VM if single else [VM] * len(out_shape),
        scratch_shapes=list(scratch),
        compiler_params=pltpu.CompilerParams(vmem_limit_bytes=12 * 1024 * 1024),
        cost_estimate=pl.CostEstimate(flops=flops, bytes_accessed=nbytes, transcendentals=0),
    )
    return run


def block_dot(m_ref, k, x):
    acc = None
    for j in range(NV):
        term = m_ref[:, j, k] * x[j][None]
        acc = term if acc is None else acc + term
    return acc


def forward_sweep(l_ref, d_ref, r_ref, s_ref, x):
    f = x
    for k in range(K):
        r = r_ref[:, k]
        f = r if f is None else r + block_dot(l_ref, k, f)
        s_ref[k] = block_dot(d_ref, k, f)
    return f


def forward_chain(l_ref, r_ref, f):
    for k in range(K):
        r = r_ref[:, k]
        f = r if f is None else r + block_dot(l_ref, k, f)
    return f


def backward_sweep(u_ref, s_ref, w_ref, y, emit=None):
    b, p = y, None
    for k in range(K - 1, -1, -1):
        s = s_ref[k]
        b = s if b is None else s - block_dot(u_ref, k, b)
        if w_ref is not None:
            p = b * w_ref[k] if p is None else p + b * w_ref[k]
        if emit is not None:
            emit(k, b)
    return b, p


def map_dot(m_ref, base, x):
    acc = None
    for j in range(NV):
        term = m_ref[base + j] * x[j][None]
        acc = term if acc is None else acc + term
    return acc


def pack_kernel(a_ref, rad_ref, lo_ref, hi_ref):
    for v in range(NV + 1):
        for k in range(K):
            cell = a_ref[v, k] if v < NV else rad_ref[k]
            at = 2 * (v * K + k)
            lo_ref[at : at + 2, :] = cell[0:2]
            hi_ref[at : at + 2, :] = cell[6:8]


def pair_dot(m_ref, k, xs):
    accs = [None] * len(xs)
    for j in range(NV):
        m = m_ref[:, j, k]
        for n, x in enumerate(xs):
            term = m * x[j][None]
            accs[n] = term if accs[n] is None else accs[n] + term
    return accs


def pair_map(m_ref, xs):
    accs = [None] * len(xs)
    for j in range(NV):
        m = m_ref[j]
        for n, x in enumerate(xs):
            term = m * x[j][None]
            accs[n] = term if accs[n] is None else accs[n] + term
    return accs


def interior(a_ref, src_ref, rad_ref, frq_ref, out_ref):
    row = lax.broadcasted_iota(jnp.int32, (H, S), 0)
    lane = lax.broadcasted_iota(jnp.int32, (H, S), 1)
    for k in range(K):
        a = a_ref[:, k]
        rad = rad_ref[k]
        applied = None
        for d, w in ((-2, -0.0625), (-1, 0.25), (1, 0.25), (2, -0.0625)):
            inside = (row + d >= 0) & (row + d < H)
            coef = jnp.where(inside, w * (rad + pltpu.roll(rad, (-d) % H, 0)), 0.0)
            term = coef[None] * pltpu.roll(a, (-d) % H, 1)
            applied = term if applied is None else applied + term
        for d in (-1, 1):
            inside = (lane + d >= 0) & (lane + d < S)
            coef = jnp.where(inside, 0.25 * (rad + pltpu.roll(rad, (-d) % S, 1)), 0.0)
            applied = applied + coef[None] * pltpu.roll(a, (-d) % S, 2)
        frq = frq_ref[k][None]
        half = NV // 2
        src = src_ref[:, k] - applied
        out_ref[:half, k] = src[:half] + frq * a[half:]
        out_ref[half:, k] = src[half:] - frq * a[:half]


def start_kernel(
    pos_ref, w_in, a_in, src_in, rad_in, frq_in, l_in, d_in, u_in,
    l_ref, d_ref, u_ref, r_ref, w_ref, map_ref, a_ref, src_ref, rad_ref, frq_ref, s0_ref, s1_ref, state_sems, block_sems,
):
    wall = pos_ref[0]
    state = [
        pltpu.make_async_copy(there, here, state_sems.at[n])
        for n, (there, here) in enumerate(((a_in, a_ref), (src_in, src_ref), (rad_in, rad_ref), (frq_in, frq_ref)))
    ]
    def block_copies(k):
        pairs = ((l_in, l_ref), (d_in, d_ref), (u_in, u_ref))
        return [
            pltpu.make_async_copy(there.at[:, :, k], here.at[:, :, k], block_sems.at[k, n])
            for n, (there, here) in enumerate(pairs)
        ]

    def depart(k):
        for copy in block_copies(k):
            copy.start()

    def arrived(k):
        for copy in block_copies(k):
            copy.wait()

    ahead = 3
    for copy in state:
        copy.start()
    for k in range(K - 1, K - 1 - ahead, -1):
        depart(k)

    @pl.when(wall != 3)
    def _():
        for k in range(K - 1 - ahead, -1, -1):
            depart(k)

    for k in range(K):
        w_ref[k] = jnp.broadcast_to(w_in[:, k : k + 1], (H, S))
    for copy in state:
        copy.wait()

    @pl.when(wall != 3)
    def _():
        interior(a_ref, src_ref, rad_ref, frq_ref, r_ref)
        for k in range(K - 1, -1, -1):
            arrived(k)

    @pl.when(wall == 3)
    def _():
        pairs = [(c, c + 1) for c in range(0, NV, 2)]

        def descend(k, old_ref, new_ref):
            arrived(k)

            @pl.when(k >= ahead)
            def _():
                depart(k - ahead)

            for cols in pairs:
                outs = pair_map(old_ref, [l_ref[:, c, k + 1] for c in cols])
                outs = pair_dot(u_ref, k, outs)
                for c, out in zip(cols, outs):
                    new_ref[c] = d_ref[:, c, k] - out

        arrived(K - 1)
        depart(K - 1 - ahead)
        for c in range(NV):
            s0_ref[c] = d_ref[:, c, K - 1]

        @pl.loop(0, K // 2 - 1)
        def _(step):
            descend(K - 2 - 2 * step, s0_ref, s1_ref)
            descend(K - 3 - 2 * step, s1_ref, s0_ref)

        descend(jnp.int32(0), s0_ref, s1_ref)
        for cols in pairs:
            for c, out in zip(cols, pair_map(s1_ref, [l_ref[:, c, 0] for c in cols])):
                map_ref[c] = out


def residual_kernel(
    pos_ref, inner_ref, a_ref, src_ref, frq_ref, left_ref, right_ref, rad_ref, l_ref, d_ref, u_ref,
    out_ref, up_ref, down_ref, s_ref, late_ref,
):
    wall, tile, last = pos_ref[0], pos_ref[1], pos_ref[2]
    row = lax.broadcasted_iota(jnp.int32, (H, S), 0)
    has_left = tile > 0
    has_right = tile < last

    def line(ref, v, k, c):
        at = 2 * (v * K + k) + c
        return jnp.broadcast_to(ref[at : at + 1, :], (H, S))

    def add_halo(r_ref):
        for k in range(K):
            rad = rad_ref[k]
            l0, l1, r0, r1 = (line(ref, NV, k, c) for ref in (left_ref, right_ref) for c in (0, 1))
            zero = jnp.zeros((H, S), F32)
            f_l0 = jnp.where((row == 0) & has_left, -0.0625 * (rad + l0), zero)
            f_l1 = jnp.where(row == 0, 0.25 * (rad + l1), jnp.where(row == 1, -0.0625 * (rad + l1), zero))
            f_l1 = jnp.where(has_left, f_l1, zero)
            f_r0 = jnp.where(row == 7, 0.25 * (rad + r0), jnp.where(row == 6, -0.0625 * (rad + r0), zero))
            f_r0 = jnp.where(has_right, f_r0, zero)
            f_r1 = jnp.where((row == 7) & has_right, -0.0625 * (rad + r1), zero)
            for v in range(NV):
                applied = f_l0 * line(left_ref, v, k, 0) + f_l1 * line(left_ref, v, k, 1)
                applied = applied + (f_r0 * line(right_ref, v, k, 0) + f_r1 * line(right_ref, v, k, 1))
                out_ref[v, k] = r_ref[v, k] - applied

    @pl.when(wall == 3)
    def _():
        interior(a_ref, src_ref, rad_ref, frq_ref, late_ref)
        add_halo(late_ref)

    @pl.when(wall != 3)
    def _():
        add_halo(inner_ref)

    @pl.when(wall == 0)
    def _():
        up_ref[...] = forward_chain(l_ref, out_ref, None)

    @pl.when(wall == 3)
    def _():
        forward_sweep(l_ref, d_ref, out_ref, s_ref, None)
        down_ref[...] = backward_sweep(u_ref, s_ref, None, None)[0]


def middle_kernel(pos_ref, x_ref, r_ref, l_ref, out_ref):
    @pl.when(pos_ref[0] == 1)
    def _():
        out_ref[...] = forward_chain(l_ref, r_ref, x_ref[...])


def shift_kernel(pos_ref, x_ref, r_ref, l_ref, d_ref, u_ref, shift_ref, s_ref):
    @pl.when(pos_ref[0] == 1)
    def _():
        forward_sweep(l_ref, d_ref, r_ref, s_ref, x_ref[...])
        shift_ref[...] = backward_sweep(u_ref, s_ref, None, None)[0]


def below_kernel(pos_ref, u_ref, below_ref):
    @pl.when(pos_ref[0] == 1)
    def _():
        @pl.loop(0, NV // 2)
        def _(pair):
            cols = [2 * pair, 2 * pair + 1]
            xs = [u_ref[:, c, K - 1] for c in cols]
            for k in range(K - 2, -1, -1):
                xs = pair_dot(u_ref, k, xs)
            for c, x in zip(cols, xs):
                below_ref[c] = x


def rise_kernel(pos_ref, x_ref, r_ref, l_ref, d_ref, x3_ref, s_ref):
    @pl.when(pos_ref[0] == 2)
    def _():
        x3_ref[...] = forward_sweep(l_ref, d_ref, r_ref, s_ref, x_ref[...])


def decide_kernel(pos_ref, x3_ref, b_ref, map_ref, s_ref, u_ref, y2_ref, y1_ref):
    @pl.when(pos_ref[0] == 2)
    def _():
        y2 = b_ref[...] + map_dot(map_ref, 0, x3_ref[...])
        y2_ref[...] = y2
        y1_ref[...] = backward_sweep(u_ref, s_ref, None, y2)[0]


def scale_kernel(pos_ref, x1_ref, x3_ref, s2_ref, r_ref, l_ref, d_ref, s_ref, x_ref):
    wall = pos_ref[0]

    @pl.when(wall == 0)
    def _():
        x_ref[...] = jnp.zeros((NV, H, S), F32)

    @pl.when(wall == 1)
    def _():
        x_ref[...] = x1_ref[...]

    @pl.when(wall == 3)
    def _():
        x_ref[...] = x3_ref[...]

    @pl.when(wall == 2)
    def _():
        s_ref[...] = s2_ref[...]

    @pl.when(wall != 2)
    def _():
        forward_sweep(l_ref, d_ref, r_ref, s_ref, x_ref[...])


def finish_kernel(
    pos_ref, y2_ref, y10_ref, y1_ref, below_ref, shift_ref, w_ref, pw_ref, s_ref, u_ref, out_ref, rows_ref, y_ref, prof_ref
):
    wall = pos_ref[0]

    @pl.when(wall == 0)
    def _():
        y_ref[...] = shift_ref[...] + map_dot(below_ref, 0, y10_ref[...])

    @pl.when(wall == 1)
    def _():
        y_ref[...] = y1_ref[...]

    @pl.when(wall == 2)
    def _():
        y_ref[...] = y2_ref[...]

    @pl.when(wall == 3)
    def _():
        y_ref[...] = jnp.zeros((NV, H, S), F32)

    def emit(k, b):
        out_ref[:, k] = b

    _, profile = backward_sweep(u_ref, s_ref, w_ref, y_ref[...], emit)
    for v in range(NV):
        prof_ref[v * H : (v + 1) * H, :] = profile[v]
    row = lax.broadcasted_iota(jnp.int32, (SLOTS, S), 0)
    lane = lax.broadcasted_iota(jnp.int32, (SLOTS, S), 1)
    prof_ref[NV * H :, :] = (row == lane).astype(F32)
    rows_ref[...] = jnp.dot(pw_ref[...], prof_ref[...], precision=highest, preferred_element_type=F32)


def place_kernel(count_ref, w_ref, owner_ref, tag_ref, out_ref):
    blocks = owner_ref.shape[1]
    owners = out_ref.shape[0] // ROWS_PER_OWNER
    owner = owner_ref[...]
    live = lax.broadcasted_iota(jnp.int32, (1, blocks), 1) < count_ref[0]
    hits = (owner == lax.broadcasted_iota(jnp.int32, (owners, blocks), 0)).astype(F32)
    earlier = lax.broadcasted_iota(jnp.int32, (blocks, blocks), 0) < lax.broadcasted_iota(jnp.int32, (blocks, blocks), 1)
    before = jnp.dot(hits, earlier.astype(F32), preferred_element_type=F32)
    slot = jnp.sum(before * hits, axis=0, keepdims=True).astype(jnp.int32)
    row = lax.broadcasted_iota(jnp.int32, (owners * ROWS_PER_OWNER, blocks), 0)
    placed = ((owner * ROWS_PER_OWNER + slot == row) & live).astype(F32)
    tagged = ((owner * ROWS_PER_OWNER + SLOTS == row) & live).astype(F32)
    width = NV * H
    lanes = lax.broadcasted_iota(jnp.int32, (SLOTS, blocks), 0)
    tags = jnp.where(lanes == slot, (tag_ref[...] + 1).astype(F32), 0.0)
    dims = (((1,), (1,)), ((), ()))
    out_ref[:, :width] = lax.dot_general(placed, w_ref[...], dims, precision=highest, preferred_element_type=F32)
    out_ref[:, width:] = lax.dot_general(tagged, tags, dims, precision=highest, preferred_element_type=F32)


def pick_kernel(got_ref, out_ref):
    rows = got_ref.shape[0]
    sources = rows // ROWS_PER_OWNER
    tag_rows = got_ref[pl.ds(SLOTS, sources, stride=ROWS_PER_OWNER), :]
    lane_of = (
        lax.broadcasted_iota(jnp.int32, (SLOTS, S), 0) == lax.broadcasted_iota(jnp.int32, (SLOTS, S), 1)
    ).astype(F32)
    tags = lax.dot_general(
        lane_of, tag_rows, (((1,), (1,)), ((), ())), precision=highest, preferred_element_type=F32
    )
    column = lax.broadcasted_iota(jnp.int32, (sources, rows), 1)
    first = lax.broadcasted_iota(jnp.int32, (sources, rows), 0) * ROWS_PER_OWNER
    spread = ((column >= first) & (column < first + ROWS_PER_OWNER)).astype(F32)
    wide = jnp.dot(tags, spread, precision=highest, preferred_element_type=F32)
    slot = lax.broadcasted_iota(jnp.int32, (SLOTS, rows), 1) % ROWS_PER_OWNER
    mine = slot == lax.broadcasted_iota(jnp.int32, (SLOTS, rows), 0)
    tag = jnp.sum(jnp.where(mine, wide, 0.0), axis=0, keepdims=True)
    target = (lax.broadcasted_iota(jnp.int32, (PATCH_DEV, rows), 0) + 1).astype(F32)
    picker = (tag == target).astype(F32)
    out_ref[...] = jnp.dot(picker, got_ref[...], precision=highest, preferred_element_type=F32)


def on_device(
    adjoint, source, radius, frequency, lower, diag, upper, wall_weight,
    surface_weight, patch_owner, patch_row, surface_count,
):
    tiles = lax.axis_size("tile")
    tie = lax.optimization_barrier
    pos = jnp.stack([lax.axis_index("wall"), lax.axis_index("tile"), jnp.int32(tiles - 1)]).astype(jnp.int32)
    levels = held(K, NV, H, S)
    block, state, cell, vec = held(NV, NV, K, H, S), held(NV, K, H, S), held(K, H, S), f32(NV, H, S)
    adjoint, source, radius, frequency, lower, diag, upper, wall_weight = (
        far_off(x)
        for x in (adjoint, source, radius, frequency, lower, diag, upper, wall_weight.reshape(1, K))
    )

    lo, hi = call("pack", pack_kernel, (f32(22 * K, S), f32(22 * K, S)), 2, nbytes=800_000)(adjoint, radius)
    left = lax.ppermute(hi, "tile", [(i, (i + 1) % tiles) for i in range(tiles)])
    right = lax.ppermute(lo, "tile", [((i + 1) % tiles, i) for i in range(tiles)])

    lo, pos1 = tie((lo, pos))
    lower, diag, upper, inner, weight, maps, adjoint, source, radius, frequency = call(
        "start", start_kernel, (block, block, block, state, cell, f32(NV, NV, H, S), state, state, cell, cell), 9, smem=(0,),
        far=(2, 3, 4, 5, 6, 7, 8),
        scratch=(
            held(NV, NV, H, S), held(NV, NV, H, S), pltpu.SemaphoreType.DMA((4,)), pltpu.SemaphoreType.DMA((K, 3)),
        ),
        flops=30_000_000, nbytes=11_000_000,
    )(pos1, wall_weight, adjoint, source, radius, frequency, lower, diag, upper)

    maps, left, right = tie((maps, left, right))
    above = lax.ppermute(maps, "wall", [(3, 2)])
    resid, up, down = call(
        "residual", residual_kernel, (state, vec, vec), 11, smem=(0,), scratch=(levels, state)
    )(pos, inner, adjoint, source, frequency, left, right, radius, lower, diag, upper)
    x1 = lax.ppermute(up, "wall", [(0, 1)])
    b3 = lax.ppermute(down, "wall", [(3, 2)])
    up, pos1 = tie((up, pos))
    below = call("below", below_kernel, f32(NV, NV, H, S), 2, smem=(0,))(pos1, upper)
    x1, below = tie((x1, below))
    below = lax.ppermute(below, "wall", [(1, 0)])
    x2 = call("middle", middle_kernel, vec, 4, smem=(0,))(pos, x1, resid, lower)
    x2, pos2 = tie((x2, pos))
    x2 = lax.ppermute(x2, "wall", [(1, 2)])
    shift = call("shift", shift_kernel, vec, 6, smem=(0,), scratch=(levels,))(pos2, x1, resid, lower, diag, upper)
    swt = surface_weight.transpose(1, 2, 0).reshape(NV * H, -1)
    placed = call("place", place_kernel, held(tiles * ROWS_PER_OWNER, NV * H + SLOTS), 4, smem=(0,))(
        surface_count, swt, patch_owner.reshape(1, -1), patch_row.reshape(1, -1)
    )

    x2, placed = tie((x2, placed))
    x3, scaled2 = call("rise", rise_kernel, (vec, levels), 5, smem=(0,))(pos, x2, resid, lower, diag)
    y2, y1 = call("decide", decide_kernel, (vec, vec), 6, smem=(0,))(pos, x3, b3, above, scaled2, upper)
    x3, y1 = tie((x3, y1))
    y1, shift = tie((y1, shift))
    x33 = lax.ppermute(x3, "wall", [(2, 3)])
    y10 = lax.ppermute(y1, "wall", [(2, 0)])
    y11 = lax.ppermute(y1, "wall", [(2, 1)])
    shift = lax.ppermute(shift, "wall", [(1, 0)])
    scaled = call("scale", scale_kernel, levels, 7, smem=(0,), scratch=(held(NV, H, S),))(
        pos, x1, x33, scaled2, resid, lower, diag
    )
    adjoint_next, rows = call(
        "finish", finish_kernel, (f32(NV, K, H, S), away(tiles * ROWS_PER_OWNER, S)), 10, smem=(0,),
        scratch=(held(NV, H, S), held(NV * H + SLOTS, S)),
    )(pos, y2, y10, y11, below, shift, weight, placed, scaled, upper)
    got = lax.all_to_all(rows.reshape(tiles, ROWS_PER_OWNER, 1, S), "tile", split_axis=0, concat_axis=0)
    got = got.reshape(tiles * ROWS_PER_OWNER, S)
    part = call("pick", pick_kernel, f32(PATCH_DEV, S), 1)(got)
    walls = lax.axis_size("wall")
    patch = part
    for d in range(1, walls):
        patch = patch + lax.ppermute(part, "wall", [(w, (w + d) % walls) for w in range(walls)])
    return adjoint_next, patch


def solution(mesh):
    in_specs = (
        P(None, "wall", "tile", None),
        P(None, "wall", "tile", None),
        P("wall", "tile", None),
        P("wall", "tile", None),
        P(None, None, "wall", "tile", None),
        P(None, None, "wall", "tile", None),
        P(None, None, "wall", "tile", None),
        P("wall"),
        P("tile", None, None),
        P("tile", None),
        P("tile"),
        P("tile"),
    )
    out_specs = (P(None, "wall", "tile", None), P("tile", None))
    return jax.shard_map(
        on_device, mesh=mesh, in_specs=in_specs, out_specs=out_specs, check_vma=False
    )
```

```python
import jax
import jax.numpy as jnp
from jax import lax
from jax.experimental import pallas as pl
from jax.experimental.pallas import tpu as pltpu
from jax.sharding import PartitionSpec as P

NV = 10
K = 8
H = 8
S = 128
PATCH_DEV = 64
SLOTS = 8
ROWS_PER_OWNER = SLOTS + 1
F32 = jnp.float32
highest = lax.Precision.HIGHEST

VM = pl.BlockSpec(memory_space=pltpu.VMEM)
SM = pl.BlockSpec(memory_space=pltpu.SMEM)
HB = pl.BlockSpec(memory_space=pltpu.HBM)


def f32(*shape):
    return jax.ShapeDtypeStruct(shape, F32)


def held(*shape):
    return pltpu.VMEM(shape, F32)


def away(*shape):
    return pltpu.HBM(shape, F32)


def far_off(x):
    return pltpu.with_memory_space_constraint(x, pltpu.HBM)


def call(name, body, out_shape, n_in, smem=(), far=(), scratch=(), flops=0, nbytes=0):
    single = not isinstance(out_shape, (tuple, list))
    run = pl.pallas_call(
        body,
        name=name,
        out_shape=out_shape,
        in_specs=[SM if i in smem else HB if i in far else VM for i in range(n_in)],
        out_specs=VM if single else [VM] * len(out_shape),
        scratch_shapes=list(scratch),
        compiler_params=pltpu.CompilerParams(vmem_limit_bytes=12 * 1024 * 1024),
        cost_estimate=pl.CostEstimate(flops=flops, bytes_accessed=nbytes, transcendentals=0),
    )
    return run


def block_dot(m_ref, k, x):
    acc = None
    for j in range(NV):
        term = m_ref[:, j, k] * x[j][None]
        acc = term if acc is None else acc + term
    return acc


def forward_sweep(l_ref, d_ref, r_ref, s_ref, x):
    f = x
    for k in range(K):
        r = r_ref[:, k]
        f = r if f is None else r + block_dot(l_ref, k, f)
        s_ref[k] = block_dot(d_ref, k, f)
    return f


def forward_chain(l_ref, r_ref, f):
    for k in range(K):
        r = r_ref[:, k]
        f = r if f is None else r + block_dot(l_ref, k, f)
    return f


def backward_sweep(u_ref, s_ref, w_ref, y, emit=None):
    b, p = y, None
    for k in range(K - 1, -1, -1):
        s = s_ref[k]
        b = s if b is None else s - block_dot(u_ref, k, b)
        if w_ref is not None:
            p = b * w_ref[k] if p is None else p + b * w_ref[k]
        if emit is not None:
            emit(k, b)
    return b, p


def split(x):
    high = x.astype(jnp.bfloat16).astype(F32)
    return high, x - high


def dot_passes(a, b):
    a_high, a_low = split(a)
    b_high, b_low = split(b)
    one = lambda p, q: jnp.dot(p, q, preferred_element_type=F32)
    return one(a_high, b_high) + (one(a_high, b_low) + one(a_low, b_high))


def map_dot(m_ref, base, x):
    acc = None
    for j in range(NV):
        term = m_ref[base + j] * x[j][None]
        acc = term if acc is None else acc + term
    return acc


def pack_kernel(a_ref, rad_ref, lo_ref, hi_ref):
    for v in range(NV + 1):
        for k in range(K):
            cell = a_ref[v, k] if v < NV else rad_ref[k]
            at = 2 * (v * K + k)
            lo_ref[at : at + 2, :] = cell[0:2]
            hi_ref[at : at + 2, :] = cell[6:8]


def pair_dot(m_ref, k, xs):
    accs = [None] * len(xs)
    for j in range(NV):
        m = m_ref[:, j, k]
        for n, x in enumerate(xs):
            term = m * x[j][None]
            accs[n] = term if accs[n] is None else accs[n] + term
    return accs


def pair_map(m_ref, xs):
    accs = [None] * len(xs)
    for j in range(NV):
        m = m_ref[j]
        for n, x in enumerate(xs):
            term = m * x[j][None]
            accs[n] = term if accs[n] is None else accs[n] + term
    return accs


def interior(a_ref, src_ref, rad_ref, frq_ref, out_ref):
    row = lax.broadcasted_iota(jnp.int32, (H, S), 0)
    lane = lax.broadcasted_iota(jnp.int32, (H, S), 1)
    for k in range(K):
        a = a_ref[:, k]
        rad = rad_ref[k]
        applied = None
        for d, w in ((-2, -0.0625), (-1, 0.25), (1, 0.25), (2, -0.0625)):
            inside = (row + d >= 0) & (row + d < H)
            coef = jnp.where(inside, w * (rad + pltpu.roll(rad, (-d) % H, 0)), 0.0)
            term = coef[None] * pltpu.roll(a, (-d) % H, 1)
            applied = term if applied is None else applied + term
        for d in (-1, 1):
            inside = (lane + d >= 0) & (lane + d < S)
            coef = jnp.where(inside, 0.25 * (rad + pltpu.roll(rad, (-d) % S, 1)), 0.0)
            applied = applied + coef[None] * pltpu.roll(a, (-d) % S, 2)
        frq = frq_ref[k][None]
        half = NV // 2
        src = src_ref[:, k] - applied
        out_ref[:half, k] = src[:half] + frq * a[half:]
        out_ref[half:, k] = src[half:] - frq * a[:half]


def start_kernel(
    pos_ref, w_in, a_in, src_in, rad_in, frq_in, l_in, d_in, u_in,
    l_ref, d_ref, u_ref, r_ref, w_ref, map_ref, a_ref, src_ref, rad_ref, frq_ref, s0_ref, s1_ref, state_sems, block_sems,
):
    wall = pos_ref[0]
    state = [
        pltpu.make_async_copy(there, here, state_sems.at[n])
        for n, (there, here) in enumerate(((a_in, a_ref), (src_in, src_ref), (rad_in, rad_ref), (frq_in, frq_ref)))
    ]
    def block_copies(k):
        pairs = ((l_in, l_ref), (d_in, d_ref), (u_in, u_ref))
        return [
            pltpu.make_async_copy(there.at[:, :, k], here.at[:, :, k], block_sems.at[k, n])
            for n, (there, here) in enumerate(pairs)
        ]

    def depart(k):
        for copy in block_copies(k):
            copy.start()

    def arrived(k):
        for copy in block_copies(k):
            copy.wait()

    ahead = 3
    for copy in state:
        copy.start()
    for k in range(K - 1, K - 1 - ahead, -1):
        depart(k)

    @pl.when(wall != 3)
    def _():
        for k in range(K - 1 - ahead, -1, -1):
            depart(k)

    for k in range(K):
        w_ref[k] = jnp.broadcast_to(w_in[:, k : k + 1], (H, S))
    for copy in state:
        copy.wait()

    @pl.when(wall != 3)
    def _():
        interior(a_ref, src_ref, rad_ref, frq_ref, r_ref)
        for k in range(K - 1, -1, -1):
            arrived(k)

    @pl.when(wall == 3)
    def _():
        pairs = [(c, c + 1) for c in range(0, NV, 2)]

        def descend(k, old_ref, new_ref):
            arrived(k)

            @pl.when(k >= ahead)
            def _():
                depart(k - ahead)

            for cols in pairs:
                outs = pair_map(old_ref, [l_ref[:, c, k + 1] for c in cols])
                outs = pair_dot(u_ref, k, outs)
                for c, out in zip(cols, outs):
                    new_ref[c] = d_ref[:, c, k] - out

        arrived(K - 1)
        depart(K - 1 - ahead)
        for c in range(NV):
            s0_ref[c] = d_ref[:, c, K - 1]

        @pl.loop(0, K // 2 - 1)
        def _(step):
            descend(K - 2 - 2 * step, s0_ref, s1_ref)
            descend(K - 3 - 2 * step, s1_ref, s0_ref)

        descend(jnp.int32(0), s0_ref, s1_ref)
        for cols in pairs:
            for c, out in zip(cols, pair_map(s1_ref, [l_ref[:, c, 0] for c in cols])):
                map_ref[c] = out


def residual_kernel(
    pos_ref, inner_ref, a_ref, src_ref, frq_ref, left_ref, right_ref, rad_ref, l_ref, d_ref, u_ref,
    out_ref, up_ref, down_ref, s_ref, late_ref,
):
    wall, tile, last = pos_ref[0], pos_ref[1], pos_ref[2]
    row = lax.broadcasted_iota(jnp.int32, (H, S), 0)
    has_left = tile > 0
    has_right = tile < last

    def line(ref, v, k, c):
        at = 2 * (v * K + k) + c
        return jnp.broadcast_to(ref[at : at + 1, :], (H, S))

    def add_halo(r_ref):
        for k in range(K):
            rad = rad_ref[k]
            l0, l1, r0, r1 = (line(ref, NV, k, c) for ref in (left_ref, right_ref) for c in (0, 1))
            zero = jnp.zeros((H, S), F32)
            f_l0 = jnp.where((row == 0) & has_left, -0.0625 * (rad + l0), zero)
            f_l1 = jnp.where(row == 0, 0.25 * (rad + l1), jnp.where(row == 1, -0.0625 * (rad + l1), zero))
            f_l1 = jnp.where(has_left, f_l1, zero)
            f_r0 = jnp.where(row == 7, 0.25 * (rad + r0), jnp.where(row == 6, -0.0625 * (rad + r0), zero))
            f_r0 = jnp.where(has_right, f_r0, zero)
            f_r1 = jnp.where((row == 7) & has_right, -0.0625 * (rad + r1), zero)
            for v in range(NV):
                applied = f_l0 * line(left_ref, v, k, 0) + f_l1 * line(left_ref, v, k, 1)
                applied = applied + (f_r0 * line(right_ref, v, k, 0) + f_r1 * line(right_ref, v, k, 1))
                out_ref[v, k] = r_ref[v, k] - applied

    @pl.when(wall == 3)
    def _():
        interior(a_ref, src_ref, rad_ref, frq_ref, late_ref)
        add_halo(late_ref)

    @pl.when(wall != 3)
    def _():
        add_halo(inner_ref)

    @pl.when(wall == 0)
    def _():
        up_ref[...] = forward_chain(l_ref, out_ref, None)

    @pl.when(wall == 3)
    def _():
        forward_sweep(l_ref, d_ref, out_ref, s_ref, None)
        down_ref[...] = backward_sweep(u_ref, s_ref, None, None)[0]


def middle_kernel(pos_ref, x_ref, r_ref, l_ref, out_ref):
    @pl.when(pos_ref[0] == 1)
    def _():
        out_ref[...] = forward_chain(l_ref, r_ref, x_ref[...])


def shift_kernel(pos_ref, x_ref, r_ref, l_ref, d_ref, u_ref, shift_ref, s_ref):
    @pl.when(pos_ref[0] == 1)
    def _():
        forward_sweep(l_ref, d_ref, r_ref, s_ref, x_ref[...])
        shift_ref[...] = backward_sweep(u_ref, s_ref, None, None)[0]


def below_kernel(pos_ref, u_ref, below_ref):
    @pl.when(pos_ref[0] == 1)
    def _():
        @pl.loop(0, NV // 2)
        def _(pair):
            cols = [2 * pair, 2 * pair + 1]
            xs = [u_ref[:, c, K - 1] for c in cols]
            for k in range(K - 2, -1, -1):
                xs = pair_dot(u_ref, k, xs)
            for c, x in zip(cols, xs):
                below_ref[c] = x


def rise_kernel(pos_ref, x_ref, r_ref, l_ref, d_ref, x3_ref, s_ref):
    @pl.when(pos_ref[0] == 2)
    def _():
        x3_ref[...] = forward_sweep(l_ref, d_ref, r_ref, s_ref, x_ref[...])


def decide_kernel(pos_ref, x3_ref, b_ref, map_ref, s_ref, u_ref, y2_ref, y1_ref):
    @pl.when(pos_ref[0] == 2)
    def _():
        y2 = b_ref[...] + map_dot(map_ref, 0, x3_ref[...])
        y2_ref[...] = y2
        y1_ref[...] = backward_sweep(u_ref, s_ref, None, y2)[0]


def scale_kernel(pos_ref, x1_ref, x3_ref, s2_ref, r_ref, l_ref, d_ref, s_ref, x_ref):
    wall = pos_ref[0]

    @pl.when(wall == 0)
    def _():
        x_ref[...] = jnp.zeros((NV, H, S), F32)

    @pl.when(wall == 1)
    def _():
        x_ref[...] = x1_ref[...]

    @pl.when(wall == 3)
    def _():
        x_ref[...] = x3_ref[...]

    @pl.when(wall == 2)
    def _():
        s_ref[...] = s2_ref[...]

    @pl.when(wall != 2)
    def _():
        forward_sweep(l_ref, d_ref, r_ref, s_ref, x_ref[...])


def finish_kernel(
    pos_ref, y2_ref, y10_ref, y1_ref, below_ref, shift_ref, w_ref, pw_ref, s_ref, u_ref, out_ref, rows_ref, y_ref, prof_ref
):
    wall = pos_ref[0]

    @pl.when(wall == 0)
    def _():
        y_ref[...] = shift_ref[...] + map_dot(below_ref, 0, y10_ref[...])

    @pl.when(wall == 1)
    def _():
        y_ref[...] = y1_ref[...]

    @pl.when(wall == 2)
    def _():
        y_ref[...] = y2_ref[...]

    @pl.when(wall == 3)
    def _():
        y_ref[...] = jnp.zeros((NV, H, S), F32)

    def emit(k, b):
        out_ref[:, k] = b

    _, profile = backward_sweep(u_ref, s_ref, w_ref, y_ref[...], emit)
    for v in range(NV):
        prof_ref[v * H : (v + 1) * H, :] = profile[v]
    row = lax.broadcasted_iota(jnp.int32, (SLOTS, S), 0)
    lane = lax.broadcasted_iota(jnp.int32, (SLOTS, S), 1)
    prof_ref[NV * H :, :] = (row == lane).astype(F32)
    rows_ref[...] = dot_passes(pw_ref[...], prof_ref[...])


def place_kernel(count_ref, w_ref, owner_ref, tag_ref, out_ref):
    blocks = owner_ref.shape[1]
    owners = out_ref.shape[0] // ROWS_PER_OWNER
    owner = owner_ref[...]
    live = lax.broadcasted_iota(jnp.int32, (1, blocks), 1) < count_ref[0]
    hits = (owner == lax.broadcasted_iota(jnp.int32, (owners, blocks), 0)).astype(F32)
    earlier = lax.broadcasted_iota(jnp.int32, (blocks, blocks), 0) < lax.broadcasted_iota(jnp.int32, (blocks, blocks), 1)
    before = jnp.dot(hits, earlier.astype(F32), preferred_element_type=F32)
    slot = jnp.sum(before * hits, axis=0, keepdims=True).astype(jnp.int32)
    row = lax.broadcasted_iota(jnp.int32, (owners * ROWS_PER_OWNER, blocks), 0)
    placed = ((owner * ROWS_PER_OWNER + slot == row) & live).astype(F32)
    tagged = ((owner * ROWS_PER_OWNER + SLOTS == row) & live).astype(F32)
    width = NV * H
    lanes = lax.broadcasted_iota(jnp.int32, (SLOTS, blocks), 0)
    tags = jnp.where(lanes == slot, (tag_ref[...] + 1).astype(F32), 0.0)
    dims = (((1,), (1,)), ((), ()))
    out_ref[:, :width] = lax.dot_general(placed, w_ref[...], dims, precision=highest, preferred_element_type=F32)
    out_ref[:, width:] = lax.dot_general(tagged, tags, dims, precision=highest, preferred_element_type=F32)


def pick_kernel(got_ref, out_ref):
    rows = got_ref.shape[0]
    sources = rows // ROWS_PER_OWNER
    tag_rows = got_ref[pl.ds(SLOTS, sources, stride=ROWS_PER_OWNER), :]
    lane_of = (
        lax.broadcasted_iota(jnp.int32, (SLOTS, S), 0) == lax.broadcasted_iota(jnp.int32, (SLOTS, S), 1)
    ).astype(F32)
    tags = lax.dot_general(
        lane_of, tag_rows, (((1,), (1,)), ((), ())), precision=highest, preferred_element_type=F32
    )
    column = lax.broadcasted_iota(jnp.int32, (sources, rows), 1)
    first = lax.broadcasted_iota(jnp.int32, (sources, rows), 0) * ROWS_PER_OWNER
    spread = ((column >= first) & (column < first + ROWS_PER_OWNER)).astype(F32)
    wide = jnp.dot(tags, spread, precision=highest, preferred_element_type=F32)
    slot = lax.broadcasted_iota(jnp.int32, (SLOTS, rows), 1) % ROWS_PER_OWNER
    mine = slot == lax.broadcasted_iota(jnp.int32, (SLOTS, rows), 0)
    tag = jnp.sum(jnp.where(mine, wide, 0.0), axis=0, keepdims=True)
    target = (lax.broadcasted_iota(jnp.int32, (PATCH_DEV, rows), 0) + 1).astype(F32)
    picker = (tag == target).astype(F32)
    high, rest = split(got_ref[...])
    middle, low = split(rest)
    one = lambda q: jnp.dot(picker, q, preferred_element_type=F32)
    out_ref[...] = one(high) + (one(middle) + one(low))


def on_device(
    adjoint, source, radius, frequency, lower, diag, upper, wall_weight,
    surface_weight, patch_owner, patch_row, surface_count,
):
    tiles = lax.axis_size("tile")
    tie = lax.optimization_barrier
    pos = jnp.stack([lax.axis_index("wall"), lax.axis_index("tile"), jnp.int32(tiles - 1)]).astype(jnp.int32)
    levels = held(K, NV, H, S)
    block, state, cell, vec = held(NV, NV, K, H, S), held(NV, K, H, S), held(K, H, S), f32(NV, H, S)
    adjoint, source, radius, frequency, lower, diag, upper, wall_weight = (
        far_off(x)
        for x in (adjoint, source, radius, frequency, lower, diag, upper, wall_weight.reshape(1, K))
    )

    lo, hi = call("pack", pack_kernel, (f32(22 * K, S), f32(22 * K, S)), 2, nbytes=800_000)(adjoint, radius)
    left = lax.ppermute(hi, "tile", [(i, (i + 1) % tiles) for i in range(tiles)])
    right = lax.ppermute(lo, "tile", [((i + 1) % tiles, i) for i in range(tiles)])

    lo, pos1 = tie((lo, pos))
    lower, diag, upper, inner, weight, maps, adjoint, source, radius, frequency = call(
        "start", start_kernel, (block, block, block, state, cell, f32(NV, NV, H, S), state, state, cell, cell), 9, smem=(0,),
        far=(2, 3, 4, 5, 6, 7, 8),
        scratch=(
            held(NV, NV, H, S), held(NV, NV, H, S), pltpu.SemaphoreType.DMA((4,)), pltpu.SemaphoreType.DMA((K, 3)),
        ),
        flops=30_000_000, nbytes=11_000_000,
    )(pos1, wall_weight, adjoint, source, radius, frequency, lower, diag, upper)

    maps, left, right = tie((maps, left, right))
    above = lax.ppermute(maps, "wall", [(3, 2)])
    resid, up, down = call(
        "residual", residual_kernel, (state, vec, vec), 11, smem=(0,), scratch=(levels, state)
    )(pos, inner, adjoint, source, frequency, left, right, radius, lower, diag, upper)
    x1 = lax.ppermute(up, "wall", [(0, 1)])
    b3 = lax.ppermute(down, "wall", [(3, 2)])
    up, pos1 = tie((up, pos))
    below = call("below", below_kernel, f32(NV, NV, H, S), 2, smem=(0,))(pos1, upper)
    x1, below = tie((x1, below))
    below = lax.ppermute(below, "wall", [(1, 0)])
    x2 = call("middle", middle_kernel, vec, 4, smem=(0,))(pos, x1, resid, lower)
    x2, pos2 = tie((x2, pos))
    x2 = lax.ppermute(x2, "wall", [(1, 2)])
    shift = call("shift", shift_kernel, vec, 6, smem=(0,), scratch=(levels,))(pos2, x1, resid, lower, diag, upper)
    swt = surface_weight.transpose(1, 2, 0).reshape(NV * H, -1)
    placed = call("place", place_kernel, held(tiles * ROWS_PER_OWNER, NV * H + SLOTS), 4, smem=(0,))(
        surface_count, swt, patch_owner.reshape(1, -1), patch_row.reshape(1, -1)
    )

    x2, placed = tie((x2, placed))
    x3, scaled2 = call("rise", rise_kernel, (vec, levels), 5, smem=(0,))(pos, x2, resid, lower, diag)
    y2, y1 = call("decide", decide_kernel, (vec, vec), 6, smem=(0,))(pos, x3, b3, above, scaled2, upper)
    x3, y1 = tie((x3, y1))
    y1, shift = tie((y1, shift))
    x33 = lax.ppermute(x3, "wall", [(2, 3)])
    y10 = lax.ppermute(y1, "wall", [(2, 0)])
    y11 = lax.ppermute(y1, "wall", [(2, 1)])
    shift = lax.ppermute(shift, "wall", [(1, 0)])
    scaled = call("scale", scale_kernel, levels, 7, smem=(0,), scratch=(held(NV, H, S),))(
        pos, x1, x33, scaled2, resid, lower, diag
    )
    adjoint_next, rows = call(
        "finish", finish_kernel, (f32(NV, K, H, S), away(tiles * ROWS_PER_OWNER, S)), 10, smem=(0,),
        scratch=(held(NV, H, S), held(NV * H + SLOTS, S)),
    )(pos, y2, y10, y11, below, shift, weight, placed, scaled, upper)
    got = lax.all_to_all(rows.reshape(tiles, ROWS_PER_OWNER, 1, S), "tile", split_axis=0, concat_axis=0)
    got = got.reshape(tiles * ROWS_PER_OWNER, S)
    part = call("pick", pick_kernel, f32(PATCH_DEV, S), 1)(got)
    walls = lax.axis_size("wall")
    patch = part
    for d in range(1, walls):
        patch = patch + lax.ppermute(part, "wall", [(w, (w + d) % walls) for w in range(walls)])
    return adjoint_next, patch


def solution(mesh):
    in_specs = (
        P(None, "wall", "tile", None),
        P(None, "wall", "tile", None),
        P("wall", "tile", None),
        P("wall", "tile", None),
        P(None, None, "wall", "tile", None),
        P(None, None, "wall", "tile", None),
        P(None, None, "wall", "tile", None),
        P("wall"),
        P("tile", None, None),
        P("tile", None),
        P("tile"),
        P("tile"),
    )
    out_specs = (P(None, "wall", "tile", None), P("tile", None))
    return jax.shard_map(
        on_device, mesh=mesh, in_specs=in_specs, out_specs=out_specs, check_vma=False
    )
```
